32 devices in a mesh: section: 2 (over x), dp: 16 (over z, y, core).
Axes of the slice: x: 2, y: 2, z: 4, core: 2. Of those that a mesh axis runs over, the one named last changes fastest.
Arguments:
- clip_tokens: bfloat16 [2, 16, 6, 320, 512], P(None, 'dp'), may hold values from -6 to 6
- window_cols: int32 [2, 16], P(None, 'dp'), may hold values from 3 to 5, as said below
- time_groups: int32 [2, 16, 6], P(None, 'dp'), may hold values from 0 to 4, never falling along the last dimension, each value on 1 to 2 neighbouring positions
- cotangent: bfloat16 [2, 16, 6, 320, 512], P(None, 'dp'), may hold values from -6 to 6
- attention_gain: float32 [2, 512], P('section'), may hold values from 0.5 to 1.5
- attention_bias: float32 [2, 512], P('section'), may hold values from -2.5 to 2.5
- projection_in: bfloat16 [2, 512, 1536], P('section'), may hold values from -0.25 to 0.25
- projection_out: bfloat16 [2, 512, 512], P('section'), may hold values from -0.5 to 0.5
- output_bias: float32 [2, 512], P('section'), may hold values from -2.5 to 2.5
- feedforward_gain: float32 [2, 512], P('section'), may hold values from 0.5 to 1.5
- feedforward_bias: float32 [2, 512], P('section'), may hold values from -2.5 to 2.5
- up_weight: bfloat16 [2, 512, 2048], P('section'), may hold values from -0.25 to 0.25
- up_bias: float32 [2, 2048], P('section'), may hold values from -2.5 to 2.5
- down_weight: bfloat16 [2, 2048, 512], P('section'), may hold values from -0.125 to 0.125
- down_bias: float32 [2, 512], P('section'), may hold values from -2.5 to 2.5
Outputs:
- activations: bfloat16 [2, 2, 16, 6, 320, 512], P('section', None, 'dp')
- input_grads: bfloat16 [2, 2, 16, 6, 320, 512], P('section', None, 'dp')
- attention_gain_grad: float32 [2, 512], P('section')
- attention_bias_grad: float32 [2, 512], P('section')
- projection_in_grad: float32 [2, 512, 1536], P('section')
- projection_out_grad: float32 [2, 512, 512], P('section')
- output_bias_grad: float32 [2, 512], P('section')
- feedforward_gain_grad: float32 [2, 512], P('section')
- feedforward_bias_grad: float32 [2, 512], P('section')
- up_weight_grad: float32 [2, 512, 2048], P('section')
- up_bias_grad: float32 [2, 2048], P('section')
- down_weight_grad: float32 [2, 2048, 512], P('section')
- down_bias_grad: float32 [2, 512], P('section')
The draws below stay inside these ranges and needn't reach their ends.
Inputs may be any that keep to these rules, and one draw needn't show every extreme that they name: `window_cols`: in every micro-batch some band has 5 windows. `time_groups`: time groups never fall along the frames; every group 0 to 4 holds a frame.
All inputs are finite; a program needn't handle non-finite values.
Results may differ from the reference program's by a relative error of at most 0.02.
Values may be sent and summed in bfloat16 or wider, within the bound.
A program may use at most 384 MiB of HBM per device.

```python
import math
import jax
import jax.numpy as jnp
import numpy as np
from jax import lax

D = 512
FF = 2048
HEADS = 8
MB = 2
TF = 6
TG = 5
WCAP = 5
BAND = 320
BANDS = 16


def draw_window_cols(key, part):
    key = jax.random.fold_in(key, 7)
    first_key, second_key = jax.random.split(key)
    columns = jax.random.randint(first_key, (MB, BANDS), WCAP - 2, WCAP + 1)
    widest = jax.random.randint(second_key, (MB,), 0, BANDS)
    chosen = jnp.arange(BANDS)[None, :] == widest[:, None]
    return jnp.where(chosen, WCAP, columns).astype(jnp.int32)


def levels(rng, extent, shards, least, largest):
    def one(dim, parts):
        steps = jax.random.uniform(jax.random.fold_in(jax.random.fold_in(rng, 6), dim), (parts,), jnp.float32, least / len(shards), largest / len(shards))
        return jnp.repeat(jnp.exp(steps), extent[dim] // parts).reshape((-1,) + (1,) * (len(extent) - dim - 1))

    level = one(*shards[0])
    for cut in shards[1:]:
        level = level * one(*cut)
    return level


def length_profile(count, total, reach, lean):
    weights = [(1 << 20) // math.isqrt(rank ** lean) + 1 for rank in range(2, count + 1)]
    surplus, counts = total - reach - (count - 1), [1] * (count - 1)
    while surplus > 0:
        movable = [i for i in range(count - 1) if counts[i] < reach]
        whole, budget = sum([weights[i] for i in movable]), surplus
        for i in movable:
            addition = min(reach - counts[i], max(1, budget * weights[i] // whole), surplus)
            counts[i] = counts[i] + addition
            surplus = surplus - addition
    return np.array([reach] + counts)


def ragged_sizes(key, count, total, most, lean):
    if count == 2:
        one = jax.random.randint(key, (), max(1, total - most), min(most, total - 1) + 1)
        return jnp.stack([one, total - one])
    sizes = jnp.asarray(length_profile(count, total, most, lean), jnp.int32)
    pairs = (count - 1) // 2
    giver, sink = sizes[1:1 + 2 * pairs:2], sizes[2:2 + 2 * pairs:2]
    room = jnp.minimum(giver - 1, most - sink)
    shifted = jax.random.randint(jax.random.fold_in(key, 1), (pairs,), 0, 1 << 20) % (room + 1)
    sizes = sizes.at[1:1 + 2 * pairs:2].set(giver - shifted).at[2:2 + 2 * pairs:2].set(sink + shifted)
    return sizes[jax.random.permutation(jax.random.fold_in(key, 2), count)]


def normal_values(rng, extent, deviation, most, cuts=(), held_as=jnp.bfloat16):
    factor_of = levels(rng, extent, cuts, -0.22, 0.18) if cuts else 1.0
    drawn = jax.random.normal(rng, extent, jnp.float32) * deviation * factor_of
    return jnp.minimum(jnp.maximum(drawn, -most), most).astype(held_as)


def setup_inputs(seed: int = 0) -> dict:
    key_list = jax.random.split(jax.random.key(seed), 16)
    clip_tokens = normal_values(key_list[0], (MB, BANDS, TF, BAND, D), 1.0, 6.0, ((1, 16),))
    window_cols = draw_window_cols(jax.random.fold_in(key_list[15], 71), 0)
    time_groups = jax.vmap(lambda own: jnp.searchsorted(jnp.cumsum(ragged_sizes(own, TG, TF, TF - TG + 1, 0)), jnp.arange(TF), side="right"))(jax.random.split(key_list[2], MB * BANDS)).reshape((MB, BANDS, TF)).astype(jnp.int32)
    cotangent = normal_values(key_list[3], (MB, BANDS, TF, BAND, D), 1.0, 6.0, ((1, 16),))
    attention_gain = jnp.clip(1.0 + 0.1 * jax.random.normal(key_list[4], (2, D), jnp.float32), 0.5, 1.5)
    attention_bias = normal_values(key_list[5], (2, D), 0.3, 2.5, ((0, 2),), jnp.float32)
    projection_in = normal_values(key_list[6], (2, D, 3 * D), D ** -0.5, 0.25, ((0, 2),))
    projection_out = normal_values(key_list[7], (2, D, D), (D // 4) ** -0.5, 0.5, ((0, 2),))
    output_bias = normal_values(key_list[8], (2, D), 0.3, 2.5, ((0, 2),), jnp.float32)
    feedforward_gain = jnp.clip(1.0 + 0.1 * jax.random.normal(key_list[9], (2, D), jnp.float32), 0.5, 1.5)
    feedforward_bias = normal_values(key_list[10], (2, D), 0.3, 2.5, ((0, 2),), jnp.float32)
    up_weight = normal_values(key_list[11], (2, D, FF), D ** -0.5, 0.25, ((0, 2),))
    up_bias = normal_values(key_list[12], (2, FF), 0.3, 2.5, ((0, 2),), jnp.float32)
    down_weight = normal_values(key_list[13], (2, FF, D), FF ** -0.5, 0.125, ((0, 2),))
    down_bias = normal_values(key_list[14], (2, D), 0.3, 2.5, ((0, 2),), jnp.float32)
    return dict(clip_tokens=clip_tokens, window_cols=window_cols, time_groups=time_groups, cotangent=cotangent, attention_gain=attention_gain, attention_bias=attention_bias, projection_in=projection_in, projection_out=projection_out, output_bias=output_bias, feedforward_gain=feedforward_gain, feedforward_bias=feedforward_bias, up_weight=up_weight, up_bias=up_bias, down_weight=down_weight, down_bias=down_bias)


@jax.custom_vjp
def low(v):
    return lax.optimization_barrier(v.astype(jnp.bfloat16)).astype(jnp.float32)

@jax.custom_vjp
def low_back(v):
    return v

def low_keep(v):
    return (low(v), None)

def low_pass(kept, grad):
    return (grad,)

def back_keep(v):
    return (v, None)

def back_low(kept, grad):
    return (low(grad),)
low.defvjp(low_keep, low_pass)
low_back.defvjp(back_keep, back_low)
EPSILON = 1e-05
MASKED = -1e+30
HIGHEST = lax.Precision.HIGHEST

def normalize(values, gain, shift):
    center = lax.optimization_barrier(jnp.mean(values, axis=-1, keepdims=True))
    centered = values - center
    spread = lax.optimization_barrier(jnp.mean(centered * centered, axis=-1, keepdims=True))
    return centered * lax.rsqrt(spread + EPSILON) * gain + shift

def attend_windows(query, keys, values, scale, window):
    count = query.shape[0] // window
    head_dim = query.shape[1] // HEADS
    q_win = query.reshape(count, window, HEADS, head_dim)
    k_win = keys.reshape(count, window, HEADS, head_dim)
    v_win = values.reshape(count, window, HEADS, head_dim)
    scores = low_back(scale * jnp.einsum('gqhd,gkhd->ghqk', q_win, k_win, precision=HIGHEST))
    total = jax.nn.logsumexp(scores, axis=-1, keepdims=True)
    probs = low(jnp.exp(scores - total))
    mixed = jnp.einsum('ghqk,gkhd->gqhd', probs, v_win, precision=HIGHEST)
    return mixed.reshape(query.shape[0], query.shape[1])

def attend_frames(query, keys, values, scale, allowed):
    frames = allowed.shape[0]
    head_dim = query.shape[1] // HEADS
    q_frm = query.reshape(frames, -1, HEADS, head_dim)
    k_frm = keys.reshape(frames, -1, HEADS, head_dim)
    v_frm = values.reshape(frames, -1, HEADS, head_dim)
    scores = low_back(scale * jnp.einsum('ibhd,jbhd->bhij', q_frm, k_frm, precision=HIGHEST))
    scores = jnp.where(allowed, scores, MASKED)
    total = jax.nn.logsumexp(scores, axis=-1, keepdims=True)
    probs = low(jnp.exp(scores - total))
    mixed = jnp.einsum('bhij,jbhd->ibhd', probs, v_frm, precision=HIGHEST)
    return mixed.reshape(query.shape[0], query.shape[1])

def block(tokens, weights, spatial, live_rows, allowed, window):
    attention_gain, attention_bias, projection_in, projection_out, output_bias, feedforward_gain, feedforward_bias, up_weight, up_bias, down_weight, down_bias = weights
    width = tokens.shape[1]
    normed = low(normalize(tokens, attention_gain, attention_bias))
    joint = low_back(low(jnp.dot(normed, projection_in, precision=HIGHEST)))
    query = joint[:, :width]
    keys = joint[:, width:2 * width]
    values = joint[:, 2 * width:]
    scale = (width // HEADS) ** (-0.5)
    if spatial:
        mixed = attend_windows(query, keys, values, scale, window)
    else:
        mixed = attend_frames(query, keys, values, scale, allowed)
    mixed = low_back(low(mixed))
    branch = low_back(jnp.dot(mixed, projection_out, precision=HIGHEST) + output_bias)
    middle = tokens + branch
    normed_two = low(normalize(middle, feedforward_gain, feedforward_bias))
    hidden_pre = low_back(jnp.dot(normed_two, up_weight, precision=HIGHEST) + up_bias)
    hidden = low(jax.nn.gelu(hidden_pre, approximate=False))
    branch_two = low_back(jnp.dot(hidden, down_weight, precision=HIGHEST) + down_bias)
    return live_rows * (middle + branch_two)

def reference(clip_tokens, window_cols, time_groups, cotangent, attention_gain, attention_bias, projection_in, projection_out, output_bias, feedforward_gain, feedforward_bias, up_weight, up_bias, down_weight, down_bias):
    micro, bands, frames, band, width = clip_tokens.shape
    row_count = frames * band
    window = band // WCAP
    stacked = (attention_gain, attention_bias, projection_in, projection_out, output_bias, feedforward_gain, feedforward_bias, up_weight, up_bias, down_weight, down_bias)
    weights_spatial = tuple((weight[0].astype(jnp.float32) for weight in stacked))
    weights_temporal = tuple((weight[1].astype(jnp.float32) for weight in stacked))
    flat_tokens = clip_tokens.reshape(micro * bands, row_count, width)
    flat_cot = cotangent.reshape(micro * bands, row_count, width)
    flat_cols = window_cols.reshape(micro * bands)
    flat_groups = time_groups.reshape(micro * bands, frames)
    slot_window = jnp.arange(row_count, dtype=jnp.int32) % band // window

    def per_item(carry, item):
        tokens_low, cot_low, cols, labels = item
        live_rows = (slot_window < cols).astype(jnp.float32)[:, None]
        allowed = labels[None, :] <= labels[:, None]

        def two_blocks(tokens, delta, first_weights, second_weights):
            spatial_out = block(tokens, first_weights, True, live_rows, allowed, window)
            passed = low_back(low(spatial_out))
            temporal_out = block(passed + delta, second_weights, False, live_rows, allowed, window)
            return (spatial_out, temporal_out)
        tokens = tokens_low.astype(jnp.float32)
        outputs, pullback = jax.vjp(two_blocks, tokens, jnp.zeros_like(tokens), weights_spatial, weights_temporal)
        tokens_grad, delta_grad, spatial_grads, temporal_grads = pullback((jnp.zeros_like(tokens), cot_low.astype(jnp.float32)))
        totals_spatial = jax.tree.map(jnp.add, carry[0], spatial_grads)
        totals_temporal = jax.tree.map(jnp.add, carry[1], temporal_grads)
        results = (outputs[0].astype(jnp.bfloat16), outputs[1].astype(jnp.bfloat16), tokens_grad.astype(jnp.bfloat16), delta_grad.astype(jnp.bfloat16))
        return ((totals_spatial, totals_temporal), results)
    start = (jax.tree.map(jnp.zeros_like, weights_spatial), jax.tree.map(jnp.zeros_like, weights_temporal))
    totals, results = lax.scan(per_item, start, (flat_tokens, flat_cot, flat_cols, flat_groups))
    shape_six = (micro, bands, frames, band, width)
    activations = jnp.stack([results[0].reshape(shape_six), results[1].reshape(shape_six)])
    input_grads = jnp.stack([results[2].reshape(shape_six), results[3].reshape(shape_six)])
    grads = [jnp.stack([spatial_part, temporal_part]) for spatial_part, temporal_part in zip(totals[0], totals[1])]
    return (activations, input_grads, grads[0], grads[1], grads[2], grads[3], grads[4], grads[5], grads[6], grads[7], grads[8], grads[9], grads[10])
```

```python
from collections import namedtuple
from functools import partial

import jax
import jax.numpy as jnp
from jax import lax
from jax.experimental import pallas as pl
from jax.experimental.pallas import tpu as pltpu
from jax.sharding import PartitionSpec as P

HEADS = 8
WCAP = 5
EPSILON = 1e-05
MASKED = -1e30
MESH = pl.DeviceIdType.MESH

F32 = jnp.float32
BF16 = jnp.bfloat16

LEAD = 4
SLOTS = LEAD + 1
Kept = namedtuple("Kept", ("x", "a1t", "qkv", "p", "ot", "xh2", "a2t", "rs2", "h", "g"))
FF_BLOCK = 512
ROWS_AT_ONCE = 32
COLS_AT_ONCE = 256

INV_SQRT2 = 0.7071067811865476
PDF = 0.3989422804014327
LOG2E = 1.4426950408889634


def mm(a, b):
    return lax.dot_general(a, b, (((1,), (0,)), ((), ())), preferred_element_type=F32)


def mm_bt(a, b):
    return lax.dot_general(a, b, (((1,), (1,)), ((), ())), preferred_element_type=F32)


def mm_at(a, b):
    return lax.dot_general(a, b, (((0,), (0,)), ((), ())), preferred_element_type=F32)


def gelu_and_slope(u):
    cdf = 0.5 + 0.5 * lax.erf(INV_SQRT2 * u)
    bell = jnp.exp2((-0.5 * LOG2E) * (u * u))
    return u * cdf, cdf + (PDF * u) * bell


def fold8(values):
    rows, cols = values.shape
    return jnp.sum(values.reshape(rows // 8, 8, cols), axis=0)


GROUP = 16
LINE = 4
LINE_ORDER = (3, 0, 2, 1)
UNIT = 384
PIECE = 128
WHOLE = slice(0, UNIT)
ACROSS_FIRST = slice(0, 256)
LINE_FIRST = slice(256, UNIT)
PART = {1: ACROSS_FIRST, 2: LINE_FIRST}
SIDES = {1: (0,), 2: (0, 1)}
FAMILIES = 32
VECTOR_ROWS = 16


def group_place():
    me = lax.axis_index("dp")
    core, across, line = lax.rem(me, 2), lax.rem(lax.div(me, 2), 2), lax.rem(lax.div(me, 4), LINE)
    sibling, beside = {"dp": me + 1 - 2 * core}, {"dp": me + 2 - 4 * across}
    return core, across, line, sibling, beside, {"dp": me + 4}, {"dp": me - 4}


def sum_over_group(packed, result, landing, vector, flat_ref, vector_ref, send_sem, recv_sem, out_sem, ready):
    core, across, line, sibling, beside, above, below = group_place()
    sides = (across, 1 - across)
    families = {}
    pending = []

    def when(condition, action):
        if condition is None:
            action()
        else:
            pl.when(condition)(action)

    def remote(family, place, source, target, device):
        number = families.setdefault(family, len(families)) * LINE + place
        return pltpu.make_async_remote_copy(
            src_ref=source,
            dst_ref=target,
            send_sem=send_sem.at[number],
            recv_sem=recv_sem.at[number],
            device_id=device,
            device_id_type=MESH,
        )

    def start(family, place, source, target, device):
        remote(family, place, source, target, device).start()

    def sent(family, place, source, device, condition=None):
        pending.append((condition, lambda: remote(family, place, source, source, device).wait_send()))

    def received(family, place, target, device):
        remote(family, place, target, target, device).wait_recv()

    def unit(ref, half, side, place, part):
        column = place * 512 if isinstance(place, int) else pl.multiple_of(place * 512, 512)
        return ref.at[half * 2 + side, part, pl.ds(column, 512)]

    def add(target, arrived):
        for r in range(0, target.shape[0], 64):
            at = slice(r, r + 64)
            target[at] = (target[at].astype(F32) + arrived[at].astype(F32)).astype(BF16)

    def store(far, rel, place, kind):
        half, side, part = (1 - core if far else core), sides[rel], PART[kind]
        row = pl.multiple_of(((half * 2 + side) * LINE + place) * UNIT + part.start, PIECE)
        return pltpu.make_async_copy(
            unit(result, half, side, place, part),
            flat_ref.at[pl.ds(row, part.stop - part.start)],
            out_sem.at[((far * 2 + rel) * 2 + kind - 1) * LINE + place],
        )

    for number, (device, condition) in enumerate(
        ((sibling, None), (beside, None), (below, line > 0), (above, line < LINE - 1))
    ):
        there = number if number < 2 else 5 - number
        when(
            condition,
            partial(pl.semaphore_signal, ready.at[there], inc=1, device_id=device, device_id_type=MESH),
        )
    pl.semaphore_wait(ready.at[0], 1)

    start("vector core", 0, vector.at[0], vector.at[1], sibling)
    sent("vector core", 0, vector.at[0], sibling)
    for place in LINE_ORDER:
        for side in range(2):
            source = unit(packed, 1 - core, side, place, WHOLE)
            start(("core", side), place, source, landing("core", side, place), sibling)
            sent(("core", side), place, source, sibling)
    pl.semaphore_wait(ready.at[1], 1)
    pl.when(line > 0)(lambda: pl.semaphore_wait(ready.at[2], 1))
    pl.when(line < LINE - 1)(lambda: pl.semaphore_wait(ready.at[3], 1))

    def line_send(kind, place, up, condition):
        device = above if up else below

        def go():
            for rel in SIDES[kind]:
                source = unit(packed, core, sides[rel], place, PART[kind])
                start((kind, up, rel), place, source, landing((kind, up), rel, place), device)

        pl.when(condition)(go)
        for rel in SIDES[kind]:
            sent((kind, up, rel), place, unit(packed, core, sides[rel], place, PART[kind]), device, condition)

    def line_take(kind, place, up, condition):
        def go():
            for rel in SIDES[kind]:
                spot = landing((kind, up), rel, place)
                received((kind, up, rel), place, spot, below if up else above)
                add(unit(packed, core, sides[rel], place, PART[kind]), spot)

        pl.when(condition)(go)

    def from_ends(kind, place):
        if place > 0:
            line_send(kind, place, True, line == 0)
        if place < LINE - 1:
            line_send(kind, place, False, line == LINE - 1)

    def inner_step(kind, k):
        place = LINE - 1 - k
        line_take(kind, place, True, (line > 0) & (line <= place))
        if place > 1:
            line_send(kind, place, True, (line > 0) & (line < place))
        place = k
        line_take(kind, place, False, (line < LINE - 1) & (line >= place))
        if place < LINE - 2:
            line_send(kind, place, False, (line < LINE - 1) & (line > place))

    def take_across(place):
        spot = landing("across", 0, place)
        received("across", place, spot, beside)
        add(unit(packed, core, sides[0], place, ACROSS_FIRST), spot)
        from_ends(1, place)

    for place in LINE_ORDER:
        for side in range(2):
            spot = landing("core", side, place)
            received(("core", side), place, spot, sibling)
            add(unit(packed, core, side, place, WHOLE), spot)
        source = unit(packed, core, sides[1], place, ACROSS_FIRST)
        start("across", place, source, landing("across", 0, place), beside)
        sent("across", place, source, beside)
        from_ends(2, place)
    received("vector core", 0, vector.at[1], sibling)
    vector[2] = vector[0] + vector[1]
    start("vector across", 0, vector.at[2], vector.at[3], beside)
    sent("vector across", 0, vector.at[2], beside)
    for k in range(LINE - 1):
        take_across(LINE_ORDER[k])
        inner_step(2, k)
    take_across(LINE_ORDER[LINE - 1])
    source = unit(packed, core, sides[1], line, LINE_FIRST)
    start("across 2", 0, source, landing("across 2", 0, 0), beside)
    sent("across 2", 0, source, beside)
    received("vector across", 0, vector.at[3], beside)
    vector[4 + line] = vector[2] + vector[3]
    inner_step(1, 0)
    inner_step(1, 1)
    spot = landing("across 2", 0, 0)
    received("across 2", 0, spot, beside)
    own = unit(packed, core, sides[0], line, LINE_FIRST)
    add(own, spot)
    own_two = unit(result, core, sides[0], line, LINE_FIRST)
    own_two[...] = own[...]
    start("gather across 2", 0, own_two, own_two, beside)
    sent("gather across 2", 0, own_two, beside)
    inner_step(1, 2)
    own_one = unit(result, core, sides[0], line, ACROSS_FIRST)
    own_one[...] = unit(packed, core, sides[0], line, ACROSS_FIRST)[...]

    def spread(family, place, spot, up, down):
        if up is not None:
            pl.when(up)(lambda: start((family, True), place, spot, spot, above))
        if down is not None:
            pl.when(down)(lambda: start((family, False), place, spot, spot, below))

    def hand_over(kind, rel, place):
        spot = unit(result, core, sides[rel], place, PART[kind])
        start(("gather core", kind, rel), place, spot, spot, sibling)
        store(0, rel, place, kind).start()

    def have(kind, rel, place, up, down):
        spot = unit(result, core, sides[rel], place, PART[kind])
        spread(("spread", kind, rel), place, spot, up, down)
        if kind == 1:
            start("gather across", place, spot, spot, beside)
        hand_over(kind, rel, place)

    def come(distance, action):
        pl.when(line >= distance)(lambda: action(line - distance, True))
        pl.when(line + distance < LINE)(lambda: action(line + distance, False))

    def arrive(kind, rel, distance):
        def action(place, up):
            spot = unit(result, core, sides[rel], place, PART[kind])
            received((("spread", kind, rel), up), place, spot, below if up else above)
            have(kind, rel, place, line < LINE - 1 if up else None, None if up else line > 0)

        come(distance, action)

    def arrive_vector(distance):
        def action(place, up):
            spot = vector.at[4 + place]
            received(("vector", up), place, spot, below if up else above)
            spread("vector", place, spot, line < LINE - 1 if up else None, None if up else line > 0)

        come(distance, action)

    def arrive_across(distance):
        def action(place, up):
            received("gather across", place, unit(result, core, sides[1], place, ACROSS_FIRST), beside)
            hand_over(1, 1, place)

        if distance == 0:
            action(line, True)
        else:
            come(distance, action)

    have(1, 0, line, line < LINE - 1, line > 0)
    have(2, 0, line, line < LINE - 1, line > 0)
    spread("vector", line, vector.at[4 + line], line < LINE - 1, line > 0)
    received("gather across 2", 0, unit(result, core, sides[1], line, LINE_FIRST), beside)
    have(2, 1, line, line < LINE - 1, line > 0)
    for distance in range(1, LINE):
        arrive(1, 0, distance)
        arrive(2, 0, distance)
        arrive(2, 1, distance)
        arrive_vector(distance)
        arrive_across(distance - 1)
    arrive_across(LINE - 1)
    vector[1] = (vector[4] + vector[5]) + (vector[6] + vector[7])
    vector_out = pltpu.make_async_copy(vector.at[1], vector_ref, out_sem.at[2 * GROUP])
    vector_out.start()
    for place in range(LINE):
        for kind in (1, 2):
            for rel in range(2):
                spot = unit(result, 1 - core, sides[rel], place, PART[kind])
                received(("gather core", kind, rel), place, spot, sibling)
                store(1, rel, place, kind).start()
    vector_out.wait()

    for place in range(LINE):
        for kind in (1, 2):
            for rel in range(2):
                spot = unit(result, core, sides[rel], place, PART[kind])
                sent(("gather core", kind, rel), place, spot, sibling)
                store(0, rel, place, kind).wait()
                store(1, rel, place, kind).wait()
            for rel in SIDES[kind]:
                spot = unit(result, core, sides[rel], place, PART[kind])
                sent((("spread", kind, rel), True), place, spot, above, (line >= place) & (line < LINE - 1))
                sent((("spread", kind, rel), False), place, spot, below, (line <= place) & (line > 0))
        sent("gather across", place, unit(result, core, sides[0], place, ACROSS_FIRST), beside)
        sent(("vector", True), place, vector.at[4 + place], above, (line >= place) & (line < LINE - 1))
        sent(("vector", False), place, vector.at[4 + place], below, (line <= place) & (line > 0))
    for condition, wait in pending:
        when(condition, wait)


def relay_kernel(
    dims,
    cols_ref,
    groups_ref,
    clip_ref,
    cot_ref,
    attention_gain,
    attention_bias,
    projection_in,
    projection_out,
    output_bias,
    feedforward_gain,
    feedforward_bias,
    up_weight,
    up_bias,
    down_weight,
    down_bias,
    act_ref,
    grad_ref,
    flat_ref,
    vector_ref,
    *scratch,
):
    micro, frames, window, width, hidden, grouped = dims
    parked, scratch = scratch[: len(Kept._fields) - 1], scratch[len(Kept._fields) - 1 :]
    kept_a, scratch = Kept(*scratch[: len(Kept._fields)]), scratch[len(Kept._fields) :]
    kept_b, scratch = Kept(*scratch[: len(Kept._fields)]), scratch[len(Kept._fields) :]
    (
    d_projection_in,
    d_projection_out,
    d_up_weight,
    d_down_weight,
    xbuf,
    dybuf,
    ybuf,
    dxbuf,
    a1_buf,
    pf_buf,
    ds_buf,
    o_buf,
    a2_buf,
    wide,
    total,
    u_buf,
    e_buf,
    et_buf,
    c_buf,
    do_buf,
    dqkv_buf,
    qkvt_buf,
    dot_buf,
    dqkvt_buf,
    sum_ag,
    sum_ab,
    sum_ob,
    sum_fg,
    sum_fb,
    sum_ub,
    sum_db,
    x_sem,
    dy_sem,
    y_sem,
    y_send,
    dx_sem,
    dx_send,
    packed,
    result,
    park_sem,
    fetch_sem,
    vector,
    group_send,
    group_recv,
    group_out,
    ready,
    ) = scratch
    rows = frames * window
    count = micro * WCAP
    head = width // HEADS
    pair = 2 * head
    scale = head ** (-0.5)
    section = lax.axis_index("section")
    leading = section == 0
    trailing = section != 0
    lead = LEAD * (1 - section)
    partner = {"section": 1 - section}

    def hbm_chunk(ref, chunk):
        start = pl.multiple_of(lax.rem(chunk, WCAP) * window, window)
        return ref.at[lax.div(chunk, WCAP), :, pl.ds(start, window), :]

    def x_load(chunk):
        slot = lax.rem(chunk, SLOTS)
        return pltpu.make_async_copy(hbm_chunk(clip_ref, chunk), xbuf.at[slot], x_sem.at[slot])

    def dy_load(chunk):
        slot = lax.rem(chunk, SLOTS)
        return pltpu.make_async_copy(hbm_chunk(cot_ref, chunk), dybuf.at[slot], dy_sem.at[slot])

    def y_store(chunk):
        slot = lax.rem(chunk, 2)
        return pltpu.make_async_copy(ybuf.at[slot], hbm_chunk(act_ref, chunk), y_sem.at[slot])

    def dx_store(chunk):
        slot = lax.rem(chunk, 2)
        return pltpu.make_async_copy(dxbuf.at[slot], hbm_chunk(grad_ref, chunk), dx_sem.at[slot])

    def park(chunk):
        slot = lax.rem(chunk, SLOTS)
        return [
            pltpu.make_async_copy(here, there.at[slot], park_sem.at[n])
            for n, (here, there) in enumerate(zip(kept_a[1:], parked))
        ]

    def fetch(chunk):
        slot = lax.rem(chunk, SLOTS)
        return [pltpu.make_async_copy(hbm_chunk(clip_ref, chunk), kept_b.x, fetch_sem.at[0])] + [
            pltpu.make_async_copy(there.at[slot], here, fetch_sem.at[n + 1])
            for n, (here, there) in enumerate(zip(kept_b[1:], parked))
        ]

    def start_all(copies):
        for copy in copies:
            copy.start()

    def wait_all(copies):
        for copy in copies:
            copy.wait()

    def y_remote(chunk):
        slot, there = lax.rem(chunk, 2), lax.rem(chunk, SLOTS)
        return pltpu.make_async_remote_copy(
            src_ref=ybuf.at[slot],
            dst_ref=xbuf.at[there],
            send_sem=y_send.at[slot],
            recv_sem=x_sem.at[there],
            device_id=partner,
            device_id_type=MESH,
        )

    def dx_remote(chunk):
        slot, there = lax.rem(chunk, 2), lax.rem(chunk, SLOTS)
        return pltpu.make_async_remote_copy(
            src_ref=dxbuf.at[slot],
            dst_ref=dybuf.at[there],
            send_sem=dx_send.at[slot],
            recv_sem=dy_sem.at[there],
            device_id=partner,
            device_id_type=MESH,
        )

    barrier = pltpu.get_barrier_semaphore()
    greeted = 1
    pl.semaphore_signal(barrier, inc=1, device_id=partner, device_id_type=MESH)
    if grouped:
        _, _, line, sibling, beside, above, below = group_place()
        has_below, has_above = line > 0, line < LINE - 1
        for device, condition in ((sibling, None), (beside, None), (below, has_below), (above, has_above)):
            greet = partial(pl.semaphore_signal, barrier, inc=1, device_id=device, device_id_type=MESH)
            if condition is None:
                greet()
            else:
                pl.when(condition)(greet)
        greeted = 3 + has_below.astype(jnp.int32) + has_above.astype(jnp.int32)

    @pl.when(leading)
    def _():
        x_load(0).start()

    @pl.when(trailing)
    def _():
        dy_load(0).start()

    for total_ref in (d_projection_in, d_projection_out, d_up_weight, d_down_weight):
        total_ref[...] = jnp.zeros_like(total_ref)
    for total_ref in (sum_ag, sum_ab, sum_ob, sum_fg, sum_fb, sum_ub, sum_db):
        total_ref[...] = jnp.zeros_like(total_ref)

    pl.semaphore_wait(barrier, greeted)

    def frame_rows(i):
        return slice(i * window, (i + 1) * window)

    half = lax.broadcasted_iota(jnp.int32, (window, pair), 1) < head
    low_half = jnp.where(half, 1.0, 0.0).astype(BF16)
    high_half = jnp.where(half, 0.0, 1.0).astype(BF16)

    def by_head(values):
        return jnp.concatenate([values * low_half, values * high_half], axis=0)

    def join_heads(values):
        return jnp.where(half, values[:window], values[window:])

    heads_of = [
        (frame_rows(f), slice(n * pair, (n + 1) * pair), n) for f in range(frames) for n in range(width // pair)
    ]

    def of_pair(ref, at, which, n):
        return ref[at, which * width + n * pair : which * width + (n + 1) * pair]

    def window_forward(kept):
        for at, lanes, n in heads_of:
            keys = of_pair(kept.qkv, at, 1, n)
            total[at, lanes] = mm_bt(keys, by_head(of_pair(kept.qkv, at, 0, n)))
        yield
        for at, lanes, n in heads_of:
            scores = total[at, lanes] * scale
            scores = jnp.exp(scores - jnp.max(scores, axis=0, keepdims=True))
            probs = scores * (1.0 / jnp.sum(scores, axis=0, keepdims=True))
            kept.p[at, lanes] = probs.astype(BF16)
        yield
        for at, lanes, n in heads_of:
            values = of_pair(kept.qkv, at, 2, n)
            o_buf[at, lanes] = join_heads(mm_at(kept.p[at, lanes], values)).astype(BF16)

    def window_backward(kept):
        for at, lanes, n in heads_of:
            up = by_head(do_buf[at, lanes])
            total[at, lanes] = mm_bt(of_pair(kept.qkv, at, 2, n), up)
            dv = mm(kept.p[at, lanes], up)
            dqkv_buf[at, 2 * width + n * pair : 2 * width + (n + 1) * pair] = dv.astype(BF16)
        yield
        for at, lanes, n in heads_of:
            probs = kept.p[at, lanes].astype(F32)
            dp = total[at, lanes]
            ds = probs * (dp - jnp.sum(probs * dp, axis=0, keepdims=True))
            e_buf[at, lanes] = ds.astype(BF16)
        yield
        for at, lanes, n in heads_of:
            ds = e_buf[at, lanes]
            dk = mm(ds, by_head(of_pair(kept.qkv, at, 0, n))) * scale
            dqkv_buf[at, width + n * pair : width + (n + 1) * pair] = dk.astype(BF16)
            dq = join_heads(mm_at(ds, of_pair(kept.qkv, at, 1, n))) * scale
            dqkv_buf[at, lanes] = dq.astype(BF16)

    low_frame = lax.broadcasted_iota(jnp.int32, (1, 128), 1) < window

    def lane_tiles(i):
        return min(i + 1, frames - 1) // 2 + 1

    def tile(t):
        return slice(t * 128, (t + 1) * 128)

    def head_rows(which, h):
        return slice(which * width + h * head, which * width + (h + 1) * head)

    def other_half(values):
        return pltpu.roll(values, window, axis=1)

    def both_frames(ref, at, t):
        values = ref[at, tile(t)]
        turned = other_half(values)
        return jnp.where(low_frame, values, turned), jnp.where(low_frame, turned, values)

    def frame_forward(chunk, kept):
        tile_count = frames // 2
        for n in range(3):
            flat = kept.qkv[:, n * width : (n + 1) * width].T
            qkvt_buf[n * width : (n + 1) * width, :] = flat.astype(F32)
        for h in range(HEADS):
            keys = [qkvt_buf[head_rows(1, h), tile(t)] for t in range(tile_count)]
            for pair_index in range(tile_count):
                queries = both_frames(qkvt_buf, head_rows(0, h), pair_index)
                for i in (2 * pair_index, 2 * pair_index + 1):
                    for t in range(lane_tiles(i)):
                        score = jnp.sum(queries[i % 2] * keys[t], axis=0, keepdims=True)
                        ds_buf[i * tile_count + t, h : h + 1, :] = score
        yield
        item = lax.div(chunk, WCAP)
        labels = [
            jnp.where(low_frame, groups_ref[item, 0, 2 * t], groups_ref[item, 0, 2 * t + 1])
            for t in range(tile_count)
        ]
        for i in range(frames):
            mine = groups_ref[item, 0, i]
            parts = [
                jnp.where(labels[t] <= mine, ds_buf[i * tile_count + t] * scale, MASKED)
                for t in range(lane_tiles(i))
            ]
            largest = parts[0]
            for part in parts[1:]:
                largest = jnp.maximum(largest, part)
            largest = jnp.maximum(largest, other_half(largest))
            parts = [jnp.exp(part - largest) for part in parts]
            whole = parts[0]
            for part in parts[1:]:
                whole = whole + part
            whole = 1.0 / (whole + other_half(whole))
            for t, part in enumerate(parts):
                pf_buf[i * tile_count + t] = part * whole
        yield
        for h in range(HEADS):
            values = [qkvt_buf[head_rows(2, h), tile(t)] for t in range(tile_count)]
            for pair_index in range(tile_count):
                mixed = []
                for i in (2 * pair_index, 2 * pair_index + 1):
                    part = 0.0
                    for t in range(lane_tiles(i)):
                        part = part + pf_buf[i * tile_count + t, h : h + 1, :] * values[t]
                    mixed.append(part + other_half(part))
                both = jnp.where(low_frame, mixed[0], mixed[1])
                kept.ot[head_rows(0, h), tile(pair_index)] = both.astype(BF16)

    def frame_backward(kept):
        tile_count = frames // 2
        for h in range(HEADS):
            values = [qkvt_buf[head_rows(2, h), tile(t)] for t in range(tile_count)]
            dv = [0.0] * tile_count
            for pair_index in range(tile_count):
                ups = both_frames(dot_buf, head_rows(0, h), pair_index)
                for i in (2 * pair_index, 2 * pair_index + 1):
                    for t in range(lane_tiles(i)):
                        ds_buf[i * tile_count + t, h : h + 1, :] = jnp.sum(
                            ups[i % 2] * values[t], axis=0, keepdims=True
                        )
                        dv[t] = dv[t] + pf_buf[i * tile_count + t, h : h + 1, :] * ups[i % 2]
            for t in range(tile_count):
                dqkvt_buf[head_rows(2, h), tile(t)] = dv[t].astype(BF16)
        yield
        for i in range(frames):
            spots = [i * tile_count + t for t in range(lane_tiles(i))]
            along = pf_buf[spots[0]] * ds_buf[spots[0]]
            for spot in spots[1:]:
                along = along + pf_buf[spot] * ds_buf[spot]
            along = along + other_half(along)
            for spot in spots:
                ds_buf[spot] = pf_buf[spot] * (ds_buf[spot] - along) * scale
        yield
        for h in range(HEADS):
            keys = [qkvt_buf[head_rows(1, h), tile(t)] for t in range(tile_count)]
            dk = [0.0] * tile_count
            for pair_index in range(tile_count):
                queries = both_frames(qkvt_buf, head_rows(0, h), pair_index)
                dq = []
                for i in (2 * pair_index, 2 * pair_index + 1):
                    part = 0.0
                    for t in range(lane_tiles(i)):
                        ds = ds_buf[i * tile_count + t, h : h + 1, :]
                        part = part + ds * keys[t]
                        dk[t] = dk[t] + ds * queries[i % 2]
                    dq.append(part + other_half(part))
                both = jnp.where(low_frame, dq[0], dq[1])
                dqkvt_buf[head_rows(0, h), tile(pair_index)] = both.astype(BF16)
            for t in range(tile_count):
                dqkvt_buf[head_rows(1, h), tile(t)] = dk[t].astype(BF16)
        yield
        for n in range(3):
            dqkv_buf[:, n * width : (n + 1) * width] = dqkvt_buf[n * width : (n + 1) * width, :].T

    def live_of(chunk):
        cols = cols_ref[lax.div(chunk, WCAP), 0]
        return jnp.where(lax.rem(chunk, WCAP) < cols, 1.0, 0.0).astype(F32)

    def standardize(values):
        centered = values - jnp.mean(values, axis=-1, keepdims=True)
        rstd = lax.rsqrt(jnp.mean(centered * centered, axis=-1, keepdims=True) + EPSILON)
        return centered * rstd, rstd

    blocks = [
        (slice(r, r + ROWS_AT_ONCE), r // window, slice(r % window, r % window + ROWS_AT_ONCE))
        for r in range(0, rows, ROWS_AT_ONCE)
    ]
    ff_parts = [slice(c, c + FF_BLOCK) for c in range(0, hidden, FF_BLOCK)]

    def halves(cols, start=0, step=COLS_AT_ONCE):
        return [slice(c, c + step) for c in range(start, start + cols, step)]

    def forward(spatial, chunk, kept, slot, y_slot):
        kept.x[...] = xbuf[slot]
        for at, f, within in blocks:
            unit, _ = standardize(kept.x[f, within].astype(F32))
            a1_buf[at, :] = (unit * attention_gain[...] + attention_bias[...]).astype(BF16)
        yield
        kept.a1t[...] = a1_buf[...].T
        for part in halves(3 * width, step=width):
            kept.qkv[:, part] = mm(a1_buf[...], projection_in[:, part]).astype(BF16)
        yield
        if spatial:
            yield from window_forward(kept)
            yield
            kept.ot[...] = o_buf[...].T
        else:
            yield from frame_forward(chunk, kept)
            yield
            o_buf[...] = kept.ot[...].T
        wide[...] = mm(o_buf[...], projection_out[...])
        yield
        for at, f, within in blocks:
            middle = kept.x[f, within].astype(F32) + (wide[at, :] + output_bias[...])
            wide[at, :] = middle + down_bias[...]
            unit, rstd = standardize(middle)
            kept.xh2[at, :] = unit.astype(BF16)
            kept.rs2[at, :] = jnp.broadcast_to(rstd, (ROWS_AT_ONCE, 128))
            a2_buf[at, :] = (unit * feedforward_gain[...] + feedforward_bias[...]).astype(BF16)
        yield
        kept.a2t[...] = a2_buf[...].T
        u_buf[0] = mm(a2_buf[...], up_weight[:, ff_parts[0]])
        yield
        for n, part in enumerate(ff_parts):
            if n + 1 < len(ff_parts):
                u_buf[(n + 1) % 2] = mm(a2_buf[...], up_weight[:, ff_parts[n + 1]])
            for at, _, _ in blocks:
                for inner, outer in zip(halves(FF_BLOCK), halves(FF_BLOCK, part.start)):
                    h, slope = gelu_and_slope(u_buf[n % 2, at, inner] + up_bias[:, outer])
                    kept.h[at, outer] = h.astype(BF16)
                    kept.g[at, outer] = slope.astype(BF16)
            yield
        total[...] = mm(kept.h[...], down_weight[...])
        yield
        live = live_of(chunk)
        for at, f, within in blocks:
            ybuf[y_slot, f, within] = ((wide[at, :] + total[at, :]) * live).astype(BF16)
        y_store(chunk).start()
        if spatial:
            y_remote(chunk).start()

    def norm_backward(d_normed, unit, rstd, gain):
        d_unit = d_normed * gain
        along = jnp.mean(d_unit * unit, axis=-1, keepdims=True)
        return rstd * (d_unit - jnp.mean(d_unit, axis=-1, keepdims=True) - unit * along)

    def weight_gradient(total_ref, left, right, cols):
        for part in cols:
            total_ref[:, part] += mm(left[...], right[:, part])

    def backward(spatial, chunk, kept, slot, dx_slot):
        if spatial:
            dx_remote(chunk).wait_recv()
        else:
            dy_load(chunk).wait()

        @pl.when(chunk >= 2)
        def _():
            dx_store(chunk - 2).wait()
            if not spatial:
                dx_remote(chunk - 2).wait_send()

        live = live_of(chunk)
        e_buf[...] = (dybuf[slot].reshape(rows, width).astype(F32) * live).astype(BF16)
        for at, f, within in blocks:
            sum_db[...] += fold8(e_buf[at, :].astype(F32))
        yield
        et_buf[...] = e_buf[...].T
        u_buf[0] = mm_bt(e_buf[...], down_weight[ff_parts[0], :])
        yield
        for n, part in enumerate(ff_parts):
            if n + 1 < len(ff_parts):
                u_buf[(n + 1) % 2] = mm_bt(e_buf[...], down_weight[ff_parts[n + 1], :])
            weight_gradient(d_down_weight, et_buf, kept.h, halves(FF_BLOCK, part.start))
            for at, _, _ in blocks:
                for inner, outer in zip(halves(FF_BLOCK), halves(FF_BLOCK, part.start)):
                    du = u_buf[n % 2, at, inner] * kept.g[at, outer].astype(F32)
                    sum_ub[:, outer] += fold8(du)
                    kept.g[at, outer] = du.astype(BF16)
            yield
        total[...] = mm_bt(kept.g[...], up_weight[...])
        yield
        for n, (at, _, _) in enumerate(blocks):
            if n % 3 == 0:
                weight_gradient(d_up_weight, kept.a2t, kept.g, halves(FF_BLOCK, n // 3 * FF_BLOCK))
            d_normed = total[at, :]
            unit = kept.xh2[at, :].astype(F32)
            sum_fg[...] += fold8(d_normed * unit)
            sum_fb[...] += fold8(d_normed)
            rstd = kept.rs2[at, 0:1]
            d_middle = e_buf[at, :].astype(F32) + norm_backward(d_normed, unit, rstd, feedforward_gain[...])
            wide[at, :] = d_middle
            sum_ob[...] += fold8(d_middle)
            c_buf[at, :] = d_middle.astype(BF16)
        yield
        if spatial:
            do_buf[...] = mm_bt(c_buf[...], projection_out[...]).astype(BF16)
        else:
            dot_buf[...] = mm_bt(projection_out[...], c_buf[...])
        weight_gradient(d_projection_out, kept.ot, c_buf, halves(width))
        yield
        yield from (window_backward(kept) if spatial else frame_backward(kept))
        yield
        total[...] = mm_bt(dqkv_buf[...], projection_in[...])
        yield
        for n, (at, f, within) in enumerate(blocks):
            if n % 2 == 0:
                weight_gradient(d_projection_in, kept.a1t, dqkv_buf, halves(COLS_AT_ONCE, n // 2 * COLS_AT_ONCE))
            d_normed = total[at, :]
            unit, rstd = standardize(kept.x[f, within].astype(F32))
            sum_ag[...] += fold8(d_normed * unit)
            sum_ab[...] += fold8(d_normed)
            dx = wide[at, :] + norm_backward(d_normed, unit, rstd, attention_gain[...])
            do_buf[at, :] = dx.astype(BF16)
        yield
        dxbuf[dx_slot] = do_buf[...].reshape(frames, window, width)
        dx_store(chunk).start()
        if not spatial:
            dx_remote(chunk).start()

    stages = []

    def emit(now, pieces):
        more = True
        while more:
            stages.append(None)

            @pl.when(now + len(stages) > 0)
            def _():
                nonlocal more
                more = next(pieces, "end") is None

    def step(t, carry):
        chunk = t - lead
        ahead = (t, kept_a, lax.rem(t, SLOTS), lax.rem(t, 2))
        behind = (chunk, lax.rem(chunk + SLOTS, SLOTS), lax.rem(chunk + 2, 2))

        @pl.when(t < count)
        def _():
            @pl.when(leading)
            def _():
                x_load(t).wait()

                @pl.when(t + 1 < count)
                def _():
                    x_load(t + 1).start()

            @pl.when(trailing)
            def _():
                y_remote(t).wait_recv()

                @pl.when(t + 1 < count)
                def _():
                    dy_load(t + 1).start()

            @pl.when(t >= 2)
            def _():
                y_store(t - 2).wait()

                @pl.when(leading)
                def _():
                    y_remote(t - 2).wait_send()

        @pl.when(leading & (t > 0) & (t <= count))
        def _():
            wait_all(park(t - 1))

        @pl.when(leading & (t == 1))
        def _():
            start_all(fetch(0))

        @pl.when(leading & (t < count))
        def _():
            emit(t, forward(True, *ahead))
            start_all(park(t))

        @pl.when(leading & (chunk >= 0))
        def _():
            wait_all(fetch(chunk))
            emit(t, backward(True, chunk, kept_b, *behind[1:]))

            @pl.when(chunk + 1 < count)
            def _():
                start_all(fetch(chunk + 1))

        @pl.when(trailing & (t < count))
        def _():
            emit(t, forward(False, *ahead))
            emit(t, backward(False, chunk, kept_a, *behind[1:]))

        return carry

    lax.fori_loop(0, count + LEAD, step, 0)

    vector[0] = jnp.zeros_like(vector[0])
    for row, partial_sum in enumerate((sum_ag, sum_ab, sum_ob, sum_fg, sum_fb, sum_db)):
        vector[0, row : row + 1, :] = jnp.sum(partial_sum[...], axis=0, keepdims=True)
    for n in range(hidden // width):
        up_sum = jnp.sum(sum_ub[:, n * width : (n + 1) * width], axis=0, keepdims=True)
        vector[0, 6 + n : 7 + n, :] = up_sum

    def block_piece(number):
        block, r = divmod(number, width // PIECE)
        at = slice(r * PIECE, (r + 1) * PIECE)
        if block < 3:
            return d_projection_in[at, block * width : (block + 1) * width].astype(BF16)
        if block < 4:
            return d_projection_out[at, :].astype(BF16)
        if block < 8:
            return d_up_weight[at, (block - 4) * width : (block - 3) * width].astype(BF16)
        start = (block - 8) * width + r * PIECE
        return d_down_weight[:, start : start + PIECE].astype(BF16).T

    for number in range(GROUP * UNIT // PIECE):
        u, r = divmod(number, UNIT // PIECE)
        at = slice(r * PIECE, (r + 1) * PIECE)
        packed[u // LINE, at, u % LINE * width : (u % LINE + 1) * width] = block_piece(number)

    for last in (count - 2, count - 1):
        y_store(last).wait()
        dx_store(last).wait()

        @pl.when(leading)
        def _():
            y_remote(last).wait_send()

        @pl.when(trailing)
        def _():
            dx_remote(last).wait_send()

    if not grouped:
        for u in range(GROUP):
            cols = slice(u % LINE * width, (u % LINE + 1) * width)
            pltpu.sync_copy(packed.at[u // LINE, :, cols], flat_ref.at[u * UNIT : (u + 1) * UNIT])
        pltpu.sync_copy(vector.at[0], vector_ref)
        return

    def landing(name, rel, place):
        col = slice(place * width, (place + 1) * width)
        if name == "core":
            return (kept_a.g if rel else kept_a.h).at[:, col]
        if name == "across":
            return kept_b.h.at[ACROSS_FIRST, col]
        if name == "across 2":
            return e_buf.at[:PIECE]
        kind, up = name
        if kind == 1:
            return (kept_b.g if up else kept_a.qkv).at[ACROSS_FIRST, col]
        if up:
            return (kept_b.g if rel else kept_b.h).at[LINE_FIRST, col]
        if rel:
            return dqkv_buf.at[:PIECE, col]
        return kept_a.qkv.at[LINE_FIRST, col]

    sum_over_group(
        packed, result, landing, vector, flat_ref, vector_ref, group_send, group_recv, group_out, ready
    )


def unpack_kernel(flat, vector, d_in, d_out, d_up, d_down, ag, ab, ob, fg, fb, d_up_bias, db):
    block = pl.program_id(0)
    width = flat.shape[1]

    @pl.when(block < 3)
    def _():
        d_in[...] = flat[...].astype(F32)

    @pl.when(block == 3)
    def _():
        d_out[...] = flat[...].astype(F32)

    @pl.when((block > 3) & (block < 8))
    def _():
        d_up[...] = flat[...].astype(F32)

    @pl.when(block > 7)
    def _():
        d_down[...] = flat[...].astype(F32)

    @pl.when(block == 0)
    def _():
        for row, out in enumerate((ag, ab, ob, fg, fb, db)):
            out[...] = vector[row : row + 1, :]
        for n in range(d_up_bias.shape[1] // width):
            d_up_bias[:, n * width : (n + 1) * width] = vector[6 + n : 7 + n, :]


def per_device(
    clip_tokens,
    window_cols,
    time_groups,
    cotangent,
    attention_gain,
    attention_bias,
    projection_in,
    projection_out,
    output_bias,
    feedforward_gain,
    feedforward_bias,
    up_weight,
    up_bias,
    down_weight,
    down_bias,
):
    micro, _, frames, band, width = clip_tokens.shape
    hidden = up_weight.shape[2]
    window = band // WCAP
    rows = frames * window
    weights = (
        attention_gain,
        attention_bias,
        projection_in[0],
        projection_out[0],
        output_bias,
        feedforward_gain,
        feedforward_bias,
        up_weight[0],
        up_bias,
        down_weight[0],
        down_bias,
    )
    smem = pl.BlockSpec(memory_space=pltpu.SMEM)
    vmem = pl.BlockSpec(memory_space=pltpu.VMEM)
    hbm = pl.BlockSpec(memory_space=pl.ANY)
    tokens = jax.ShapeDtypeStruct((micro, frames, band, width), BF16)
    chunk = (frames, window, width)
    group_size = lax.axis_size("dp")
    grouped = group_size % GROUP == 0
    flat_shape = (GROUP * UNIT, width)
    kept_shapes = Kept(
        x=(chunk, BF16),
        a1t=((width, rows), BF16),
        qkv=((rows, 3 * width), BF16),
        p=((rows, width), BF16),
        ot=((width, rows), BF16),
        xh2=((rows, width), BF16),
        a2t=((width, rows), BF16),
        rs2=((rows, 128), F32),
        h=((rows, hidden), BF16),
        g=((rows, hidden), BF16),
    )
    results = pl.pallas_call(
        partial(relay_kernel, (micro, frames, window, width, hidden, grouped)),
        out_shape=(
            tokens,
            tokens,
            jax.ShapeDtypeStruct(flat_shape, BF16),
            jax.ShapeDtypeStruct((VECTOR_ROWS, width), F32),
        )
        + tuple(jax.ShapeDtypeStruct((SLOTS,) + shape, kind) for shape, kind in kept_shapes[1:]),
        in_specs=[smem, smem, hbm, hbm] + [vmem] * len(weights),
        out_specs=[hbm] * (3 + len(kept_shapes)),
        scratch_shapes=[pltpu.VMEM(*kept) for kept in kept_shapes * 2]
        + [
            pltpu.VMEM((width, 3 * width), F32),
            pltpu.VMEM((width, width), F32),
            pltpu.VMEM((width, hidden), F32),
            pltpu.VMEM((width, hidden), F32),
            pltpu.VMEM((SLOTS,) + chunk, BF16),
            pltpu.VMEM((SLOTS,) + chunk, BF16),
            pltpu.VMEM((2,) + chunk, BF16),
            pltpu.VMEM((2,) + chunk, BF16),
            pltpu.VMEM((rows, width), BF16),
            pltpu.VMEM((frames * frames // 2, HEADS, 128), F32),
            pltpu.VMEM((frames * frames // 2, HEADS, 128), F32),
            pltpu.VMEM((rows, width), BF16),
            pltpu.VMEM((rows, width), BF16),
            pltpu.VMEM((rows, width), F32),
            pltpu.VMEM((rows, width), F32),
            pltpu.VMEM((2, rows, FF_BLOCK), F32),
            pltpu.VMEM((rows, width), BF16),
            pltpu.VMEM((width, rows), BF16),
            pltpu.VMEM((rows, width), BF16),
            pltpu.VMEM((rows, width), BF16),
            pltpu.VMEM((rows, 3 * width), BF16),
            pltpu.VMEM((3 * width, rows), F32),
            pltpu.VMEM((width, rows), F32),
            pltpu.VMEM((3 * width, rows), BF16),
            pltpu.VMEM((8, width), F32),
            pltpu.VMEM((8, width), F32),
            pltpu.VMEM((8, width), F32),
            pltpu.VMEM((8, width), F32),
            pltpu.VMEM((8, width), F32),
            pltpu.VMEM((8, hidden), F32),
            pltpu.VMEM((8, width), F32),
            pltpu.SemaphoreType.DMA((SLOTS,)),
            pltpu.SemaphoreType.DMA((SLOTS,)),
            pltpu.SemaphoreType.DMA((2,)),
            pltpu.SemaphoreType.DMA((2,)),
            pltpu.SemaphoreType.DMA((2,)),
            pltpu.SemaphoreType.DMA((2,)),
            pltpu.VMEM((LINE, UNIT, hidden), BF16),
            pltpu.VMEM((LINE, UNIT, hidden), BF16),
            pltpu.SemaphoreType.DMA((len(kept_shapes),)),
            pltpu.SemaphoreType.DMA((len(kept_shapes),)),
            pltpu.VMEM((4 + LINE, VECTOR_ROWS, width), F32),
            pltpu.SemaphoreType.DMA((FAMILIES * LINE,)),
            pltpu.SemaphoreType.DMA((FAMILIES * LINE,)),
            pltpu.SemaphoreType.DMA((2 * GROUP + 1,)),
            pltpu.SemaphoreType.REGULAR((4,)),
        ],
        compiler_params=pltpu.CompilerParams(
            collective_id=0, has_side_effects=True, vmem_limit_bytes=63 * 1024 * 1024
        ),
        name="relay",
    )(
        window_cols,
        time_groups,
        clip_tokens.reshape(micro, frames, band, width),
        cotangent.reshape(micro, frames, band, width),
        *weights,
    )
    activations, input_grads, flat, vector = results[:4]
    if group_size != GROUP:
        groups = None
        if grouped:
            groups = [[first + n for first in range(0, group_size, GROUP)] for n in range(GROUP)]
        flat, vector = lax.psum((flat, vector), "dp", axis_index_groups=groups)
    square = (width, width)
    row = jax.ShapeDtypeStruct((1, width), F32)
    whole_row = pl.BlockSpec((1, width), lambda i: (0, 0))
    wide_row = pl.BlockSpec((1, hidden), lambda i: (0, 0))
    d_in, d_out, d_up, d_down, ag, ab, ob, fg, fb, d_up_bias, db = pl.pallas_call(
        unpack_kernel,
        grid=(GROUP * UNIT // width,),
        in_specs=[
            pl.BlockSpec(square, lambda i: (i, 0)),
            pl.BlockSpec((VECTOR_ROWS, width), lambda i: (0, 0)),
        ],
        out_specs=[
            pl.BlockSpec(square, lambda i: (0, jnp.minimum(i, 2))),
            pl.BlockSpec(square, lambda i: (0, 0)),
            pl.BlockSpec(square, lambda i: (0, jnp.clip(i - 4, 0, 3))),
            pl.BlockSpec(square, lambda i: (jnp.clip(i - 8, 0, 3), 0)),
        ]
        + [whole_row] * 5
        + [wide_row, whole_row],
        out_shape=[
            jax.ShapeDtypeStruct((width, 3 * width), F32),
            jax.ShapeDtypeStruct(square, F32),
            jax.ShapeDtypeStruct((width, hidden), F32),
            jax.ShapeDtypeStruct((hidden, width), F32),
        ]
        + [row] * 5
        + [jax.ShapeDtypeStruct((1, hidden), F32), row],
        name="unpack",
    )(flat, vector)
    shape_out = (1, micro, 1, frames, band, width)
    return (
        activations.reshape(shape_out),
        input_grads.reshape(shape_out),
        ag,
        ab,
        d_in[None],
        d_out[None],
        ob,
        fg,
        fb,
        d_up[None],
        d_up_bias,
        d_down[None],
        db,
    )


def solution(mesh):
    wide, deep = P("section", None), P("section", None, None)
    tokens = P(None, "dp", None, None, None)
    weights = (wide, wide, deep, deep, wide, wide, wide, deep, wide, deep, wide)
    outputs = P("section", None, "dp", None, None, None)
    return jax.shard_map(
        per_device,
        mesh=mesh,
        in_specs=(tokens, P(None, "dp"), P(None, "dp", None), tokens) + weights,
        out_specs=(outputs, outputs) + weights,
        check_vma=False,
    )
```

```python
from collections import namedtuple
from functools import partial

import jax
import jax.numpy as jnp
from jax import lax
from jax.experimental import pallas as pl
from jax.experimental.pallas import tpu as pltpu
from jax.sharding import PartitionSpec as P

HEADS = 8
WCAP = 5
EPSILON = 1e-05
MASKED = -1e30
MESH = pl.DeviceIdType.MESH

F32 = jnp.float32
BF16 = jnp.bfloat16

LEAD = 4
SLOTS = LEAD + 1
Kept = namedtuple("Kept", ("x", "a1t", "qkv", "p", "ot", "xh2", "a2t", "rs2", "h", "g"))
FF_BLOCK = 512
ROWS_AT_ONCE = 32
COLS_AT_ONCE = 256

INV_SQRT2 = 0.7071067811865476
PDF = 0.3989422804014327
LOG2E = 1.4426950408889634


def mm(a, b):
    return lax.dot_general(a, b, (((1,), (0,)), ((), ())), preferred_element_type=F32)


def mm_bt(a, b):
    return lax.dot_general(a, b, (((1,), (1,)), ((), ())), preferred_element_type=F32)


def mm_at(a, b):
    return lax.dot_general(a, b, (((0,), (0,)), ((), ())), preferred_element_type=F32)


def gelu_and_slope(u):
    cdf = 0.5 + 0.5 * lax.erf(INV_SQRT2 * u)
    bell = jnp.exp2((-0.5 * LOG2E) * (u * u))
    return u * cdf, cdf + (PDF * u) * bell


def fold8(values):
    rows, cols = values.shape
    return jnp.sum(values.reshape(rows // 8, 8, cols), axis=0)


GROUP = 16
LINE = 4
LINE_ORDER = (3, 0, 2, 1)
UNIT = 384
PIECE = 128
WHOLE = slice(0, UNIT)
ACROSS_FIRST = slice(0, 256)
LINE_FIRST = slice(256, UNIT)
PART = {1: ACROSS_FIRST, 2: LINE_FIRST}
SIDES = {1: (0,), 2: (0, 1)}
FAMILIES = 32
VECTOR_ROWS = 16


def group_place():
    me = lax.axis_index("dp")
    core, across, line = lax.rem(me, 2), lax.rem(lax.div(me, 2), 2), lax.rem(lax.div(me, 4), LINE)
    sibling, beside = {"dp": me + 1 - 2 * core}, {"dp": me + 2 - 4 * across}
    return core, across, line, sibling, beside, {"dp": me + 4}, {"dp": me - 4}


def sum_over_group(packed, result, landing, vector, flat_ref, vector_ref, send_sem, recv_sem, out_sem, ready):
    core, across, line, sibling, beside, above, below = group_place()
    sides = (across, 1 - across)
    families = {}
    pending = []

    def when(condition, action):
        if condition is None:
            action()
        else:
            pl.when(condition)(action)

    def remote(family, place, source, target, device):
        number = families.setdefault(family, len(families)) * LINE + place
        return pltpu.make_async_remote_copy(
            src_ref=source,
            dst_ref=target,
            send_sem=send_sem.at[number],
            recv_sem=recv_sem.at[number],
            device_id=device,
            device_id_type=MESH,
        )

    def start(family, place, source, target, device):
        remote(family, place, source, target, device).start()

    def sent(family, place, source, device, condition=None):
        pending.append((condition, lambda: remote(family, place, source, source, device).wait_send()))

    def received(family, place, target, device):
        remote(family, place, target, target, device).wait_recv()

    def unit(ref, half, side, place, part):
        column = place * 512 if isinstance(place, int) else pl.multiple_of(place * 512, 512)
        return ref.at[half * 2 + side, part, pl.ds(column, 512)]

    def add(target, arrived):
        for r in range(0, target.shape[0], 64):
            at = slice(r, r + 64)
            target[at] = (target[at].astype(F32) + arrived[at].astype(F32)).astype(BF16)

    def store(far, rel, place, kind):
        half, side, part = (1 - core if far else core), sides[rel], PART[kind]
        row = pl.multiple_of(((half * 2 + side) * LINE + place) * UNIT + part.start, PIECE)
        return pltpu.make_async_copy(
            unit(result, half, side, place, part),
            flat_ref.at[pl.ds(row, part.stop - part.start)],
            out_sem.at[((far * 2 + rel) * 2 + kind - 1) * LINE + place],
        )

    for number, (device, condition) in enumerate(
        ((sibling, None), (beside, None), (below, line > 0), (above, line < LINE - 1))
    ):
        there = number if number < 2 else 5 - number
        when(
            condition,
            partial(pl.semaphore_signal, ready.at[there], inc=1, device_id=device, device_id_type=MESH),
        )
    pl.semaphore_wait(ready.at[0], 1)

    start("vector core", 0, vector.at[0], vector.at[1], sibling)
    sent("vector core", 0, vector.at[0], sibling)
    for place in LINE_ORDER:
        for side in range(2):
            source = unit(packed, 1 - core, side, place, WHOLE)
            start(("core", side), place, source, landing("core", side, place), sibling)
            sent(("core", side), place, source, sibling)
    pl.semaphore_wait(ready.at[1], 1)
    pl.when(line > 0)(lambda: pl.semaphore_wait(ready.at[2], 1))
    pl.when(line < LINE - 1)(lambda: pl.semaphore_wait(ready.at[3], 1))

    def line_send(kind, place, up, condition):
        device = above if up else below

        def go():
            for rel in SIDES[kind]:
                source = unit(packed, core, sides[rel], place, PART[kind])
                start((kind, up, rel), place, source, landing((kind, up), rel, place), device)

        pl.when(condition)(go)
        for rel in SIDES[kind]:
            sent((kind, up, rel), place, unit(packed, core, sides[rel], place, PART[kind]), device, condition)

    def line_take(kind, place, up, condition):
        def go():
            for rel in SIDES[kind]:
                spot = landing((kind, up), rel, place)
                received((kind, up, rel), place, spot, below if up else above)
                add(unit(packed, core, sides[rel], place, PART[kind]), spot)

        pl.when(condition)(go)

    def from_ends(kind, place):
        if place > 0:
            line_send(kind, place, True, line == 0)
        if place < LINE - 1:
            line_send(kind, place, False, line == LINE - 1)

    def inner_step(kind, k):
        place = LINE - 1 - k
        line_take(kind, place, True, (line > 0) & (line <= place))
        if place > 1:
            line_send(kind, place, True, (line > 0) & (line < place))
        place = k
        line_take(kind, place, False, (line < LINE - 1) & (line >= place))
        if place < LINE - 2:
            line_send(kind, place, False, (line < LINE - 1) & (line > place))

    def take_across(place):
        spot = landing("across", 0, place)
        received("across", place, spot, beside)
        add(unit(packed, core, sides[0], place, ACROSS_FIRST), spot)
        from_ends(1, place)

    for place in LINE_ORDER:
        for side in range(2):
            spot = landing("core", side, place)
            received(("core", side), place, spot, sibling)
            add(unit(packed, core, side, place, WHOLE), spot)
        source = unit(packed, core, sides[1], place, ACROSS_FIRST)
        start("across", place, source, landing("across", 0, place), beside)
        sent("across", place, source, beside)
        from_ends(2, place)
    received("vector core", 0, vector.at[1], sibling)
    vector[2] = vector[0] + vector[1]
    start("vector across", 0, vector.at[2], vector.at[3], beside)
    sent("vector across", 0, vector.at[2], beside)
    for k in range(LINE - 1):
        take_across(LINE_ORDER[k])
        inner_step(2, k)
    take_across(LINE_ORDER[LINE - 1])
    source = unit(packed, core, sides[1], line, LINE_FIRST)
    start("across 2", 0, source, landing("across 2", 0, 0), beside)
    sent("across 2", 0, source, beside)
    received("vector across", 0, vector.at[3], beside)
    vector[4 + line] = vector[2] + vector[3]
    inner_step(1, 0)
    inner_step(1, 1)
    spot = landing("across 2", 0, 0)
    received("across 2", 0, spot, beside)
    own = unit(packed, core, sides[0], line, LINE_FIRST)
    add(own, spot)
    own_two = unit(result, core, sides[0], line, LINE_FIRST)
    own_two[...] = own[...]
    start("gather across 2", 0, own_two, own_two, beside)
    sent("gather across 2", 0, own_two, beside)
    inner_step(1, 2)
    own_one = unit(result, core, sides[0], line, ACROSS_FIRST)
    own_one[...] = unit(packed, core, sides[0], line, ACROSS_FIRST)[...]

    def spread(family, place, spot, up, down):
        if up is not None:
            pl.when(up)(lambda: start((family, True), place, spot, spot, above))
        if down is not None:
            pl.when(down)(lambda: start((family, False), place, spot, spot, below))

    def hand_over(kind, rel, place):
        spot = unit(result, core, sides[rel], place, PART[kind])
        start(("gather core", kind, rel), place, spot, spot, sibling)
        store(0, rel, place, kind).start()

    def have(kind, rel, place, up, down):
        spot = unit(result, core, sides[rel], place, PART[kind])
        spread(("spread", kind, rel), place, spot, up, down)
        if kind == 1:
            start("gather across", place, spot, spot, beside)
        hand_over(kind, rel, place)

    def come(distance, action):
        pl.when(line >= distance)(lambda: action(line - distance, True))
        pl.when(line + distance < LINE)(lambda: action(line + distance, False))

    def arrive(kind, rel, distance):
        def action(place, up):
            spot = unit(result, core, sides[rel], place, PART[kind])
            received((("spread", kind, rel), up), place, spot, below if up else above)
            have(kind, rel, place, line < LINE - 1 if up else None, None if up else line > 0)

        come(distance, action)

    def arrive_vector(distance):
        def action(place, up):
            spot = vector.at[4 + place]
            received(("vector", up), place, spot, below if up else above)
            spread("vector", place, spot, line < LINE - 1 if up else None, None if up else line > 0)

        come(distance, action)

    def arrive_across(distance):
        def action(place, up):
            received("gather across", place, unit(result, core, sides[1], place, ACROSS_FIRST), beside)
            hand_over(1, 1, place)

        if distance == 0:
            action(line, True)
        else:
            come(distance, action)

    have(1, 0, line, line < LINE - 1, line > 0)
    have(2, 0, line, line < LINE - 1, line > 0)
    spread("vector", line, vector.at[4 + line], line < LINE - 1, line > 0)
    received("gather across 2", 0, unit(result, core, sides[1], line, LINE_FIRST), beside)
    have(2, 1, line, line < LINE - 1, line > 0)
    for distance in range(1, LINE):
        arrive(1, 0, distance)
        arrive(2, 0, distance)
        arrive(2, 1, distance)
        arrive_vector(distance)
        arrive_across(distance - 1)
    arrive_across(LINE - 1)
    vector[1] = (vector[4] + vector[5]) + (vector[6] + vector[7])
    vector_out = pltpu.make_async_copy(vector.at[1], vector_ref, out_sem.at[2 * GROUP])
    vector_out.start()
    for place in range(LINE):
        for kind in (1, 2):
            for rel in range(2):
                spot = unit(result, 1 - core, sides[rel], place, PART[kind])
                received(("gather core", kind, rel), place, spot, sibling)
                store(1, rel, place, kind).start()
    vector_out.wait()

    for place in range(LINE):
        for kind in (1, 2):
            for rel in range(2):
                spot = unit(result, core, sides[rel], place, PART[kind])
                sent(("gather core", kind, rel), place, spot, sibling)
                store(0, rel, place, kind).wait()
                store(1, rel, place, kind).wait()
            for rel in SIDES[kind]:
                spot = unit(result, core, sides[rel], place, PART[kind])
                sent((("spread", kind, rel), True), place, spot, above, (line >= place) & (line < LINE - 1))
                sent((("spread", kind, rel), False), place, spot, below, (line <= place) & (line > 0))
        sent("gather across", place, unit(result, core, sides[0], place, ACROSS_FIRST), beside)
        sent(("vector", True), place, vector.at[4 + place], above, (line >= place) & (line < LINE - 1))
        sent(("vector", False), place, vector.at[4 + place], below, (line <= place) & (line > 0))
    for condition, wait in pending:
        when(condition, wait)


def relay_kernel(
    dims,
    cols_ref,
    groups_ref,
    clip_ref,
    cot_ref,
    attention_gain,
    attention_bias,
    projection_in,
    projection_out,
    output_bias,
    feedforward_gain,
    feedforward_bias,
    up_weight,
    up_bias,
    down_weight,
    down_bias,
    act_ref,
    grad_ref,
    flat_ref,
    vector_ref,
    *scratch,
):
    micro, frames, window, width, hidden, grouped = dims
    parked, scratch = scratch[: len(Kept._fields) - 1], scratch[len(Kept._fields) - 1 :]
    kept_a, scratch = Kept(*scratch[: len(Kept._fields)]), scratch[len(Kept._fields) :]
    kept_b, scratch = Kept(*scratch[: len(Kept._fields)]), scratch[len(Kept._fields) :]
    (
    d_projection_in,
    d_projection_out,
    d_up_weight,
    d_down_weight,
    xbuf,
    dybuf,
    ybuf,
    dxbuf,
    a1_buf,
    pf_buf,
    ds_buf,
    o_buf,
    a2_buf,
    wide,
    total,
    u_buf,
    e_buf,
    et_buf,
    c_buf,
    do_buf,
    dqkv_buf,
    qkvt_buf,
    dot_buf,
    dqkvt_buf,
    sum_ag,
    sum_ab,
    sum_ob,
    sum_fg,
    sum_fb,
    sum_ub,
    sum_db,
    x_sem,
    dy_sem,
    y_sem,
    y_send,
    dx_sem,
    dx_send,
    packed,
    result,
    park_sem,
    fetch_sem,
    vector,
    group_send,
    group_recv,
    group_out,
    ready,
    ) = scratch
    rows = frames * window
    count = micro * WCAP
    head = width // HEADS
    pair = 2 * head
    scale = head ** (-0.5)
    section = lax.axis_index("section")
    leading = section == 0
    trailing = section != 0
    lead = LEAD * (1 - section)
    partner = {"section": 1 - section}

    def hbm_chunk(ref, chunk):
        start = pl.multiple_of(lax.rem(chunk, WCAP) * window, window)
        return ref.at[lax.div(chunk, WCAP), :, pl.ds(start, window), :]

    def x_load(chunk):
        slot = lax.rem(chunk, SLOTS)
        return pltpu.make_async_copy(hbm_chunk(clip_ref, chunk), xbuf.at[slot], x_sem.at[slot])

    def dy_load(chunk):
        slot = lax.rem(chunk, SLOTS)
        return pltpu.make_async_copy(hbm_chunk(cot_ref, chunk), dybuf.at[slot], dy_sem.at[slot])

    def y_store(chunk):
        slot = lax.rem(chunk, 2)
        return pltpu.make_async_copy(ybuf.at[slot], hbm_chunk(act_ref, chunk), y_sem.at[slot])

    def dx_store(chunk):
        slot = lax.rem(chunk, 2)
        return pltpu.make_async_copy(dxbuf.at[slot], hbm_chunk(grad_ref, chunk), dx_sem.at[slot])

    def park(chunk):
        slot = lax.rem(chunk, SLOTS)
        return [
            pltpu.make_async_copy(here, there.at[slot], park_sem.at[n])
            for n, (here, there) in enumerate(zip(kept_a[1:], parked))
        ]

    def fetch(chunk):
        slot = lax.rem(chunk, SLOTS)
        return [pltpu.make_async_copy(hbm_chunk(clip_ref, chunk), kept_b.x, fetch_sem.at[0])] + [
            pltpu.make_async_copy(there.at[slot], here, fetch_sem.at[n + 1])
            for n, (here, there) in enumerate(zip(kept_b[1:], parked))
        ]

    def start_all(copies):
        for copy in copies:
            copy.start()

    def wait_all(copies):
        for copy in copies:
            copy.wait()

    def y_remote(chunk):
        slot, there = lax.rem(chunk, 2), lax.rem(chunk, SLOTS)
        return pltpu.make_async_remote_copy(
            src_ref=ybuf.at[slot],
            dst_ref=xbuf.at[there],
            send_sem=y_send.at[slot],
            recv_sem=x_sem.at[there],
            device_id=partner,
            device_id_type=MESH,
        )

    def dx_remote(chunk):
        slot, there = lax.rem(chunk, 2), lax.rem(chunk, SLOTS)
        return pltpu.make_async_remote_copy(
            src_ref=dxbuf.at[slot],
            dst_ref=dybuf.at[there],
            send_sem=dx_send.at[slot],
            recv_sem=dy_sem.at[there],
            device_id=partner,
            device_id_type=MESH,
        )

    barrier = pltpu.get_barrier_semaphore()
    greeted = 1
    pl.semaphore_signal(barrier, inc=1, device_id=partner, device_id_type=MESH)
    if grouped:
        _, _, line, sibling, beside, above, below = group_place()
        has_below, has_above = line > 0, line < LINE - 1
        for device, condition in ((sibling, None), (beside, None), (below, has_below), (above, has_above)):
            greet = partial(pl.semaphore_signal, barrier, inc=1, device_id=device, device_id_type=MESH)
            if condition is None:
                greet()
            else:
                pl.when(condition)(greet)
        greeted = 3 + has_below.astype(jnp.int32) + has_above.astype(jnp.int32)

    @pl.when(leading)
    def _():
        x_load(0).start()

    @pl.when(trailing)
    def _():
        dy_load(0).start()

    for total_ref in (d_projection_in, d_projection_out, d_up_weight, d_down_weight):
        total_ref[...] = jnp.zeros_like(total_ref)
    for total_ref in (sum_ag, sum_ab, sum_ob, sum_fg, sum_fb, sum_ub, sum_db):
        total_ref[...] = jnp.zeros_like(total_ref)

    pl.semaphore_wait(barrier, greeted)

    def frame_rows(i):
        return slice(i * window, (i + 1) * window)

    half = lax.broadcasted_iota(jnp.int32, (window, pair), 1) < head
    low_half = jnp.where(half, 1.0, 0.0).astype(BF16)
    high_half = jnp.where(half, 0.0, 1.0).astype(BF16)

    def by_head(values):
        return jnp.concatenate([values * low_half, values * high_half], axis=0)

    def join_heads(values):
        return jnp.where(half, values[:window], values[window:])

    heads_of = [
        (frame_rows(f), slice(n * pair, (n + 1) * pair), n) for f in range(frames) for n in range(width // pair)
    ]

    def of_pair(ref, at, which, n):
        return ref[at, which * width + n * pair : which * width + (n + 1) * pair]

    def window_forward(kept):
        for at, lanes, n in heads_of:
            keys = of_pair(kept.qkv, at, 1, n)
            total[at, lanes] = mm_bt(keys, by_head(of_pair(kept.qkv, at, 0, n)))
        yield
        for at, lanes, n in heads_of:
            scores = total[at, lanes] * scale
            scores = jnp.exp(scores - jnp.max(scores, axis=0, keepdims=True))
            probs = scores * (1.0 / jnp.sum(scores, axis=0, keepdims=True))
            kept.p[at, lanes] = probs.astype(BF16)
        yield
        for at, lanes, n in heads_of:
            values = of_pair(kept.qkv, at, 2, n)
            o_buf[at, lanes] = join_heads(mm_at(kept.p[at, lanes], values)).astype(BF16)

    def window_backward(kept):
        for at, lanes, n in heads_of:
            up = by_head(do_buf[at, lanes])
            total[at, lanes] = mm_bt(of_pair(kept.qkv, at, 2, n), up)
            dv = mm(kept.p[at, lanes], up)
            dqkv_buf[at, 2 * width + n * pair : 2 * width + (n + 1) * pair] = dv.astype(BF16)
        yield
        for at, lanes, n in heads_of:
            probs = kept.p[at, lanes].astype(F32)
            dp = total[at, lanes]
            ds = probs * (dp - jnp.sum(probs * dp, axis=0, keepdims=True))
            e_buf[at, lanes] = ds.astype(BF16)
        yield
        for at, lanes, n in heads_of:
            ds = e_buf[at, lanes]
            dk = mm(ds, by_head(of_pair(kept.qkv, at, 0, n))) * scale
            dqkv_buf[at, width + n * pair : width + (n + 1) * pair] = dk.astype(BF16)
            dq = join_heads(mm_at(ds, of_pair(kept.qkv, at, 1, n))) * scale
            dqkv_buf[at, lanes] = dq.astype(BF16)

    low_frame = lax.broadcasted_iota(jnp.int32, (1, 128), 1) < window

    def lane_tiles(i):
        return min(i + 1, frames - 1) // 2 + 1

    def tile(t):
        return slice(t * 128, (t + 1) * 128)

    def head_rows(which, h):
        return slice(which * width + h * head, which * width + (h + 1) * head)

    def other_half(values):
        return pltpu.roll(values, window, axis=1)

    def both_frames(ref, at, t):
        values = ref[at, tile(t)]
        turned = other_half(values)
        return jnp.where(low_frame, values, turned), jnp.where(low_frame, turned, values)

    def frame_forward(chunk, kept):
        tile_count = frames // 2
        for n in range(3):
            flat = kept.qkv[:, n * width : (n + 1) * width].T
            qkvt_buf[n * width : (n + 1) * width, :] = flat.astype(F32)
        for h in range(HEADS):
            keys = [qkvt_buf[head_rows(1, h), tile(t)] for t in range(tile_count)]
            for pair_index in range(tile_count):
                queries = both_frames(qkvt_buf, head_rows(0, h), pair_index)
                for i in (2 * pair_index, 2 * pair_index + 1):
                    for t in range(lane_tiles(i)):
                        score = jnp.sum(queries[i % 2] * keys[t], axis=0, keepdims=True)
                        ds_buf[i * tile_count + t, h : h + 1, :] = score
        yield
        item = lax.div(chunk, WCAP)
        labels = [
            jnp.where(low_frame, groups_ref[item, 0, 2 * t], groups_ref[item, 0, 2 * t + 1])
            for t in range(tile_count)
        ]
        for i in range(frames):
            mine = groups_ref[item, 0, i]
            parts = [
                jnp.where(labels[t] <= mine, ds_buf[i * tile_count + t] * scale, MASKED)
                for t in range(lane_tiles(i))
            ]
            largest = parts[0]
            for part in parts[1:]:
                largest = jnp.maximum(largest, part)
            largest = jnp.maximum(largest, other_half(largest))
            parts = [jnp.exp(part - largest) for part in parts]
            whole = parts[0]
            for part in parts[1:]:
                whole = whole + part
            whole = 1.0 / (whole + other_half(whole))
            for t, part in enumerate(parts):
                pf_buf[i * tile_count + t] = part * whole
        yield
        for h in range(HEADS):
            values = [qkvt_buf[head_rows(2, h), tile(t)] for t in range(tile_count)]
            for pair_index in range(tile_count):
                mixed = []
                for i in (2 * pair_index, 2 * pair_index + 1):
                    part = 0.0
                    for t in range(lane_tiles(i)):
                        part = part + pf_buf[i * tile_count + t, h : h + 1, :] * values[t]
                    mixed.append(part + other_half(part))
                both = jnp.where(low_frame, mixed[0], mixed[1])
                kept.ot[head_rows(0, h), tile(pair_index)] = both.astype(BF16)

    def frame_backward(kept, beside):
        tile_count = frames // 2
        for h in range(HEADS):
            beside()
            values = [qkvt_buf[head_rows(2, h), tile(t)] for t in range(tile_count)]
            dv = [0.0] * tile_count
            for pair_index in range(tile_count):
                ups = both_frames(dot_buf, head_rows(0, h), pair_index)
                for i in (2 * pair_index, 2 * pair_index + 1):
                    for t in range(lane_tiles(i)):
                        ds_buf[i * tile_count + t, h : h + 1, :] = jnp.sum(
                            ups[i % 2] * values[t], axis=0, keepdims=True
                        )
                        dv[t] = dv[t] + pf_buf[i * tile_count + t, h : h + 1, :] * ups[i % 2]
            for t in range(tile_count):
                dqkvt_buf[head_rows(2, h), tile(t)] = dv[t].astype(BF16)
        for i in range(frames):
            spots = [i * tile_count + t for t in range(lane_tiles(i))]
            along = pf_buf[spots[0]] * ds_buf[spots[0]]
            for spot in spots[1:]:
                along = along + pf_buf[spot] * ds_buf[spot]
            along = along + other_half(along)
            for spot in spots:
                ds_buf[spot] = pf_buf[spot] * (ds_buf[spot] - along) * scale
        for h in range(HEADS):
            beside()
            keys = [qkvt_buf[head_rows(1, h), tile(t)] for t in range(tile_count)]
            dk = [0.0] * tile_count
            for pair_index in range(tile_count):
                queries = both_frames(qkvt_buf, head_rows(0, h), pair_index)
                dq = []
                for i in (2 * pair_index, 2 * pair_index + 1):
                    part = 0.0
                    for t in range(lane_tiles(i)):
                        ds = ds_buf[i * tile_count + t, h : h + 1, :]
                        part = part + ds * keys[t]
                        dk[t] = dk[t] + ds * queries[i % 2]
                    dq.append(part + other_half(part))
                both = jnp.where(low_frame, dq[0], dq[1])
                dqkvt_buf[head_rows(0, h), tile(pair_index)] = both.astype(BF16)
            for t in range(tile_count):
                dqkvt_buf[head_rows(1, h), tile(t)] = dk[t].astype(BF16)
        for n in range(3):
            dqkv_buf[:, n * width : (n + 1) * width] = dqkvt_buf[n * width : (n + 1) * width, :].T

    def live_of(chunk):
        cols = cols_ref[lax.div(chunk, WCAP), 0]
        return jnp.where(lax.rem(chunk, WCAP) < cols, 1.0, 0.0).astype(F32)

    def standardize(values):
        centered = values - jnp.mean(values, axis=-1, keepdims=True)
        rstd = lax.rsqrt(jnp.mean(centered * centered, axis=-1, keepdims=True) + EPSILON)
        return centered * rstd, rstd

    blocks = [
        (slice(r, r + ROWS_AT_ONCE), r // window, slice(r % window, r % window + ROWS_AT_ONCE))
        for r in range(0, rows, ROWS_AT_ONCE)
    ]
    ff_parts = [slice(c, c + FF_BLOCK) for c in range(0, hidden, FF_BLOCK)]

    def halves(cols, start=0, step=COLS_AT_ONCE):
        return [slice(c, c + step) for c in range(start, start + cols, step)]

    def forward(spatial, chunk, kept, slot, y_slot):
        kept.x[...] = xbuf[slot]
        for at, f, within in blocks:
            unit, _ = standardize(kept.x[f, within].astype(F32))
            a1_buf[at, :] = (unit * attention_gain[...] + attention_bias[...]).astype(BF16)
        yield
        kept.a1t[...] = a1_buf[...].T
        for part in halves(3 * width, step=width):
            kept.qkv[:, part] = mm(a1_buf[...], projection_in[:, part]).astype(BF16)
        yield
        if spatial:
            yield from window_forward(kept)
            yield
            kept.ot[...] = o_buf[...].T
        else:
            yield from frame_forward(chunk, kept)
            yield
            o_buf[...] = kept.ot[...].T
        wide[...] = mm(o_buf[...], projection_out[...])
        yield
        for at, f, within in blocks:
            middle = kept.x[f, within].astype(F32) + (wide[at, :] + output_bias[...])
            wide[at, :] = middle + down_bias[...]
            unit, rstd = standardize(middle)
            kept.xh2[at, :] = unit.astype(BF16)
            kept.rs2[at, :] = jnp.broadcast_to(rstd, (ROWS_AT_ONCE, 128))
            a2_buf[at, :] = (unit * feedforward_gain[...] + feedforward_bias[...]).astype(BF16)
        yield
        kept.a2t[...] = a2_buf[...].T
        u_buf[0] = mm(a2_buf[...], up_weight[:, ff_parts[0]])
        yield
        for n, part in enumerate(ff_parts):
            if n + 1 < len(ff_parts):
                u_buf[(n + 1) % 2] = mm(a2_buf[...], up_weight[:, ff_parts[n + 1]])
            for at, _, _ in blocks:
                for inner, outer in zip(halves(FF_BLOCK), halves(FF_BLOCK, part.start)):
                    h, slope = gelu_and_slope(u_buf[n % 2, at, inner] + up_bias[:, outer])
                    kept.h[at, outer] = h.astype(BF16)
                    kept.g[at, outer] = slope.astype(BF16)
            yield
        total[...] = mm(kept.h[...], down_weight[...])
        yield
        live = live_of(chunk)
        for at, f, within in blocks:
            ybuf[y_slot, f, within] = ((wide[at, :] + total[at, :]) * live).astype(BF16)
        y_store(chunk).start()
        if spatial:
            y_remote(chunk).start()

    def norm_backward(d_normed, unit, rstd, gain):
        d_unit = d_normed * gain
        along = jnp.mean(d_unit * unit, axis=-1, keepdims=True)
        return rstd * (d_unit - jnp.mean(d_unit, axis=-1, keepdims=True) - unit * along)

    def weight_gradient(total_ref, left, right, cols):
        for part in cols:
            total_ref[:, part] += mm(left[...], right[:, part])

    def backward(spatial, chunk, kept, slot, dx_slot):
        if spatial:
            dx_remote(chunk).wait_recv()
        else:
            dy_load(chunk).wait()

        @pl.when(chunk >= 2)
        def _():
            dx_store(chunk - 2).wait()
            if not spatial:
                dx_remote(chunk - 2).wait_send()

        live = live_of(chunk)
        e_buf[...] = (dybuf[slot].reshape(rows, width).astype(F32) * live).astype(BF16)
        for at, f, within in blocks:
            sum_db[...] += fold8(e_buf[at, :].astype(F32))
        yield
        et_buf[...] = e_buf[...].T
        u_buf[0] = mm_bt(e_buf[...], down_weight[ff_parts[0], :])
        yield
        for n, part in enumerate(ff_parts):
            if n + 1 < len(ff_parts):
                u_buf[(n + 1) % 2] = mm_bt(e_buf[...], down_weight[ff_parts[n + 1], :])
            if spatial:
                weight_gradient(d_down_weight, et_buf, kept.h, halves(FF_BLOCK, part.start))
            for at, _, _ in blocks:
                for inner, outer in zip(halves(FF_BLOCK), halves(FF_BLOCK, part.start)):
                    du = u_buf[n % 2, at, inner] * kept.g[at, outer].astype(F32)
                    sum_ub[:, outer] += fold8(du)
                    kept.g[at, outer] = du.astype(BF16)
            yield
        total[...] = mm_bt(kept.g[...], up_weight[...])
        yield
        for n, (at, _, _) in enumerate(blocks):
            if n % 3 == 0:
                grown = (d_up_weight, kept.a2t, kept.g) if spatial else (d_down_weight, et_buf, kept.h)
                weight_gradient(*grown, halves(FF_BLOCK, n // 3 * FF_BLOCK))
            d_normed = total[at, :]
            unit = kept.xh2[at, :].astype(F32)
            sum_fg[...] += fold8(d_normed * unit)
            sum_fb[...] += fold8(d_normed)
            rstd = kept.rs2[at, 0:1]
            d_middle = e_buf[at, :].astype(F32) + norm_backward(d_normed, unit, rstd, feedforward_gain[...])
            wide[at, :] = d_middle
            sum_ob[...] += fold8(d_middle)
            c_buf[at, :] = d_middle.astype(BF16)
        yield
        if spatial:
            do_buf[...] = mm_bt(c_buf[...], projection_out[...]).astype(BF16)
        else:
            dot_buf[...] = mm_bt(projection_out[...], c_buf[...])
        if spatial:
            weight_gradient(d_projection_out, kept.ot, c_buf, halves(width))
            yield from window_backward(kept)
        else:
            waiting = [(d_up_weight, kept.a2t, kept.g, [part]) for part in halves(hidden)]
            waiting += [(d_projection_out, kept.ot, c_buf, [part]) for part in halves(width)]

            def beside():
                if waiting:
                    weight_gradient(*waiting.pop(0))

            frame_backward(kept, beside)
        total[...] = mm_bt(dqkv_buf[...], projection_in[...])
        yield
        for n, (at, f, within) in enumerate(blocks):
            if n % 2 == 0:
                weight_gradient(d_projection_in, kept.a1t, dqkv_buf, halves(COLS_AT_ONCE, n // 2 * COLS_AT_ONCE))
            d_normed = total[at, :]
            unit, rstd = standardize(kept.x[f, within].astype(F32))
            sum_ag[...] += fold8(d_normed * unit)
            sum_ab[...] += fold8(d_normed)
            dx = wide[at, :] + norm_backward(d_normed, unit, rstd, attention_gain[...])
            do_buf[at, :] = dx.astype(BF16)
        yield
        dxbuf[dx_slot] = do_buf[...].reshape(frames, window, width)
        dx_store(chunk).start()
        if not spatial:
            dx_remote(chunk).start()

    def emit(pieces):
        for _ in pieces:
            pass

    def step(t, carry):
        chunk = t - lead
        ahead = (t, kept_a, lax.rem(t, SLOTS), lax.rem(t, 2))
        behind = (chunk, lax.rem(chunk + SLOTS, SLOTS), lax.rem(chunk + 2, 2))

        @pl.when(t < count)
        def _():
            @pl.when(leading)
            def _():
                x_load(t).wait()

                @pl.when(t + 1 < count)
                def _():
                    x_load(t + 1).start()

            @pl.when(trailing)
            def _():
                y_remote(t).wait_recv()

                @pl.when(t + 1 < count)
                def _():
                    dy_load(t + 1).start()

            @pl.when(t >= 2)
            def _():
                y_store(t - 2).wait()

                @pl.when(leading)
                def _():
                    y_remote(t - 2).wait_send()

        @pl.when(leading & (t > 0) & (t <= count))
        def _():
            wait_all(park(t - 1))

        @pl.when(leading & (t == 1))
        def _():
            start_all(fetch(0))

        @pl.when(leading & (t < count))
        def _():
            emit(forward(True, *ahead))
            start_all(park(t))

        @pl.when(leading & (chunk >= 0))
        def _():
            wait_all(fetch(chunk))
            emit(backward(True, chunk, kept_b, *behind[1:]))

            @pl.when(chunk + 1 < count)
            def _():
                start_all(fetch(chunk + 1))

        @pl.when(trailing & (t < count))
        def _():
            emit(forward(False, *ahead))
            emit(backward(False, chunk, kept_a, *behind[1:]))

        return carry

    lax.fori_loop(0, count + LEAD, step, 0)

    vector[0] = jnp.zeros_like(vector[0])
    for row, partial_sum in enumerate((sum_ag, sum_ab, sum_ob, sum_fg, sum_fb, sum_db)):
        vector[0, row : row + 1, :] = jnp.sum(partial_sum[...], axis=0, keepdims=True)
    for n in range(hidden // width):
        up_sum = jnp.sum(sum_ub[:, n * width : (n + 1) * width], axis=0, keepdims=True)
        vector[0, 6 + n : 7 + n, :] = up_sum

    def block_piece(number):
        block, r = divmod(number, width // PIECE)
        at = slice(r * PIECE, (r + 1) * PIECE)
        if block < 3:
            return d_projection_in[at, block * width : (block + 1) * width].astype(BF16)
        if block < 4:
            return d_projection_out[at, :].astype(BF16)
        if block < 8:
            return d_up_weight[at, (block - 4) * width : (block - 3) * width].astype(BF16)
        start = (block - 8) * width + r * PIECE
        return d_down_weight[:, start : start + PIECE].astype(BF16).T

    for number in range(GROUP * UNIT // PIECE):
        u, r = divmod(number, UNIT // PIECE)
        at = slice(r * PIECE, (r + 1) * PIECE)
        packed[u // LINE, at, u % LINE * width : (u % LINE + 1) * width] = block_piece(number)

    for last in (count - 2, count - 1):
        y_store(last).wait()
        dx_store(last).wait()

        @pl.when(leading)
        def _():
            y_remote(last).wait_send()

        @pl.when(trailing)
        def _():
            dx_remote(last).wait_send()

    if not grouped:
        for u in range(GROUP):
            cols = slice(u % LINE * width, (u % LINE + 1) * width)
            pltpu.sync_copy(packed.at[u // LINE, :, cols], flat_ref.at[u * UNIT : (u + 1) * UNIT])
        pltpu.sync_copy(vector.at[0], vector_ref)
        return

    def landing(name, rel, place):
        col = slice(place * width, (place + 1) * width)
        if name == "core":
            return (kept_a.g if rel else kept_a.h).at[:, col]
        if name == "across":
            return kept_b.h.at[ACROSS_FIRST, col]
        if name == "across 2":
            return e_buf.at[:PIECE]
        kind, up = name
        if kind == 1:
            return (kept_b.g if up else kept_a.qkv).at[ACROSS_FIRST, col]
        if up:
            return (kept_b.g if rel else kept_b.h).at[LINE_FIRST, col]
        if rel:
            return dqkv_buf.at[:PIECE, col]
        return kept_a.qkv.at[LINE_FIRST, col]

    sum_over_group(
        packed, result, landing, vector, flat_ref, vector_ref, group_send, group_recv, group_out, ready
    )


def output_kernel(
    flat,
    vector,
    act,
    grad,
    d_in,
    d_out,
    d_up,
    d_down,
    ag,
    ab,
    ob,
    fg,
    fb,
    d_up_bias,
    db,
    act_out,
    grad_out,
    low,
    wide,
    carried,
    low_sem,
    wide_sem,
    in_sem,
    out_sem,
):
    blocks, width, _ = low.shape

    def load(n):
        return pltpu.make_async_copy(flat.at[n * width : (n + 1) * width], low.at[n], low_sem.at[n])

    def target(n):
        if n < 3:
            return d_in.at[:, n * width : (n + 1) * width]
        if n == 3:
            return d_out
        if n < 8:
            return d_up.at[:, (n - 4) * width : (n - 3) * width]
        return d_down.at[(n - 8) * width : (n - 7) * width]

    def store(n):
        return pltpu.make_async_copy(wide.at[n], target(n), wide_sem.at[n])

    arrays = [(ref.at[n], out.at[n]) for ref, out in ((act, act_out), (grad, grad_out)) for n in range(act.shape[0])]

    def bring(n):
        return pltpu.make_async_copy(arrays[n][0], carried.at[n], in_sem.at[n])

    def take(n):
        return pltpu.make_async_copy(carried.at[n], arrays[n][1], out_sem.at[n])

    for n in range(blocks):
        load(n).start()
    for n in range(len(arrays)):
        bring(n).start()
    for row, out in enumerate((ag, ab, ob, fg, fb, db)):
        out[...] = vector[row : row + 1, :]
    for n in range(d_up_bias.shape[1] // width):
        d_up_bias[:, n * width : (n + 1) * width] = vector[6 + n : 7 + n, :]
    for n in range(blocks):
        load(n).wait()
        wide[n] = low[n].astype(F32)
        store(n).start()
    for n in range(len(arrays)):
        bring(n).wait()
        take(n).start()
    for n in range(blocks):
        store(n).wait()
    for n in range(len(arrays)):
        take(n).wait()


def per_device(
    clip_tokens,
    window_cols,
    time_groups,
    cotangent,
    attention_gain,
    attention_bias,
    projection_in,
    projection_out,
    output_bias,
    feedforward_gain,
    feedforward_bias,
    up_weight,
    up_bias,
    down_weight,
    down_bias,
):
    micro, _, frames, band, width = clip_tokens.shape
    hidden = up_weight.shape[2]
    window = band // WCAP
    rows = frames * window
    weights = (
        attention_gain,
        attention_bias,
        projection_in[0],
        projection_out[0],
        output_bias,
        feedforward_gain,
        feedforward_bias,
        up_weight[0],
        up_bias,
        down_weight[0],
        down_bias,
    )
    smem = pl.BlockSpec(memory_space=pltpu.SMEM)
    vmem = pl.BlockSpec(memory_space=pltpu.VMEM)
    hbm = pl.BlockSpec(memory_space=pl.ANY)
    tokens = jax.ShapeDtypeStruct((micro, frames, band, width), BF16)
    chunk = (frames, window, width)
    group_size = lax.axis_size("dp")
    grouped = group_size % GROUP == 0
    flat_shape = (GROUP * UNIT, width)
    kept_shapes = Kept(
        x=(chunk, BF16),
        a1t=((width, rows), BF16),
        qkv=((rows, 3 * width), BF16),
        p=((rows, width), BF16),
        ot=((width, rows), BF16),
        xh2=((rows, width), BF16),
        a2t=((width, rows), BF16),
        rs2=((rows, 128), F32),
        h=((rows, hidden), BF16),
        g=((rows, hidden), BF16),
    )
    results = pl.pallas_call(
        partial(relay_kernel, (micro, frames, window, width, hidden, grouped)),
        out_shape=(
            tokens,
            tokens,
            jax.ShapeDtypeStruct(flat_shape, BF16),
            jax.ShapeDtypeStruct((VECTOR_ROWS, width), F32),
        )
        + tuple(jax.ShapeDtypeStruct((SLOTS,) + shape, kind) for shape, kind in kept_shapes[1:]),
        in_specs=[smem, smem, hbm, hbm] + [vmem] * len(weights),
        out_specs=[hbm] * (3 + len(kept_shapes)),
        scratch_shapes=[pltpu.VMEM(*kept) for kept in kept_shapes * 2]
        + [
            pltpu.VMEM((width, 3 * width), F32),
            pltpu.VMEM((width, width), F32),
            pltpu.VMEM((width, hidden), F32),
            pltpu.VMEM((width, hidden), F32),
            pltpu.VMEM((SLOTS,) + chunk, BF16),
            pltpu.VMEM((SLOTS,) + chunk, BF16),
            pltpu.VMEM((2,) + chunk, BF16),
            pltpu.VMEM((2,) + chunk, BF16),
            pltpu.VMEM((rows, width), BF16),
            pltpu.VMEM((frames * frames // 2, HEADS, 128), F32),
            pltpu.VMEM((frames * frames // 2, HEADS, 128), F32),
            pltpu.VMEM((rows, width), BF16),
            pltpu.VMEM((rows, width), BF16),
            pltpu.VMEM((rows, width), F32),
            pltpu.VMEM((rows, width), F32),
            pltpu.VMEM((2, rows, FF_BLOCK), F32),
            pltpu.VMEM((rows, width), BF16),
            pltpu.VMEM((width, rows), BF16),
            pltpu.VMEM((rows, width), BF16),
            pltpu.VMEM((rows, width), BF16),
            pltpu.VMEM((rows, 3 * width), BF16),
            pltpu.VMEM((3 * width, rows), F32),
            pltpu.VMEM((width, rows), F32),
            pltpu.VMEM((3 * width, rows), BF16),
            pltpu.VMEM((8, width), F32),
            pltpu.VMEM((8, width), F32),
            pltpu.VMEM((8, width), F32),
            pltpu.VMEM((8, width), F32),
            pltpu.VMEM((8, width), F32),
            pltpu.VMEM((8, hidden), F32),
            pltpu.VMEM((8, width), F32),
            pltpu.SemaphoreType.DMA((SLOTS,)),
            pltpu.SemaphoreType.DMA((SLOTS,)),
            pltpu.SemaphoreType.DMA((2,)),
            pltpu.SemaphoreType.DMA((2,)),
            pltpu.SemaphoreType.DMA((2,)),
            pltpu.SemaphoreType.DMA((2,)),
            pltpu.VMEM((LINE, UNIT, hidden), BF16),
            pltpu.VMEM((LINE, UNIT, hidden), BF16),
            pltpu.SemaphoreType.DMA((len(kept_shapes),)),
            pltpu.SemaphoreType.DMA((len(kept_shapes),)),
            pltpu.VMEM((4 + LINE, VECTOR_ROWS, width), F32),
            pltpu.SemaphoreType.DMA((FAMILIES * LINE,)),
            pltpu.SemaphoreType.DMA((FAMILIES * LINE,)),
            pltpu.SemaphoreType.DMA((2 * GROUP + 1,)),
            pltpu.SemaphoreType.REGULAR((4,)),
        ],
        compiler_params=pltpu.CompilerParams(
            collective_id=0, has_side_effects=True, vmem_limit_bytes=63 * 1024 * 1024
        ),
        name="relay",
    )(
        window_cols,
        time_groups,
        clip_tokens.reshape(micro, frames, band, width),
        cotangent.reshape(micro, frames, band, width),
        *weights,
    )
    activations, input_grads, flat, vector = results[:4]
    if group_size != GROUP:
        groups = None
        if grouped:
            groups = [[first + n for first in range(0, group_size, GROUP)] for n in range(GROUP)]
        flat, vector = lax.psum((flat, vector), "dp", axis_index_groups=groups)
    square = (width, width)
    row = jax.ShapeDtypeStruct((1, width), F32)
    blocks = GROUP * UNIT // width
    d_in, d_out, d_up, d_down, ag, ab, ob, fg, fb, d_up_bias, db, activations, input_grads = pl.pallas_call(
        output_kernel,
        in_specs=[hbm, vmem, hbm, hbm],
        out_specs=[hbm] * 4 + [vmem] * 7 + [hbm] * 2,
        out_shape=[
            jax.ShapeDtypeStruct((width, 3 * width), F32),
            jax.ShapeDtypeStruct(square, F32),
            jax.ShapeDtypeStruct((width, hidden), F32),
            jax.ShapeDtypeStruct((hidden, width), F32),
        ]
        + [row] * 5
        + [jax.ShapeDtypeStruct((1, hidden), F32), row, tokens, tokens],
        scratch_shapes=[
            pltpu.VMEM((blocks,) + square, BF16),
            pltpu.VMEM((blocks,) + square, F32),
            pltpu.VMEM((2 * micro, frames, band, width), BF16),
            pltpu.SemaphoreType.DMA((blocks,)),
            pltpu.SemaphoreType.DMA((blocks,)),
            pltpu.SemaphoreType.DMA((2 * micro,)),
            pltpu.SemaphoreType.DMA((2 * micro,)),
        ],
        compiler_params=pltpu.CompilerParams(vmem_limit_bytes=62 * 1024 * 1024),
        name="outputs",
    )(flat, vector, activations, input_grads)
    shape_out = (1, micro, 1, frames, band, width)
    return (
        activations.reshape(shape_out),
        input_grads.reshape(shape_out),
        ag,
        ab,
        d_in[None],
        d_out[None],
        ob,
        fg,
        fb,
        d_up[None],
        d_up_bias,
        d_down[None],
        db,
    )


def solution(mesh):
    wide, deep = P("section", None), P("section", None, None)
    tokens = P(None, "dp", None, None, None)
    weights = (wide, wide, deep, deep, wide, wide, wide, deep, wide, deep, wide)
    outputs = P("section", None, "dp", None, None, None)
    return jax.shard_map(
        per_device,
        mesh=mesh,
        in_specs=(tokens, P(None, "dp"), P(None, "dp", None), tokens) + weights,
        out_specs=(outputs, outputs) + weights,
        check_vma=False,
    )
```

```python
from collections import namedtuple
from functools import partial

import jax
import jax.numpy as jnp
from jax import lax
from jax.experimental import pallas as pl
from jax.experimental.pallas import tpu as pltpu
from jax.sharding import PartitionSpec as P

HEADS = 8
WCAP = 5
EPSILON = 1e-05
MASKED = -1e30
MESH = pl.DeviceIdType.MESH

F32 = jnp.float32
BF16 = jnp.bfloat16

LEAD = 4
SLOTS = LEAD + 1
Kept = namedtuple("Kept", ("x", "a1t", "qkv", "p", "ot", "xh2", "a2t", "rs2", "h", "g"))
FF_BLOCK = 512
ROWS_AT_ONCE = 32
COLS_AT_ONCE = 256

INV_SQRT2 = 0.7071067811865476
PDF = 0.3989422804014327
LOG2E = 1.4426950408889634


def mm(a, b):
    return lax.dot_general(a, b, (((1,), (0,)), ((), ())), preferred_element_type=F32)


def mm_bt(a, b):
    return lax.dot_general(a, b, (((1,), (1,)), ((), ())), preferred_element_type=F32)


def mm_at(a, b):
    return lax.dot_general(a, b, (((0,), (0,)), ((), ())), preferred_element_type=F32)


def gelu_and_slope(u):
    cdf = 0.5 + 0.5 * lax.erf(INV_SQRT2 * u)
    bell = jnp.exp2((-0.5 * LOG2E) * (u * u))
    return u * cdf, cdf + (PDF * u) * bell


def fold8(values):
    rows, cols = values.shape
    return jnp.sum(values.reshape(rows // 8, 8, cols), axis=0)


GROUP = 16
LINE = 4
LINE_ORDER = (3, 0, 2, 1)
UNIT = 384
PIECE = 128
WHOLE = slice(0, UNIT)
ACROSS_FIRST = slice(0, 256)
LINE_FIRST = slice(256, UNIT)
PART = {1: ACROSS_FIRST, 2: LINE_FIRST}
SIDES = {1: (0,), 2: (0, 1)}
FAMILIES = 32
VECTOR_ROWS = 16


def group_place():
    me = lax.axis_index("dp")
    core, across, line = lax.rem(me, 2), lax.rem(lax.div(me, 2), 2), lax.rem(lax.div(me, 4), LINE)
    sibling, beside = {"dp": me + 1 - 2 * core}, {"dp": me + 2 - 4 * across}
    return core, across, line, sibling, beside, {"dp": me + 4}, {"dp": me - 4}


def sum_over_group(packed, result, landing, vector, flat_ref, vector_ref, send_sem, recv_sem, out_sem, ready):
    core, across, line, sibling, beside, above, below = group_place()
    sides = (across, 1 - across)
    families = {}
    pending = []

    def when(condition, action):
        if condition is None:
            action()
        else:
            pl.when(condition)(action)

    def remote(family, place, source, target, device):
        number = families.setdefault(family, len(families)) * LINE + place
        return pltpu.make_async_remote_copy(
            src_ref=source,
            dst_ref=target,
            send_sem=send_sem.at[number],
            recv_sem=recv_sem.at[number],
            device_id=device,
            device_id_type=MESH,
        )

    def start(family, place, source, target, device):
        remote(family, place, source, target, device).start()

    def sent(family, place, source, device, condition=None):
        pending.append((condition, lambda: remote(family, place, source, source, device).wait_send()))

    def received(family, place, target, device):
        remote(family, place, target, target, device).wait_recv()

    def unit(ref, half, side, place, part):
        column = place * 512 if isinstance(place, int) else pl.multiple_of(place * 512, 512)
        return ref.at[half * 2 + side, part, pl.ds(column, 512)]

    def add(target, arrived):
        for r in range(0, target.shape[0], 64):
            at = slice(r, r + 64)
            target[at] = (target[at].astype(F32) + arrived[at].astype(F32)).astype(BF16)

    def store(far, rel, place, kind):
        half, side, part = (1 - core if far else core), sides[rel], PART[kind]
        row = pl.multiple_of(((half * 2 + side) * LINE + place) * UNIT + part.start, PIECE)
        return pltpu.make_async_copy(
            unit(result, half, side, place, part),
            flat_ref.at[pl.ds(row, part.stop - part.start)],
            out_sem.at[((far * 2 + rel) * 2 + kind - 1) * LINE + place],
        )

    for number, (device, condition) in enumerate(
        ((sibling, None), (beside, None), (below, line > 0), (above, line < LINE - 1))
    ):
        there = number if number < 2 else 5 - number
        when(
            condition,
            partial(pl.semaphore_signal, ready.at[there], inc=1, device_id=device, device_id_type=MESH),
        )
    pl.semaphore_wait(ready.at[0], 1)

    start("vector core", 0, vector.at[0], vector.at[1], sibling)
    sent("vector core", 0, vector.at[0], sibling)
    for place in LINE_ORDER:
        for side in range(2):
            source = unit(packed, 1 - core, side, place, WHOLE)
            start(("core", side), place, source, landing("core", side, place), sibling)
            sent(("core", side), place, source, sibling)
    pl.semaphore_wait(ready.at[1], 1)
    pl.when(line > 0)(lambda: pl.semaphore_wait(ready.at[2], 1))
    pl.when(line < LINE - 1)(lambda: pl.semaphore_wait(ready.at[3], 1))

    def line_send(kind, place, up, condition):
        device = above if up else below

        def go():
            for rel in SIDES[kind]:
                source = unit(packed, core, sides[rel], place, PART[kind])
                start((kind, up, rel), place, source, landing((kind, up), rel, place), device)

        pl.when(condition)(go)
        for rel in SIDES[kind]:
            sent((kind, up, rel), place, unit(packed, core, sides[rel], place, PART[kind]), device, condition)

    def line_take(kind, place, up, condition):
        def go():
            for rel in SIDES[kind]:
                spot = landing((kind, up), rel, place)
                received((kind, up, rel), place, spot, below if up else above)
                add(unit(packed, core, sides[rel], place, PART[kind]), spot)

        pl.when(condition)(go)

    def from_ends(kind, place):
        if place > 0:
            line_send(kind, place, True, line == 0)
        if place < LINE - 1:
            line_send(kind, place, False, line == LINE - 1)

    def inner_step(kind, k):
        place = LINE - 1 - k
        line_take(kind, place, True, (line > 0) & (line <= place))
        if place > 1:
            line_send(kind, place, True, (line > 0) & (line < place))
        place = k
        line_take(kind, place, False, (line < LINE - 1) & (line >= place))
        if place < LINE - 2:
            line_send(kind, place, False, (line < LINE - 1) & (line > place))

    def take_across(place):
        spot = landing("across", 0, place)
        received("across", place, spot, beside)
        add(unit(packed, core, sides[0], place, ACROSS_FIRST), spot)
        from_ends(1, place)

    for place in LINE_ORDER:
        for side in range(2):
            spot = landing("core", side, place)
            received(("core", side), place, spot, sibling)
            add(unit(packed, core, side, place, WHOLE), spot)
        source = unit(packed, core, sides[1], place, ACROSS_FIRST)
        start("across", place, source, landing("across", 0, place), beside)
        sent("across", place, source, beside)
        from_ends(2, place)
    received("vector core", 0, vector.at[1], sibling)
    vector[2] = vector[0] + vector[1]
    start("vector across", 0, vector.at[2], vector.at[3], beside)
    sent("vector across", 0, vector.at[2], beside)
    for k in range(LINE - 1):
        take_across(LINE_ORDER[k])
        inner_step(2, k)
    take_across(LINE_ORDER[LINE - 1])
    source = unit(packed, core, sides[1], line, LINE_FIRST)
    start("across 2", 0, source, landing("across 2", 0, 0), beside)
    sent("across 2", 0, source, beside)
    received("vector across", 0, vector.at[3], beside)
    vector[4 + line] = vector[2] + vector[3]
    inner_step(1, 0)
    inner_step(1, 1)
    spot = landing("across 2", 0, 0)
    received("across 2", 0, spot, beside)
    own = unit(packed, core, sides[0], line, LINE_FIRST)
    add(own, spot)
    own_two = unit(result, core, sides[0], line, LINE_FIRST)
    own_two[...] = own[...]
    start("gather across 2", 0, own_two, own_two, beside)
    sent("gather across 2", 0, own_two, beside)
    inner_step(1, 2)
    own_one = unit(result, core, sides[0], line, ACROSS_FIRST)
    own_one[...] = unit(packed, core, sides[0], line, ACROSS_FIRST)[...]

    def spread(family, place, spot, up, down):
        if up is not None:
            pl.when(up)(lambda: start((family, True), place, spot, spot, above))
        if down is not None:
            pl.when(down)(lambda: start((family, False), place, spot, spot, below))

    def hand_over(kind, rel, place):
        spot = unit(result, core, sides[rel], place, PART[kind])
        start(("gather core", kind, rel), place, spot, spot, sibling)
        store(0, rel, place, kind).start()

    def have(kind, rel, place, up, down):
        spot = unit(result, core, sides[rel], place, PART[kind])
        spread(("spread", kind, rel), place, spot, up, down)
        if kind == 1:
            start("gather across", place, spot, spot, beside)
        hand_over(kind, rel, place)

    def come(distance, action):
        pl.when(line >= distance)(lambda: action(line - distance, True))
        pl.when(line + distance < LINE)(lambda: action(line + distance, False))

    def arrive(kind, rel, distance):
        def action(place, up):
            spot = unit(result, core, sides[rel], place, PART[kind])
            received((("spread", kind, rel), up), place, spot, below if up else above)
            have(kind, rel, place, line < LINE - 1 if up else None, None if up else line > 0)

        come(distance, action)

    def arrive_vector(distance):
        def action(place, up):
            spot = vector.at[4 + place]
            received(("vector", up), place, spot, below if up else above)
            spread("vector", place, spot, line < LINE - 1 if up else None, None if up else line > 0)

        come(distance, action)

    def arrive_across(distance):
        def action(place, up):
            received("gather across", place, unit(result, core, sides[1], place, ACROSS_FIRST), beside)
            hand_over(1, 1, place)

        if distance == 0:
            action(line, True)
        else:
            come(distance, action)

    have(1, 0, line, line < LINE - 1, line > 0)
    have(2, 0, line, line < LINE - 1, line > 0)
    spread("vector", line, vector.at[4 + line], line < LINE - 1, line > 0)
    received("gather across 2", 0, unit(result, core, sides[1], line, LINE_FIRST), beside)
    have(2, 1, line, line < LINE - 1, line > 0)
    for distance in range(1, LINE):
        arrive(1, 0, distance)
        arrive(2, 0, distance)
        arrive(2, 1, distance)
        arrive_vector(distance)
        arrive_across(distance - 1)
    arrive_across(LINE - 1)
    vector[1] = (vector[4] + vector[5]) + (vector[6] + vector[7])
    vector_out = pltpu.make_async_copy(vector.at[1], vector_ref, out_sem.at[2 * GROUP])
    vector_out.start()
    for place in range(LINE):
        for kind in (1, 2):
            for rel in range(2):
                spot = unit(result, 1 - core, sides[rel], place, PART[kind])
                received(("gather core", kind, rel), place, spot, sibling)
                store(1, rel, place, kind).start()
    vector_out.wait()

    for place in range(LINE):
        for kind in (1, 2):
            for rel in range(2):
                spot = unit(result, core, sides[rel], place, PART[kind])
                sent(("gather core", kind, rel), place, spot, sibling)
                store(0, rel, place, kind).wait()
                store(1, rel, place, kind).wait()
            for rel in SIDES[kind]:
                spot = unit(result, core, sides[rel], place, PART[kind])
                sent((("spread", kind, rel), True), place, spot, above, (line >= place) & (line < LINE - 1))
                sent((("spread", kind, rel), False), place, spot, below, (line <= place) & (line > 0))
        sent("gather across", place, unit(result, core, sides[0], place, ACROSS_FIRST), beside)
        sent(("vector", True), place, vector.at[4 + place], above, (line >= place) & (line < LINE - 1))
        sent(("vector", False), place, vector.at[4 + place], below, (line <= place) & (line > 0))
    for condition, wait in pending:
        when(condition, wait)


def relay_kernel(
    dims,
    cols_ref,
    groups_ref,
    clip_ref,
    cot_ref,
    attention_gain,
    attention_bias,
    projection_in,
    projection_out,
    output_bias,
    feedforward_gain,
    feedforward_bias,
    up_weight,
    up_bias,
    down_weight,
    down_bias,
    act_ref,
    grad_ref,
    flat_ref,
    vector_ref,
    *scratch,
):
    micro, frames, window, width, hidden, grouped = dims
    parked, scratch = scratch[: len(Kept._fields) - 1], scratch[len(Kept._fields) - 1 :]
    small = len(Kept._fields) - 2
    (packed, in_t, out_t, up_t, down_t), scratch = scratch[:5], scratch[5:]
    kept_a, scratch = Kept(*scratch[:small], packed.at[0], packed.at[1]), scratch[small:]
    kept_b, scratch = Kept(*scratch[:small], packed.at[2], packed.at[3]), scratch[small:]
    (
    d_projection_in,
    d_projection_out,
    d_up_weight,
    d_down_weight,
    xbuf,
    dybuf,
    ybuf,
    dxbuf,
    pf_buf,
    ds_buf,
    wide,
    total,
    u_buf,
    e_buf,
    et_buf,
    c_buf,
    do_buf,
    dqkv_buf,
    qkvt_buf,
    dqkvt_buf,
    sum_ag,
    sum_ab,
    sum_ob,
    sum_fg,
    sum_fb,
    sum_ub,
    sum_db,
    x_sem,
    dy_sem,
    y_sem,
    y_send,
    dx_sem,
    dx_send,
    result,
    park_sem,
    fetch_sem,
    vector,
    group_send,
    group_recv,
    group_out,
    ready,
    ) = scratch
    a1_buf, o_buf, a2_buf, wide_b = do_buf, e_buf, c_buf, wide
    rows = frames * window
    count = micro * WCAP
    head = width // HEADS
    pair = 2 * head
    scale = head ** (-0.5)
    section = lax.axis_index("section")
    leading = section == 0
    trailing = section != 0
    lead = LEAD * (1 - section)
    partner = {"section": 1 - section}

    def hbm_chunk(ref, chunk):
        start = pl.multiple_of(lax.rem(chunk, WCAP) * window, window)
        return ref.at[lax.div(chunk, WCAP), :, pl.ds(start, window), :]

    def x_load(chunk):
        slot = lax.rem(chunk, SLOTS)
        return pltpu.make_async_copy(hbm_chunk(clip_ref, chunk), xbuf.at[slot], x_sem.at[slot])

    def dy_load(chunk):
        slot = lax.rem(chunk, SLOTS)
        return pltpu.make_async_copy(hbm_chunk(cot_ref, chunk), dybuf.at[slot], dy_sem.at[slot])

    def y_store(chunk):
        slot = lax.rem(chunk, 2)
        return pltpu.make_async_copy(ybuf.at[slot], hbm_chunk(act_ref, chunk), y_sem.at[slot])

    def dx_store(chunk):
        slot = lax.rem(chunk, 2)
        return pltpu.make_async_copy(dxbuf.at[slot], hbm_chunk(grad_ref, chunk), dx_sem.at[slot])

    def park(chunk):
        slot = lax.rem(chunk, SLOTS)
        return [
            pltpu.make_async_copy(here, there.at[slot], park_sem.at[n])
            for n, (here, there) in enumerate(zip(kept_a[1:], parked))
        ]

    def fetch(chunk):
        slot = lax.rem(chunk, SLOTS)
        return [pltpu.make_async_copy(hbm_chunk(clip_ref, chunk), kept_b.x, fetch_sem.at[0])] + [
            pltpu.make_async_copy(there.at[slot], here, fetch_sem.at[n + 1])
            for n, (here, there) in enumerate(zip(kept_b[1:], parked))
        ]

    def start_all(copies):
        for copy in copies:
            copy.start()

    def wait_all(copies):
        for copy in copies:
            copy.wait()

    def y_remote(chunk):
        slot, there = lax.rem(chunk, 2), lax.rem(chunk, SLOTS)
        return pltpu.make_async_remote_copy(
            src_ref=ybuf.at[slot],
            dst_ref=xbuf.at[there],
            send_sem=y_send.at[slot],
            recv_sem=x_sem.at[there],
            device_id=partner,
            device_id_type=MESH,
        )

    def dx_remote(chunk):
        slot, there = lax.rem(chunk, 2), lax.rem(chunk, SLOTS)
        return pltpu.make_async_remote_copy(
            src_ref=dxbuf.at[slot],
            dst_ref=dybuf.at[there],
            send_sem=dx_send.at[slot],
            recv_sem=dy_sem.at[there],
            device_id=partner,
            device_id_type=MESH,
        )

    barrier = pltpu.get_barrier_semaphore()
    greeted = 1
    pl.semaphore_signal(barrier, inc=1, device_id=partner, device_id_type=MESH)
    if grouped:
        _, _, line, sibling, beside, above, below = group_place()
        has_below, has_above = line > 0, line < LINE - 1
        for device, condition in ((sibling, None), (beside, None), (below, has_below), (above, has_above)):
            greet = partial(pl.semaphore_signal, barrier, inc=1, device_id=device, device_id_type=MESH)
            if condition is None:
                greet()
            else:
                pl.when(condition)(greet)
        greeted = 3 + has_below.astype(jnp.int32) + has_above.astype(jnp.int32)

    @pl.when(leading)
    def _():
        x_load(0).start()

    @pl.when(trailing)
    def _():
        dy_load(0).start()

    for total_ref in (d_projection_in, d_projection_out, d_up_weight, d_down_weight):
        total_ref[...] = jnp.zeros_like(total_ref)
    for total_ref in (sum_ag, sum_ab, sum_ob, sum_fg, sum_fb, sum_ub, sum_db):
        total_ref[...] = jnp.zeros_like(total_ref)

    pl.semaphore_wait(barrier, greeted)

    def frame_rows(i):
        return slice(i * window, (i + 1) * window)

    half = lax.broadcasted_iota(jnp.int32, (window, pair), 1) < head
    low_half = jnp.where(half, 1.0, 0.0).astype(BF16)
    high_half = jnp.where(half, 0.0, 1.0).astype(BF16)

    def by_head(values):
        return jnp.concatenate([values * low_half, values * high_half], axis=0)

    def join_heads(values):
        return jnp.where(half, values[:window], values[window:])

    heads_of = [
        (frame_rows(f), slice(n * pair, (n + 1) * pair), n) for f in range(frames) for n in range(width // pair)
    ]

    def of_pair(ref, at, which, n):
        return ref[at, which * width + n * pair : which * width + (n + 1) * pair]

    def window_forward(kept):
        for at, lanes, n in heads_of:
            keys = of_pair(kept.qkv, at, 1, n)
            total[at, lanes] = mm_bt(keys, by_head(of_pair(kept.qkv, at, 0, n)))
        yield 0
        for at, lanes, n in heads_of:
            scores = total[at, lanes] * scale
            scores = jnp.exp(scores - jnp.max(scores, axis=0, keepdims=True))
            probs = scores * (1.0 / jnp.sum(scores, axis=0, keepdims=True))
            kept.p[at, lanes] = probs.astype(BF16)
        yield 0
        for at, lanes, n in heads_of:
            values = of_pair(kept.qkv, at, 2, n)
            o_buf[at, lanes] = join_heads(mm_at(kept.p[at, lanes], values)).astype(BF16)

    def window_backward(kept):
        for at, lanes, n in heads_of:
            up = by_head(do_buf[at, lanes])
            total[at, lanes] = mm_bt(of_pair(kept.qkv, at, 2, n), up)
            dv = mm(kept.p[at, lanes], up)
            dqkv_buf[at, 2 * width + n * pair : 2 * width + (n + 1) * pair] = dv.astype(BF16)
        yield 0
        for at, lanes, n in heads_of:
            probs = kept.p[at, lanes].astype(F32)
            dp = total[at, lanes]
            ds = probs * (dp - jnp.sum(probs * dp, axis=0, keepdims=True))
            e_buf[at, lanes] = ds.astype(BF16)
        yield 0
        for at, lanes, n in heads_of:
            ds = e_buf[at, lanes]
            dk = mm(ds, by_head(of_pair(kept.qkv, at, 0, n))) * scale
            dqkv_buf[at, width + n * pair : width + (n + 1) * pair] = dk.astype(BF16)
            dq = join_heads(mm_at(ds, of_pair(kept.qkv, at, 1, n))) * scale
            dqkv_buf[at, lanes] = dq.astype(BF16)

    low_frame = lax.broadcasted_iota(jnp.int32, (1, 128), 1) < window

    def lane_tiles(i):
        return min(i + 1, frames - 1) // 2 + 1

    def tile(t):
        return slice(t * 128, (t + 1) * 128)

    def head_rows(which, h):
        return slice(which * width + h * head, which * width + (h + 1) * head)

    def other_half(values):
        return pltpu.roll(values, window, axis=1)

    def both_frames(ref, at, t):
        values = ref[at, tile(t)].astype(F32)
        turned = other_half(values)
        return jnp.where(low_frame, values, turned), jnp.where(low_frame, turned, values)

    tile_count = frames // 2

    def frame_forward(chunk, kept):
        for n in range(3):
            flat = kept.qkv[:, n * width : (n + 1) * width].T
            qkvt_buf[n * width : (n + 1) * width, :] = flat.astype(F32)
            yield 150
        for h in range(HEADS):
            keys = [qkvt_buf[head_rows(1, h), tile(t)] for t in range(tile_count)]
            for pair_index in range(tile_count):
                queries = both_frames(qkvt_buf, head_rows(0, h), pair_index)
                for i in (2 * pair_index, 2 * pair_index + 1):
                    for t in range(lane_tiles(i)):
                        score = jnp.sum(queries[i % 2] * keys[t], axis=0, keepdims=True)
                        ds_buf[i * tile_count + t, h : h + 1, :] = score
            yield 120
        item = lax.div(chunk, WCAP)
        labels = [
            jnp.where(low_frame, groups_ref[item, 0, 2 * t], groups_ref[item, 0, 2 * t + 1])
            for t in range(tile_count)
        ]
        for i in range(frames):
            mine = groups_ref[item, 0, i]
            parts = [
                jnp.where(labels[t] <= mine, ds_buf[i * tile_count + t] * scale, MASKED)
                for t in range(lane_tiles(i))
            ]
            largest = parts[0]
            for part in parts[1:]:
                largest = jnp.maximum(largest, part)
            largest = jnp.maximum(largest, other_half(largest))
            parts = [jnp.exp(part - largest) for part in parts]
            whole = parts[0]
            for part in parts[1:]:
                whole = whole + part
            whole = 1.0 / (whole + other_half(whole))
            for t, part in enumerate(parts):
                pf_buf[i * tile_count + t] = part * whole
        yield 150
        for h in range(HEADS):
            values = [qkvt_buf[head_rows(2, h), tile(t)] for t in range(tile_count)]
            for pair_index in range(tile_count):
                mixed = []
                for i in (2 * pair_index, 2 * pair_index + 1):
                    part = 0.0
                    for t in range(lane_tiles(i)):
                        part = part + pf_buf[i * tile_count + t, h : h + 1, :] * values[t]
                    mixed.append(part + other_half(part))
                both = jnp.where(low_frame, mixed[0], mixed[1])
                kept.ot[head_rows(0, h), tile(pair_index)] = both.astype(BF16)
            yield 120

    def frame_backward(dot_buf, beside):
        for h in range(HEADS):
            beside()
            values = [qkvt_buf[head_rows(2, h), tile(t)] for t in range(tile_count)]
            dv = [0.0] * tile_count
            for pair_index in range(tile_count):
                ups = both_frames(dot_buf, head_rows(0, h), pair_index)
                for i in (2 * pair_index, 2 * pair_index + 1):
                    for t in range(lane_tiles(i)):
                        ds_buf[i * tile_count + t, h : h + 1, :] = jnp.sum(
                            ups[i % 2] * values[t], axis=0, keepdims=True
                        )
                        dv[t] = dv[t] + pf_buf[i * tile_count + t, h : h + 1, :] * ups[i % 2]
            for t in range(tile_count):
                dqkvt_buf[head_rows(2, h), tile(t)] = dv[t].astype(BF16)
            yield 220
        for i in range(frames):
            spots = [i * tile_count + t for t in range(lane_tiles(i))]
            along = pf_buf[spots[0]] * ds_buf[spots[0]]
            for spot in spots[1:]:
                along = along + pf_buf[spot] * ds_buf[spot]
            along = along + other_half(along)
            for spot in spots:
                ds_buf[spot] = pf_buf[spot] * (ds_buf[spot] - along) * scale
        yield 100
        for h in range(HEADS):
            beside()
            keys = [qkvt_buf[head_rows(1, h), tile(t)] for t in range(tile_count)]
            dk = [0.0] * tile_count
            dq_tiles = []
            for pair_index in range(tile_count):
                queries = both_frames(qkvt_buf, head_rows(0, h), pair_index)
                dq = []
                for i in (2 * pair_index, 2 * pair_index + 1):
                    part = 0.0
                    for t in range(lane_tiles(i)):
                        ds = ds_buf[i * tile_count + t, h : h + 1, :]
                        part = part + ds * keys[t]
                        dk[t] = dk[t] + ds * queries[i % 2]
                    dq.append(part + other_half(part))
                dq_tiles.append(jnp.where(low_frame, dq[0], dq[1]))
            for t in range(tile_count):
                dqkvt_buf[head_rows(0, h), tile(t)] = dq_tiles[t].astype(BF16)
                dqkvt_buf[head_rows(1, h), tile(t)] = dk[t].astype(BF16)
            yield 240
        for n in range(3):
            dqkv_buf[:, n * width : (n + 1) * width] = dqkvt_buf[n * width : (n + 1) * width, :].T
            yield 100

    def live_of(chunk):
        cols = cols_ref[lax.div(chunk, WCAP), 0]
        return jnp.where(lax.rem(chunk, WCAP) < cols, 1.0, 0.0).astype(F32)

    def standardize(values):
        centered = values - jnp.mean(values, axis=-1, keepdims=True)
        rstd = lax.rsqrt(jnp.mean(centered * centered, axis=-1, keepdims=True) + EPSILON)
        return centered * rstd, rstd

    blocks = [
        (slice(r, r + ROWS_AT_ONCE), r // window, slice(r % window, r % window + ROWS_AT_ONCE))
        for r in range(0, rows, ROWS_AT_ONCE)
    ]
    ff_parts = [slice(c, c + FF_BLOCK) for c in range(0, hidden, FF_BLOCK)]

    def halves(cols, start=0, step=COLS_AT_ONCE):
        return [slice(c, c + step) for c in range(start, start + cols, step)]

    def forward(spatial, chunk, kept, slot, y_slot):
        kept.x[...] = xbuf[slot]
        for at, f, within in blocks:
            unit, _ = standardize(kept.x[f, within].astype(F32))
            a1_buf[at, :] = (unit * attention_gain[...] + attention_bias[...]).astype(BF16)
            yield 90
        kept.a1t[...] = a1_buf[...].T
        for part in halves(3 * width, step=width):
            kept.qkv[:, part] = mm(a1_buf[...], projection_in[:, part]).astype(BF16)
            yield 400
        if spatial:
            yield from window_forward(kept)
            kept.ot[...] = o_buf[...].T
        else:
            yield from frame_forward(chunk, kept)
            o_buf[...] = kept.ot[...].T
        wide[...] = mm(o_buf[...], projection_out[...])
        yield 400
        yield "half"
        for at, f, within in blocks:
            middle = kept.x[f, within].astype(F32) + (wide[at, :] + output_bias[...])
            wide[at, :] = middle + down_bias[...]
            unit, rstd = standardize(middle)
            kept.xh2[at, :] = unit.astype(BF16)
            kept.rs2[at, :] = jnp.broadcast_to(rstd, (ROWS_AT_ONCE, 128))
            a2_buf[at, :] = (unit * feedforward_gain[...] + feedforward_bias[...]).astype(BF16)
            yield 110
        kept.a2t[...] = a2_buf[...].T
        u_buf[0] = mm(a2_buf[...], up_weight[:, ff_parts[0]])
        yield 400
        for n, part in enumerate(ff_parts):
            if n + 1 < len(ff_parts):
                u_buf[(n + 1) % 2] = mm(a2_buf[...], up_weight[:, ff_parts[n + 1]])
                yield 400
            for at, _, _ in blocks:
                for inner, outer in zip(halves(FF_BLOCK), halves(FF_BLOCK, part.start)):
                    h, slope = gelu_and_slope(u_buf[n % 2, at, inner] + up_bias[:, outer])
                    kept.h[at, outer] = h.astype(BF16)
                    kept.g[at, outer] = slope.astype(BF16)
                    yield 30
        u_buf[0] = mm(kept.h[...], down_weight[...])
        yield 1500
        live = live_of(chunk)
        for at, f, within in blocks:
            ybuf[y_slot, f, within] = ((wide[at, :] + u_buf[0, at, :]) * live).astype(BF16)
            yield 15
        y_store(chunk).start()
        if spatial:
            y_remote(chunk).start()
        yield "half"

    def norm_backward(d_normed, unit, rstd, gain):
        d_unit = d_normed * gain
        along = jnp.mean(d_unit * unit, axis=-1, keepdims=True)
        return rstd * (d_unit - jnp.mean(d_unit, axis=-1, keepdims=True) - unit * along)

    def weight_gradient(total_ref, left, right, cols):
        for part in cols:
            total_ref[:, part] += mm(left[...], right[:, part])
            yield 300

    def backward(spatial, chunk, kept, slot, dx_slot):
        if spatial:
            dx_remote(chunk).wait_recv()
        else:
            dy_load(chunk).wait()

        @pl.when(chunk >= 2)
        def _():
            dx_store(chunk - 2).wait()
            if not spatial:
                dx_remote(chunk - 2).wait_send()

        live = live_of(chunk)
        e_buf[...] = (dybuf[slot].reshape(rows, width).astype(F32) * live).astype(BF16)
        for at, f, within in blocks:
            sum_db[...] += fold8(e_buf[at, :].astype(F32))
        et_buf[...] = e_buf[...].T
        u_buf[0] = mm(e_buf[...], down_t[:, ff_parts[0]])
        yield 600
        for n, part in enumerate(ff_parts):
            if n + 1 < len(ff_parts):
                u_buf[(n + 1) % 2] = mm(e_buf[...], down_t[:, ff_parts[n + 1]])
                yield 400
            if spatial:
                yield from weight_gradient(d_down_weight, et_buf, kept.h, halves(FF_BLOCK, part.start))
            for at, _, _ in blocks:
                for inner, outer in zip(halves(FF_BLOCK), halves(FF_BLOCK, part.start)):
                    du = u_buf[n % 2, at, inner] * kept.g[at, outer].astype(F32)
                    sum_ub[:, outer] += fold8(du)
                    kept.g[at, outer] = du.astype(BF16)
                    yield 12
        total[...] = mm(kept.g[...], up_t[...])
        yield 1500
        grown = (d_up_weight, kept.a2t, kept.g) if spatial else (d_down_weight, et_buf, kept.h)
        grown = weight_gradient(*grown, halves(hidden))
        for n, (at, _, _) in enumerate(blocks):
            if n % 3 < 2:
                yield next(grown)
            d_normed = total[at, :]
            unit = kept.xh2[at, :].astype(F32)
            sum_fg[...] += fold8(d_normed * unit)
            sum_fb[...] += fold8(d_normed)
            rstd = kept.rs2[at, 0:1]
            d_middle = e_buf[at, :].astype(F32) + norm_backward(d_normed, unit, rstd, feedforward_gain[...])
            wide_b[at, :] = d_middle
            sum_ob[...] += fold8(d_middle)
            c_buf[at, :] = d_middle.astype(BF16)
            yield 120
        yield "half"
        if spatial:
            do_buf[...] = mm(c_buf[...], out_t[...]).astype(BF16)
        else:
            kept_b.a2t[...] = mm_bt(projection_out[...], c_buf[...]).astype(BF16)
        yield 400
        out_gradient = weight_gradient(d_projection_out, kept.ot, c_buf, halves(width))
        if spatial:
            yield from out_gradient
            yield from window_backward(kept)
        else:
            grown = weight_gradient(d_up_weight, kept.a2t, kept.g, halves(hidden))

            def beside():
                if next(grown, None) is None:
                    next(out_gradient, None)

            yield from frame_backward(kept_b.a2t, beside)
        total[...] = mm(dqkv_buf[...], in_t[...])
        yield 1100
        for n, (at, f, within) in enumerate(blocks):
            if n % 2 == 0:
                part = halves(COLS_AT_ONCE, n // 2 * COLS_AT_ONCE)
                yield from weight_gradient(d_projection_in, kept.a1t, dqkv_buf, part)
            d_normed = total[at, :]
            unit, rstd = standardize(kept.x[f, within].astype(F32))
            sum_ag[...] += fold8(d_normed * unit)
            sum_ab[...] += fold8(d_normed)
            dx = wide_b[at, :] + norm_backward(d_normed, unit, rstd, attention_gain[...])
            do_buf[at, :] = dx.astype(BF16)
            yield 140
        dxbuf[dx_slot] = do_buf[...].reshape(frames, window, width)
        dx_store(chunk).start()
        if not spatial:
            dx_remote(chunk).start()
        yield "half"

    def emit(pieces):
        for _ in pieces:
            pass

    def transpose_weights():
        for weight, transposed in (
            (down_weight, down_t),
            (up_weight, up_t),
            (projection_out, out_t),
            (projection_in, in_t),
        ):
            transposed[...] = weight[...].T

    @pl.when(trailing)
    def _():
        transpose_weights()

    def step(t, carry):
        chunk = t - lead
        ahead = (t, kept_a, lax.rem(t, SLOTS), lax.rem(t, 2))
        behind = (chunk, lax.rem(chunk + SLOTS, SLOTS), lax.rem(chunk + 2, 2))

        @pl.when(t < count)
        def _():
            @pl.when(leading)
            def _():
                x_load(t).wait()

                @pl.when(t + 1 < count)
                def _():
                    x_load(t + 1).start()

            @pl.when(leading & (t >= 2))
            def _():
                y_store(t - 2).wait()
                y_remote(t - 2).wait_send()

        @pl.when(leading & (t > 0) & (t <= count))
        def _():
            wait_all(park(t - 1))

        @pl.when(leading & (t == 1))
        def _():
            start_all(fetch(0))

        @pl.when(leading & (t < count))
        def _():
            emit(forward(True, *ahead))
            start_all(park(t))

        @pl.when(leading & (chunk >= 0))
        def _():
            wait_all(fetch(chunk))
            emit(backward(True, chunk, kept_b, *behind[1:]))

            @pl.when(chunk + 1 < count)
            def _():
                start_all(fetch(chunk + 1))

        @pl.when(leading & (t == 0))
        def _():
            transpose_weights()

        @pl.when(trailing & (t < count))
        def _():
            y_remote(t).wait_recv()

            @pl.when(t + 1 < count)
            def _():
                dy_load(t + 1).start()

            @pl.when(t >= 2)
            def _():
                y_store(t - 2).wait()

            emit(forward(False, *ahead))
            emit(backward(False, chunk, kept_a, *behind[1:]))

        return carry

    lax.fori_loop(0, count + LEAD, step, 0)

    vector[0] = jnp.zeros_like(vector[0])
    for row, partial_sum in enumerate((sum_ag, sum_ab, sum_ob, sum_fg, sum_fb, sum_db)):
        vector[0, row : row + 1, :] = jnp.sum(partial_sum[...], axis=0, keepdims=True)
    for n in range(hidden // width):
        up_sum = jnp.sum(sum_ub[:, n * width : (n + 1) * width], axis=0, keepdims=True)
        vector[0, 6 + n : 7 + n, :] = up_sum

    def block_piece(number):
        block, r = divmod(number, width // PIECE)
        at = slice(r * PIECE, (r + 1) * PIECE)
        if block < 3:
            return d_projection_in[at, block * width : (block + 1) * width].astype(BF16)
        if block < 4:
            return d_projection_out[at, :].astype(BF16)
        if block < 8:
            return d_up_weight[at, (block - 4) * width : (block - 3) * width].astype(BF16)
        start = (block - 8) * width + r * PIECE
        return d_down_weight[:, start : start + PIECE].astype(BF16).T

    for number in range(GROUP * UNIT // PIECE):
        u, r = divmod(number, UNIT // PIECE)
        at = slice(r * PIECE, (r + 1) * PIECE)
        packed[u // LINE, at, u % LINE * width : (u % LINE + 1) * width] = block_piece(number)

    for last in (count - 2, count - 1):
        y_store(last).wait()
        dx_store(last).wait()

        @pl.when(leading)
        def _():
            y_remote(last).wait_send()

        @pl.when(trailing)
        def _():
            dx_remote(last).wait_send()

    if not grouped:
        for u in range(GROUP):
            cols = slice(u % LINE * width, (u % LINE + 1) * width)
            pltpu.sync_copy(packed.at[u // LINE, :, cols], flat_ref.at[u * UNIT : (u + 1) * UNIT])
        pltpu.sync_copy(vector.at[0], vector_ref)
        return

    def landing(name, rel, place):
        col = slice(place * width, (place + 1) * width)
        if name == "core":
            return up_t.at[place * width : place * width + UNIT] if rel else down_t.at[:UNIT, col]
        if name == "across 2":
            return e_buf.at[:PIECE]
        spots = [ref.at[:, n * width : (n + 1) * width] for ref in (kept_a.qkv, kept_b.qkv) for n in range(3)]
        spots += [kept_a.p, kept_a.xh2, kept_b.p, kept_b.xh2]
        if name == "across":
            return spots[place].at[ACROSS_FIRST]
        kind, up = name
        if kind == 1:
            return spots[3 + place if up else 7 + place].at[ACROSS_FIRST]
        if up:
            return spots[3 * rel + place - 1].at[LINE_FIRST]
        if rel:
            return dqkv_buf.at[:PIECE, col]
        return spots[6 + place].at[LINE_FIRST]

    sum_over_group(
        packed, result, landing, vector, flat_ref, vector_ref, group_send, group_recv, group_out, ready
    )


def output_kernel(
    flat,
    vector,
    act,
    grad,
    d_in,
    d_out,
    d_up,
    d_down,
    ag,
    ab,
    ob,
    fg,
    fb,
    d_up_bias,
    db,
    act_out,
    grad_out,
    low,
    wide,
    carried,
    low_sem,
    wide_sem,
    in_sem,
    out_sem,
):
    blocks, width, _ = low.shape

    def load(n):
        return pltpu.make_async_copy(flat.at[n * width : (n + 1) * width], low.at[n], low_sem.at[n])

    def target(n):
        if n < 3:
            return d_in.at[:, n * width : (n + 1) * width]
        if n == 3:
            return d_out
        if n < 8:
            return d_up.at[:, (n - 4) * width : (n - 3) * width]
        return d_down.at[(n - 8) * width : (n - 7) * width]

    def store(n):
        return pltpu.make_async_copy(wide.at[n], target(n), wide_sem.at[n])

    arrays = [(ref.at[n], out.at[n]) for ref, out in ((act, act_out), (grad, grad_out)) for n in range(act.shape[0])]

    def bring(n):
        return pltpu.make_async_copy(arrays[n][0], carried.at[n], in_sem.at[n])

    def take(n):
        return pltpu.make_async_copy(carried.at[n], arrays[n][1], out_sem.at[n])

    for n in range(blocks):
        load(n).start()
    for n in range(len(arrays)):
        bring(n).start()
    for row, out in enumerate((ag, ab, ob, fg, fb, db)):
        out[...] = vector[row : row + 1, :]
    for n in range(d_up_bias.shape[1] // width):
        d_up_bias[:, n * width : (n + 1) * width] = vector[6 + n : 7 + n, :]
    for n in range(blocks):
        load(n).wait()
        wide[n] = low[n].astype(F32)
        store(n).start()
    for n in range(len(arrays)):
        bring(n).wait()
        take(n).start()
    for n in range(blocks):
        store(n).wait()
    for n in range(len(arrays)):
        take(n).wait()


def per_device(
    clip_tokens,
    window_cols,
    time_groups,
    cotangent,
    attention_gain,
    attention_bias,
    projection_in,
    projection_out,
    output_bias,
    feedforward_gain,
    feedforward_bias,
    up_weight,
    up_bias,
    down_weight,
    down_bias,
):
    micro, _, frames, band, width = clip_tokens.shape
    hidden = up_weight.shape[2]
    window = band // WCAP
    rows = frames * window
    weights = (
        attention_gain,
        attention_bias,
        projection_in[0],
        projection_out[0],
        output_bias,
        feedforward_gain,
        feedforward_bias,
        up_weight[0],
        up_bias,
        down_weight[0],
        down_bias,
    )
    smem = pl.BlockSpec(memory_space=pltpu.SMEM)
    vmem = pl.BlockSpec(memory_space=pltpu.VMEM)
    hbm = pl.BlockSpec(memory_space=pl.ANY)
    tokens = jax.ShapeDtypeStruct((micro, frames, band, width), BF16)
    chunk = (frames, window, width)
    group_size = lax.axis_size("dp")
    grouped = group_size % GROUP == 0
    flat_shape = (GROUP * UNIT, width)
    kept_shapes = Kept(
        x=(chunk, BF16),
        a1t=((width, rows), BF16),
        qkv=((rows, 3 * width), BF16),
        p=((rows, width), BF16),
        ot=((width, rows), BF16),
        xh2=((rows, width), BF16),
        a2t=((width, rows), BF16),
        rs2=((rows, 128), F32),
        h=((rows, hidden), BF16),
        g=((rows, hidden), BF16),
    )
    results = pl.pallas_call(
        partial(relay_kernel, (micro, frames, window, width, hidden, grouped)),
        out_shape=(
            tokens,
            tokens,
            jax.ShapeDtypeStruct(flat_shape, BF16),
            jax.ShapeDtypeStruct((VECTOR_ROWS, width), F32),
        )
        + tuple(jax.ShapeDtypeStruct((SLOTS,) + shape, kind) for shape, kind in kept_shapes[1:]),
        in_specs=[smem, smem, hbm, hbm] + [vmem] * len(weights),
        out_specs=[hbm] * (3 + len(kept_shapes)),
        scratch_shapes=[
            pltpu.VMEM((LINE, UNIT, hidden), BF16),
            pltpu.VMEM((3 * width, width), BF16),
            pltpu.VMEM((width, width), BF16),
            pltpu.VMEM((hidden, width), BF16),
            pltpu.VMEM((width, hidden), BF16),
        ]
        + [pltpu.VMEM(*kept) for kept in kept_shapes[:-2] * 2]
        + [
            pltpu.VMEM((width, 3 * width), F32),
            pltpu.VMEM((width, width), F32),
            pltpu.VMEM((width, hidden), F32),
            pltpu.VMEM((width, hidden), F32),
            pltpu.VMEM((SLOTS,) + chunk, BF16),
            pltpu.VMEM((SLOTS,) + chunk, BF16),
            pltpu.VMEM((2,) + chunk, BF16),
            pltpu.VMEM((2,) + chunk, BF16),
            pltpu.VMEM((frames * frames // 2, HEADS, 128), F32),
            pltpu.VMEM((frames * frames // 2, HEADS, 128), F32),
            pltpu.VMEM((rows, width), F32),
            pltpu.VMEM((rows, width), F32),
            pltpu.VMEM((2, rows, FF_BLOCK), F32),
            pltpu.VMEM((rows, width), BF16),
            pltpu.VMEM((width, rows), BF16),
            pltpu.VMEM((rows, width), BF16),
            pltpu.VMEM((rows, width), BF16),
            pltpu.VMEM((rows, 3 * width), BF16),
            pltpu.VMEM((3 * width, rows), F32),
            pltpu.VMEM((3 * width, rows), BF16),
            pltpu.VMEM((8, width), F32),
            pltpu.VMEM((8, width), F32),
            pltpu.VMEM((8, width), F32),
            pltpu.VMEM((8, width), F32),
            pltpu.VMEM((8, width), F32),
            pltpu.VMEM((8, hidden), F32),
            pltpu.VMEM((8, width), F32),
            pltpu.SemaphoreType.DMA((SLOTS,)),
            pltpu.SemaphoreType.DMA((SLOTS,)),
            pltpu.SemaphoreType.DMA((2,)),
            pltpu.SemaphoreType.DMA((2,)),
            pltpu.SemaphoreType.DMA((2,)),
            pltpu.SemaphoreType.DMA((2,)),
            pltpu.VMEM((LINE, UNIT, hidden), BF16),
            pltpu.SemaphoreType.DMA((len(kept_shapes),)),
            pltpu.SemaphoreType.DMA((len(kept_shapes),)),
            pltpu.VMEM((4 + LINE, VECTOR_ROWS, width), F32),
            pltpu.SemaphoreType.DMA((FAMILIES * LINE,)),
            pltpu.SemaphoreType.DMA((FAMILIES * LINE,)),
            pltpu.SemaphoreType.DMA((2 * GROUP + 1,)),
            pltpu.SemaphoreType.REGULAR((4,)),
        ],
        compiler_params=pltpu.CompilerParams(
            collective_id=0, has_side_effects=True, vmem_limit_bytes=63 * 1024 * 1024
        ),
        name="relay",
    )(
        window_cols,
        time_groups,
        clip_tokens.reshape(micro, frames, band, width),
        cotangent.reshape(micro, frames, band, width),
        *weights,
    )
    activations, input_grads, flat, vector = results[:4]
    if group_size != GROUP:
        groups = None
        if grouped:
            groups = [[first + n for first in range(0, group_size, GROUP)] for n in range(GROUP)]
        flat, vector = lax.psum((flat, vector), "dp", axis_index_groups=groups)
    square = (width, width)
    row = jax.ShapeDtypeStruct((1, width), F32)
    blocks = GROUP * UNIT // width
    d_in, d_out, d_up, d_down, ag, ab, ob, fg, fb, d_up_bias, db, activations, input_grads = pl.pallas_call(
        output_kernel,
        in_specs=[hbm, vmem, hbm, hbm],
        out_specs=[hbm] * 4 + [vmem] * 7 + [hbm] * 2,
        out_shape=[
            jax.ShapeDtypeStruct((width, 3 * width), F32),
            jax.ShapeDtypeStruct(square, F32),
            jax.ShapeDtypeStruct((width, hidden), F32),
            jax.ShapeDtypeStruct((hidden, width), F32),
        ]
        + [row] * 5
        + [jax.ShapeDtypeStruct((1, hidden), F32), row, tokens, tokens],
        scratch_shapes=[
            pltpu.VMEM((blocks,) + square, BF16),
            pltpu.VMEM((blocks,) + square, F32),
            pltpu.VMEM((2 * micro, frames, band, width), BF16),
            pltpu.SemaphoreType.DMA((blocks,)),
            pltpu.SemaphoreType.DMA((blocks,)),
            pltpu.SemaphoreType.DMA((2 * micro,)),
            pltpu.SemaphoreType.DMA((2 * micro,)),
        ],
        compiler_params=pltpu.CompilerParams(vmem_limit_bytes=62 * 1024 * 1024),
        name="outputs",
    )(flat, vector, activations, input_grads)
    shape_out = (1, micro, 1, frames, band, width)
    return (
        activations.reshape(shape_out),
        input_grads.reshape(shape_out),
        ag,
        ab,
        d_in[None],
        d_out[None],
        ob,
        fg,
        fb,
        d_up[None],
        d_up_bias,
        d_down[None],
        db,
    )


def solution(mesh):
    wide, deep = P("section", None), P("section", None, None)
    tokens = P(None, "dp", None, None, None)
    weights = (wide, wide, deep, deep, wide, wide, wide, deep, wide, deep, wide)
    outputs = P("section", None, "dp", None, None, None)
    return jax.shard_map(
        per_device,
        mesh=mesh,
        in_specs=(tokens, P(None, "dp"), P(None, "dp", None), tokens) + weights,
        out_specs=(outputs, outputs) + weights,
        check_vma=False,
    )
```

```python
from collections import namedtuple
from functools import partial

import jax
import jax.numpy as jnp
from jax import lax
from jax.experimental import pallas as pl
from jax.experimental.pallas import tpu as pltpu
from jax.sharding import PartitionSpec as P

HEADS = 8
WCAP = 5
EPSILON = 1e-05
MASKED = -1e30
MESH = pl.DeviceIdType.MESH

F32 = jnp.float32
BF16 = jnp.bfloat16

LEAD = 4
SLOTS = LEAD + 1
Kept = namedtuple("Kept", ("x", "a1t", "qkv", "p", "ot", "xh2", "a2t", "rs2", "h", "g"))
FF_BLOCK = 512
ROWS_AT_ONCE = 32
COLS_AT_ONCE = 256

INV_SQRT2 = 0.7071067811865476
PDF = 0.3989422804014327
LOG2E = 1.4426950408889634


def mm(a, b):
    return lax.dot_general(a, b, (((1,), (0,)), ((), ())), preferred_element_type=F32)


def mm_bt(a, b):
    return lax.dot_general(a, b, (((1,), (1,)), ((), ())), preferred_element_type=F32)


def mm_at(a, b):
    return lax.dot_general(a, b, (((0,), (0,)), ((), ())), preferred_element_type=F32)


def gelu_and_slope(u):
    cdf = 0.5 + 0.5 * lax.erf(INV_SQRT2 * u)
    bell = jnp.exp2((-0.5 * LOG2E) * (u * u))
    return u * cdf, cdf + (PDF * u) * bell


def fold8(values):
    rows, cols = values.shape
    return jnp.sum(values.reshape(rows // 8, 8, cols), axis=0)


GROUP = 16
LINE = 4
LINE_ORDER = (3, 0, 2, 1)
UNIT = 384
PIECE = 128
WHOLE = slice(0, UNIT)
ACROSS_FIRST = slice(0, 256)
LINE_FIRST = slice(256, UNIT)
PART = {1: ACROSS_FIRST, 2: LINE_FIRST}
SIDES = {1: (0,), 2: (0, 1)}
FAMILIES = 32
VECTOR_ROWS = 16


def group_place():
    me = lax.axis_index("dp")
    core, across, line = lax.rem(me, 2), lax.rem(lax.div(me, 2), 2), lax.rem(lax.div(me, 4), LINE)
    sibling, beside = {"dp": me + 1 - 2 * core}, {"dp": me + 2 - 4 * across}
    return core, across, line, sibling, beside, {"dp": me + 4}, {"dp": me - 4}


def sum_over_group(pack, packed, result, landing, vector, flat_ref, vector_ref, send_sem, recv_sem, out_sem, ready):
    core, across, line, sibling, beside, above, below = group_place()
    sides = (across, 1 - across)
    families = {}
    pending = []

    def when(condition, action):
        if condition is None:
            action()
        else:
            pl.when(condition)(action)

    def remote(family, place, source, target, device):
        number = families.setdefault(family, len(families)) * LINE + place
        return pltpu.make_async_remote_copy(
            src_ref=source,
            dst_ref=target,
            send_sem=send_sem.at[number],
            recv_sem=recv_sem.at[number],
            device_id=device,
            device_id_type=MESH,
        )

    def start(family, place, source, target, device):
        remote(family, place, source, target, device).start()

    def sent(family, place, source, device, condition=None):
        pending.append((condition, lambda: remote(family, place, source, source, device).wait_send()))

    def received(family, place, target, device):
        remote(family, place, target, target, device).wait_recv()

    def unit(ref, half, side, place, part):
        column = place * 512 if isinstance(place, int) else pl.multiple_of(place * 512, 512)
        return ref.at[half * 2 + side, part, pl.ds(column, 512)]

    def add(target, arrived):
        for r in range(0, target.shape[0], 64):
            at = slice(r, r + 64)
            target[at] = (target[at].astype(F32) + arrived[at].astype(F32)).astype(BF16)

    def store(far, rel, place, kind):
        half, side, part = (1 - core if far else core), sides[rel], PART[kind]
        row = pl.multiple_of(((half * 2 + side) * LINE + place) * UNIT + part.start, PIECE)
        return pltpu.make_async_copy(
            unit(result, half, side, place, part),
            flat_ref.at[pl.ds(row, part.stop - part.start)],
            out_sem.at[((far * 2 + rel) * 2 + kind - 1) * LINE + place],
        )

    for number, (device, condition) in enumerate(
        ((sibling, None), (beside, None), (below, line > 0), (above, line < LINE - 1))
    ):
        there = number if number < 2 else 5 - number
        when(
            condition,
            partial(pl.semaphore_signal, ready.at[there], inc=1, device_id=device, device_id_type=MESH),
        )
    for half in range(2):
        pl.when(core == half)(partial(pack, 1 - half))
    pl.semaphore_wait(ready.at[0], 1)

    start("vector core", 0, vector.at[0], vector.at[1], sibling)
    sent("vector core", 0, vector.at[0], sibling)
    for place in LINE_ORDER:
        for side in range(2):
            source = unit(packed, 1 - core, side, place, WHOLE)
            start(("core", side), place, source, landing("core", side, place), sibling)
            sent(("core", side), place, source, sibling)
    for half in range(2):
        pl.when(core == half)(partial(pack, half))
    pl.semaphore_wait(ready.at[1], 1)
    pl.when(line > 0)(lambda: pl.semaphore_wait(ready.at[2], 1))
    pl.when(line < LINE - 1)(lambda: pl.semaphore_wait(ready.at[3], 1))

    def line_send(kind, place, up, condition):
        device = above if up else below

        def go():
            for rel in SIDES[kind]:
                source = unit(packed, core, sides[rel], place, PART[kind])
                start((kind, up, rel), place, source, landing((kind, up), rel, place), device)

        pl.when(condition)(go)
        for rel in SIDES[kind]:
            sent((kind, up, rel), place, unit(packed, core, sides[rel], place, PART[kind]), device, condition)

    def line_take(kind, place, up, condition):
        def go():
            for rel in SIDES[kind]:
                spot = landing((kind, up), rel, place)
                received((kind, up, rel), place, spot, below if up else above)
                add(unit(packed, core, sides[rel], place, PART[kind]), spot)

        pl.when(condition)(go)

    def from_ends(kind, place):
        if place > 0:
            line_send(kind, place, True, line == 0)
        if place < LINE - 1:
            line_send(kind, place, False, line == LINE - 1)

    def inner_step(kind, k):
        place = LINE - 1 - k
        line_take(kind, place, True, (line > 0) & (line <= place))
        if place > 1:
            line_send(kind, place, True, (line > 0) & (line < place))
        place = k
        line_take(kind, place, False, (line < LINE - 1) & (line >= place))
        if place < LINE - 2:
            line_send(kind, place, False, (line < LINE - 1) & (line > place))

    def take_across(place):
        spot = landing("across", 0, place)
        received("across", place, spot, beside)
        add(unit(packed, core, sides[0], place, ACROSS_FIRST), spot)
        from_ends(1, place)

    for place in LINE_ORDER:
        for side in range(2):
            spot = landing("core", side, place)
            received(("core", side), place, spot, sibling)
            add(unit(packed, core, side, place, WHOLE), spot)
        source = unit(packed, core, sides[1], place, ACROSS_FIRST)
        start("across", place, source, landing("across", 0, place), beside)
        sent("across", place, source, beside)
        from_ends(2, place)
    received("vector core", 0, vector.at[1], sibling)
    vector[2] = vector[0] + vector[1]
    start("vector across", 0, vector.at[2], vector.at[3], beside)
    sent("vector across", 0, vector.at[2], beside)
    for k in range(LINE - 1):
        take_across(LINE_ORDER[k])
        inner_step(2, k)
    take_across(LINE_ORDER[LINE - 1])
    source = unit(packed, core, sides[1], line, LINE_FIRST)
    start("across 2", 0, source, landing("across 2", 0, 0), beside)
    sent("across 2", 0, source, beside)
    received("vector across", 0, vector.at[3], beside)
    vector[4 + line] = vector[2] + vector[3]
    inner_step(1, 0)
    inner_step(1, 1)
    spot = landing("across 2", 0, 0)
    received("across 2", 0, spot, beside)
    own = unit(packed, core, sides[0], line, LINE_FIRST)
    add(own, spot)
    own_two = unit(result, core, sides[0], line, LINE_FIRST)
    own_two[...] = own[...]
    start("gather across 2", 0, own_two, own_two, beside)
    sent("gather across 2", 0, own_two, beside)
    inner_step(1, 2)
    own_one = unit(result, core, sides[0], line, ACROSS_FIRST)
    own_one[...] = unit(packed, core, sides[0], line, ACROSS_FIRST)[...]

    def spread(family, place, spot, up, down):
        if up is not None:
            pl.when(up)(lambda: start((family, True), place, spot, spot, above))
        if down is not None:
            pl.when(down)(lambda: start((family, False), place, spot, spot, below))

    def hand_over(kind, rel, place):
        spot = unit(result, core, sides[rel], place, PART[kind])
        start(("gather core", kind, rel), place, spot, spot, sibling)
        store(0, rel, place, kind).start()

    def have(kind, rel, place, up, down):
        spot = unit(result, core, sides[rel], place, PART[kind])
        spread(("spread", kind, rel), place, spot, up, down)
        if kind == 1:
            start("gather across", place, spot, spot, beside)
        hand_over(kind, rel, place)

    def come(distance, action):
        pl.when(line >= distance)(lambda: action(line - distance, True))
        pl.when(line + distance < LINE)(lambda: action(line + distance, False))

    def arrive(kind, rel, distance):
        def action(place, up):
            spot = unit(result, core, sides[rel], place, PART[kind])
            received((("spread", kind, rel), up), place, spot, below if up else above)
            have(kind, rel, place, line < LINE - 1 if up else None, None if up else line > 0)

        come(distance, action)

    def arrive_vector(distance):
        def action(place, up):
            spot = vector.at[4 + place]
            received(("vector", up), place, spot, below if up else above)
            spread("vector", place, spot, line < LINE - 1 if up else None, None if up else line > 0)

        come(distance, action)

    def arrive_across(distance):
        def action(place, up):
            received("gather across", place, unit(result, core, sides[1], place, ACROSS_FIRST), beside)
            hand_over(1, 1, place)

        if distance == 0:
            action(line, True)
        else:
            come(distance, action)

    have(1, 0, line, line < LINE - 1, line > 0)
    have(2, 0, line, line < LINE - 1, line > 0)
    spread("vector", line, vector.at[4 + line], line < LINE - 1, line > 0)
    received("gather across 2", 0, unit(result, core, sides[1], line, LINE_FIRST), beside)
    have(2, 1, line, line < LINE - 1, line > 0)
    for distance in range(1, LINE):
        arrive(1, 0, distance)
        arrive(2, 0, distance)
        arrive(2, 1, distance)
        arrive_vector(distance)
        arrive_across(distance - 1)
    arrive_across(LINE - 1)
    vector[1] = (vector[4] + vector[5]) + (vector[6] + vector[7])
    vector_out = pltpu.make_async_copy(vector.at[1], vector_ref, out_sem.at[2 * GROUP])
    vector_out.start()
    for place in range(LINE):
        for kind in (1, 2):
            for rel in range(2):
                spot = unit(result, 1 - core, sides[rel], place, PART[kind])
                received(("gather core", kind, rel), place, spot, sibling)
                store(1, rel, place, kind).start()
    vector_out.wait()

    for place in range(LINE):
        for kind in (1, 2):
            for rel in range(2):
                spot = unit(result, core, sides[rel], place, PART[kind])
                sent(("gather core", kind, rel), place, spot, sibling)
                store(0, rel, place, kind).wait()
                store(1, rel, place, kind).wait()
            for rel in SIDES[kind]:
                spot = unit(result, core, sides[rel], place, PART[kind])
                sent((("spread", kind, rel), True), place, spot, above, (line >= place) & (line < LINE - 1))
                sent((("spread", kind, rel), False), place, spot, below, (line <= place) & (line > 0))
        sent("gather across", place, unit(result, core, sides[0], place, ACROSS_FIRST), beside)
        sent(("vector", True), place, vector.at[4 + place], above, (line >= place) & (line < LINE - 1))
        sent(("vector", False), place, vector.at[4 + place], below, (line <= place) & (line > 0))
    for condition, wait in pending:
        when(condition, wait)


def relay_kernel(
    dims,
    cols_ref,
    groups_ref,
    clip_ref,
    cot_ref,
    attention_gain,
    attention_bias,
    projection_in_ref,
    projection_out_ref,
    output_bias,
    feedforward_gain,
    feedforward_bias,
    up_weight_ref,
    up_bias,
    down_weight_ref,
    down_bias,
    act_ref,
    grad_ref,
    flat_ref,
    vector_ref,
    *scratch,
):
    micro, frames, window, width, hidden, grouped = dims
    parked, scratch = scratch[: len(Kept._fields) - 1], scratch[len(Kept._fields) - 1 :]
    kept_a, scratch = Kept(*scratch[: len(Kept._fields)]), scratch[len(Kept._fields) :]
    kept_b, scratch = Kept(*scratch[: len(Kept._fields)]), scratch[len(Kept._fields) :]
    (
    d_projection_in,
    d_projection_out,
    d_up_weight,
    d_down_weight,
    xbuf,
    dybuf,
    ybuf,
    dxbuf,
    a1_buf,
    pf_buf,
    ds_buf,
    o_buf,
    a2_buf,
    wide,
    total,
    u_buf,
    e_buf,
    et_buf,
    c_buf,
    do_buf,
    dqkv_buf,
    qkvt_buf,
    dot_buf,
    dqkvt_buf,
    sum_ag,
    sum_ab,
    sum_ob,
    sum_fg,
    sum_fb,
    sum_ub,
    sum_db,
    x_sem,
    dy_sem,
    y_sem,
    y_send,
    dx_sem,
    dx_send,
    packed,
    result,
    projection_in,
    projection_out,
    up_weight,
    down_weight,
    weight_sem,
    park_sem,
    fetch_sem,
    vector,
    group_send,
    group_recv,
    group_out,
    ready,
    ) = scratch
    rows = frames * window
    count = micro * WCAP
    head = width // HEADS
    pair = 2 * head
    scale = head ** (-0.5)
    section = lax.axis_index("section")
    leading = section == 0
    trailing = section != 0
    lead = LEAD * (1 - section)
    partner = {"section": 1 - section}

    def hbm_chunk(ref, chunk):
        start = pl.multiple_of(lax.rem(chunk, WCAP) * window, window)
        return ref.at[lax.div(chunk, WCAP), :, pl.ds(start, window), :]

    def x_load(chunk):
        slot = lax.rem(chunk, SLOTS)
        return pltpu.make_async_copy(hbm_chunk(clip_ref, chunk), xbuf.at[slot], x_sem.at[slot])

    def dy_load(chunk):
        slot = lax.rem(chunk, SLOTS)
        return pltpu.make_async_copy(hbm_chunk(cot_ref, chunk), dybuf.at[slot], dy_sem.at[slot])

    def y_store(chunk):
        slot = lax.rem(chunk, 2)
        return pltpu.make_async_copy(ybuf.at[slot], hbm_chunk(act_ref, chunk), y_sem.at[slot])

    def dx_store(chunk):
        slot = lax.rem(chunk, 2)
        return pltpu.make_async_copy(dxbuf.at[slot], hbm_chunk(grad_ref, chunk), dx_sem.at[slot])

    def park(chunk):
        slot = lax.rem(chunk, SLOTS)
        return [
            pltpu.make_async_copy(here, there.at[slot], park_sem.at[n])
            for n, (here, there) in enumerate(zip(kept_a[1:], parked))
        ]

    def fetch(chunk):
        slot = lax.rem(chunk, SLOTS)
        return [pltpu.make_async_copy(hbm_chunk(clip_ref, chunk), kept_b.x, fetch_sem.at[0])] + [
            pltpu.make_async_copy(there.at[slot], here, fetch_sem.at[n + 1])
            for n, (here, there) in enumerate(zip(kept_b[1:], parked))
        ]

    def start_all(copies):
        for copy in copies:
            copy.start()

    def wait_all(copies):
        for copy in copies:
            copy.wait()

    def y_remote(chunk):
        slot, there = lax.rem(chunk, 2), lax.rem(chunk, SLOTS)
        return pltpu.make_async_remote_copy(
            src_ref=ybuf.at[slot],
            dst_ref=xbuf.at[there],
            send_sem=y_send.at[slot],
            recv_sem=x_sem.at[there],
            device_id=partner,
            device_id_type=MESH,
        )

    def dx_remote(chunk):
        slot, there = lax.rem(chunk, 2), lax.rem(chunk, SLOTS)
        return pltpu.make_async_remote_copy(
            src_ref=dxbuf.at[slot],
            dst_ref=dybuf.at[there],
            send_sem=dx_send.at[slot],
            recv_sem=dy_sem.at[there],
            device_id=partner,
            device_id_type=MESH,
        )

    weight_loads = [
        pltpu.make_async_copy(source, target, weight_sem.at[n])
        for n, (source, target) in enumerate(
            (
                (projection_in_ref, projection_in),
                (projection_out_ref, projection_out),
                (up_weight_ref, up_weight),
                (down_weight_ref, down_weight),
            )
        )
    ]
    for load in weight_loads:
        load.start()
    barrier = pltpu.get_barrier_semaphore()
    greeted = 1
    pl.semaphore_signal(barrier, inc=1, device_id=partner, device_id_type=MESH)
    if grouped:
        _, _, line, sibling, beside, above, below = group_place()
        has_below, has_above = line > 0, line < LINE - 1
        for device, condition in ((sibling, None), (beside, None), (below, has_below), (above, has_above)):
            greet = partial(pl.semaphore_signal, barrier, inc=1, device_id=device, device_id_type=MESH)
            if condition is None:
                greet()
            else:
                pl.when(condition)(greet)
        greeted = 3 + has_below.astype(jnp.int32) + has_above.astype(jnp.int32)

    @pl.when(leading)
    def _():
        x_load(0).start()

    @pl.when(trailing)
    def _():
        dy_load(0).start()

    for total_ref in (d_projection_in, d_projection_out, d_up_weight, d_down_weight):
        total_ref[...] = jnp.zeros_like(total_ref)
    for total_ref in (sum_ag, sum_ab, sum_ob, sum_fg, sum_fb, sum_ub, sum_db):
        total_ref[...] = jnp.zeros_like(total_ref)

    for load in weight_loads:
        load.wait()
    pl.semaphore_wait(barrier, greeted)

    def frame_rows(i):
        return slice(i * window, (i + 1) * window)

    half = lax.broadcasted_iota(jnp.int32, (window, pair), 1) < head
    low_half = jnp.where(half, 1.0, 0.0).astype(BF16)
    high_half = jnp.where(half, 0.0, 1.0).astype(BF16)

    def by_head(values):
        return jnp.concatenate([values * low_half, values * high_half], axis=0)

    def join_heads(values):
        return jnp.where(half, values[:window], values[window:])

    heads_of = [
        (frame_rows(f), slice(n * pair, (n + 1) * pair), n) for f in range(frames) for n in range(width // pair)
    ]

    def of_pair(ref, at, which, n):
        return ref[at, which * width + n * pair : which * width + (n + 1) * pair]

    def window_forward(kept):
        for at, lanes, n in heads_of:
            keys = of_pair(kept.qkv, at, 1, n)
            total[at, lanes] = mm_bt(keys, by_head(of_pair(kept.qkv, at, 0, n)))
        yield
        for at, lanes, n in heads_of:
            scores = total[at, lanes] * scale
            scores = jnp.exp(scores - jnp.max(scores, axis=0, keepdims=True))
            probs = scores * (1.0 / jnp.sum(scores, axis=0, keepdims=True))
            kept.p[at, lanes] = probs.astype(BF16)
        yield
        for at, lanes, n in heads_of:
            values = of_pair(kept.qkv, at, 2, n)
            o_buf[at, lanes] = join_heads(mm_at(kept.p[at, lanes], values)).astype(BF16)

    def window_backward(kept):
        for at, lanes, n in heads_of:
            up = by_head(do_buf[at, lanes])
            total[at, lanes] = mm_bt(of_pair(kept.qkv, at, 2, n), up)
            dv = mm(kept.p[at, lanes], up)
            dqkv_buf[at, 2 * width + n * pair : 2 * width + (n + 1) * pair] = dv.astype(BF16)
        yield
        for at, lanes, n in heads_of:
            probs = kept.p[at, lanes].astype(F32)
            dp = total[at, lanes]
            ds = probs * (dp - jnp.sum(probs * dp, axis=0, keepdims=True))
            e_buf[at, lanes] = ds.astype(BF16)
        yield
        for at, lanes, n in heads_of:
            ds = e_buf[at, lanes]
            dk = mm(ds, by_head(of_pair(kept.qkv, at, 0, n))) * scale
            dqkv_buf[at, width + n * pair : width + (n + 1) * pair] = dk.astype(BF16)
            dq = join_heads(mm_at(ds, of_pair(kept.qkv, at, 1, n))) * scale
            dqkv_buf[at, lanes] = dq.astype(BF16)

    low_frame = lax.broadcasted_iota(jnp.int32, (1, 128), 1) < window

    def lane_tiles(i):
        return min(i + 1, frames - 1) // 2 + 1

    def tile(t):
        return slice(t * 128, (t + 1) * 128)

    def head_rows(which, h):
        return slice(which * width + h * head, which * width + (h + 1) * head)

    def other_half(values):
        return pltpu.roll(values, window, axis=1)

    def both_frames(ref, at, t):
        values = ref[at, tile(t)]
        turned = other_half(values)
        return jnp.where(low_frame, values, turned), jnp.where(low_frame, turned, values)

    def frame_forward(chunk, kept):
        tile_count = frames // 2
        for n in range(3):
            flat = kept.qkv[:, n * width : (n + 1) * width].T
            qkvt_buf[n * width : (n + 1) * width, :] = flat.astype(F32)
        for h in range(HEADS):
            keys = [qkvt_buf[head_rows(1, h), tile(t)] for t in range(tile_count)]
            for pair_index in range(tile_count):
                queries = both_frames(qkvt_buf, head_rows(0, h), pair_index)
                for i in (2 * pair_index, 2 * pair_index + 1):
                    for t in range(lane_tiles(i)):
                        score = jnp.sum(queries[i % 2] * keys[t], axis=0, keepdims=True)
                        ds_buf[i * tile_count + t, h : h + 1, :] = score
        yield
        item = lax.div(chunk, WCAP)
        labels = [
            jnp.where(low_frame, groups_ref[item, 0, 2 * t], groups_ref[item, 0, 2 * t + 1])
            for t in range(tile_count)
        ]
        for i in range(frames):
            mine = groups_ref[item, 0, i]
            parts = [
                jnp.where(labels[t] <= mine, ds_buf[i * tile_count + t] * scale, MASKED)
                for t in range(lane_tiles(i))
            ]
            largest = parts[0]
            for part in parts[1:]:
                largest = jnp.maximum(largest, part)
            largest = jnp.maximum(largest, other_half(largest))
            parts = [jnp.exp(part - largest) for part in parts]
            whole = parts[0]
            for part in parts[1:]:
                whole = whole + part
            whole = 1.0 / (whole + other_half(whole))
            for t, part in enumerate(parts):
                pf_buf[i * tile_count + t] = part * whole
        yield
        for h in range(HEADS):
            values = [qkvt_buf[head_rows(2, h), tile(t)] for t in range(tile_count)]
            for pair_index in range(tile_count):
                mixed = []
                for i in (2 * pair_index, 2 * pair_index + 1):
                    part = 0.0
                    for t in range(lane_tiles(i)):
                        part = part + pf_buf[i * tile_count + t, h : h + 1, :] * values[t]
                    mixed.append(part + other_half(part))
                both = jnp.where(low_frame, mixed[0], mixed[1])
                kept.ot[head_rows(0, h), tile(pair_index)] = both.astype(BF16)

    def frame_backward(kept, beside):
        tile_count = frames // 2
        for h in range(HEADS):
            beside()
            values = [qkvt_buf[head_rows(2, h), tile(t)] for t in range(tile_count)]
            dv = [0.0] * tile_count
            for pair_index in range(tile_count):
                ups = both_frames(dot_buf, head_rows(0, h), pair_index)
                for i in (2 * pair_index, 2 * pair_index + 1):
                    for t in range(lane_tiles(i)):
                        ds_buf[i * tile_count + t, h : h + 1, :] = jnp.sum(
                            ups[i % 2] * values[t], axis=0, keepdims=True
                        )
                        dv[t] = dv[t] + pf_buf[i * tile_count + t, h : h + 1, :] * ups[i % 2]
            for t in range(tile_count):
                dqkvt_buf[head_rows(2, h), tile(t)] = dv[t].astype(BF16)
        for i in range(frames):
            spots = [i * tile_count + t for t in range(lane_tiles(i))]
            along = pf_buf[spots[0]] * ds_buf[spots[0]]
            for spot in spots[1:]:
                along = along + pf_buf[spot] * ds_buf[spot]
            along = along + other_half(along)
            for spot in spots:
                ds_buf[spot] = pf_buf[spot] * (ds_buf[spot] - along) * scale
        for h in range(HEADS):
            beside()
            keys = [qkvt_buf[head_rows(1, h), tile(t)] for t in range(tile_count)]
            dk = [0.0] * tile_count
            for pair_index in range(tile_count):
                queries = both_frames(qkvt_buf, head_rows(0, h), pair_index)
                dq = []
                for i in (2 * pair_index, 2 * pair_index + 1):
                    part = 0.0
                    for t in range(lane_tiles(i)):
                        ds = ds_buf[i * tile_count + t, h : h + 1, :]
                        part = part + ds * keys[t]
                        dk[t] = dk[t] + ds * queries[i % 2]
                    dq.append(part + other_half(part))
                both = jnp.where(low_frame, dq[0], dq[1])
                dqkvt_buf[head_rows(0, h), tile(pair_index)] = both.astype(BF16)
            for t in range(tile_count):
                dqkvt_buf[head_rows(1, h), tile(t)] = dk[t].astype(BF16)
        for n in range(3):
            dqkv_buf[:, n * width : (n + 1) * width] = dqkvt_buf[n * width : (n + 1) * width, :].T

    def live_of(chunk):
        cols = cols_ref[0, lax.div(chunk, WCAP)]
        return jnp.where(lax.rem(chunk, WCAP) < cols, 1.0, 0.0).astype(F32)

    def standardize(values):
        centered = values - jnp.mean(values, axis=-1, keepdims=True)
        rstd = lax.rsqrt(jnp.mean(centered * centered, axis=-1, keepdims=True) + EPSILON)
        return centered * rstd, rstd

    blocks = [
        (slice(r, r + ROWS_AT_ONCE), r // window, slice(r % window, r % window + ROWS_AT_ONCE))
        for r in range(0, rows, ROWS_AT_ONCE)
    ]
    ff_parts = [slice(c, c + FF_BLOCK) for c in range(0, hidden, FF_BLOCK)]

    def halves(cols, start=0, step=COLS_AT_ONCE):
        return [slice(c, c + step) for c in range(start, start + cols, step)]

    def forward(spatial, chunk, kept, slot, y_slot):
        kept.x[...] = xbuf[slot]
        for at, f, within in blocks:
            unit, _ = standardize(kept.x[f, within].astype(F32))
            a1_buf[at, :] = (unit * attention_gain[...] + attention_bias[...]).astype(BF16)
        yield
        kept.a1t[...] = a1_buf[...].T
        for part in halves(3 * width, step=width):
            kept.qkv[:, part] = mm(a1_buf[...], projection_in[:, part]).astype(BF16)
        yield
        if spatial:
            yield from window_forward(kept)
            yield
            kept.ot[...] = o_buf[...].T
        else:
            yield from frame_forward(chunk, kept)
            yield
            o_buf[...] = kept.ot[...].T
        wide[...] = mm(o_buf[...], projection_out[...])
        yield
        for at, f, within in blocks:
            middle = kept.x[f, within].astype(F32) + (wide[at, :] + output_bias[...])
            wide[at, :] = middle + down_bias[...]
            unit, rstd = standardize(middle)
            kept.xh2[at, :] = unit.astype(BF16)
            kept.rs2[at, :] = jnp.broadcast_to(rstd, (ROWS_AT_ONCE, 128))
            a2_buf[at, :] = (unit * feedforward_gain[...] + feedforward_bias[...]).astype(BF16)
        yield
        kept.a2t[...] = a2_buf[...].T
        u_buf[0] = mm(a2_buf[...], up_weight[:, ff_parts[0]])
        yield
        for n, part in enumerate(ff_parts):
            if n + 1 < len(ff_parts):
                u_buf[(n + 1) % 2] = mm(a2_buf[...], up_weight[:, ff_parts[n + 1]])
            for at, _, _ in blocks:
                for inner, outer in zip(halves(FF_BLOCK), halves(FF_BLOCK, part.start)):
                    h, slope = gelu_and_slope(u_buf[n % 2, at, inner] + up_bias[:, outer])
                    kept.h[at, outer] = h.astype(BF16)
                    kept.g[at, outer] = slope.astype(BF16)
            yield
        total[...] = mm(kept.h[...], down_weight[...])
        yield
        live = live_of(chunk)
        for at, f, within in blocks:
            ybuf[y_slot, f, within] = ((wide[at, :] + total[at, :]) * live).astype(BF16)
        y_store(chunk).start()
        if spatial:
            y_remote(chunk).start()

    def norm_backward(d_normed, unit, rstd, gain):
        d_unit = d_normed * gain
        along = jnp.mean(d_unit * unit, axis=-1, keepdims=True)
        return rstd * (d_unit - jnp.mean(d_unit, axis=-1, keepdims=True) - unit * along)

    def weight_gradient(total_ref, left, right, cols):
        for part in cols:
            total_ref[:, part] += mm(left[...], right[:, part])

    def backward(spatial, chunk, kept, slot, dx_slot):
        if spatial:
            dx_remote(chunk).wait_recv()
        else:
            dy_load(chunk).wait()

        @pl.when(chunk >= 2)
        def _():
            dx_store(chunk - 2).wait()
            if not spatial:
                dx_remote(chunk - 2).wait_send()

        live = live_of(chunk)
        e_buf[...] = (dybuf[slot].reshape(rows, width).astype(F32) * live).astype(BF16)
        for at, f, within in blocks:
            sum_db[...] += fold8(e_buf[at, :].astype(F32))
        yield
        et_buf[...] = e_buf[...].T
        u_buf[0] = mm_bt(e_buf[...], down_weight[ff_parts[0], :])
        yield
        for n, part in enumerate(ff_parts):
            if n + 1 < len(ff_parts):
                u_buf[(n + 1) % 2] = mm_bt(e_buf[...], down_weight[ff_parts[n + 1], :])
            if spatial:
                weight_gradient(d_down_weight, et_buf, kept.h, halves(FF_BLOCK, part.start))
            for at, _, _ in blocks:
                for inner, outer in zip(halves(FF_BLOCK), halves(FF_BLOCK, part.start)):
                    du = u_buf[n % 2, at, inner] * kept.g[at, outer].astype(F32)
                    sum_ub[:, outer] += fold8(du)
                    kept.g[at, outer] = du.astype(BF16)
            yield
        total[...] = mm_bt(kept.g[...], up_weight[...])
        yield
        for n, (at, _, _) in enumerate(blocks):
            if n % 3 == 0:
                grown = (d_up_weight, kept.a2t, kept.g) if spatial else (d_down_weight, et_buf, kept.h)
                weight_gradient(*grown, halves(FF_BLOCK, n // 3 * FF_BLOCK))
            d_normed = total[at, :]
            unit = kept.xh2[at, :].astype(F32)
            sum_fg[...] += fold8(d_normed * unit)
            sum_fb[...] += fold8(d_normed)
            rstd = kept.rs2[at, 0:1]
            d_middle = e_buf[at, :].astype(F32) + norm_backward(d_normed, unit, rstd, feedforward_gain[...])
            wide[at, :] = d_middle
            sum_ob[...] += fold8(d_middle)
            c_buf[at, :] = d_middle.astype(BF16)
        yield
        if spatial:
            do_buf[...] = mm_bt(c_buf[...], projection_out[...]).astype(BF16)
        else:
            dot_buf[...] = mm_bt(projection_out[...], c_buf[...])
        if spatial:
            weight_gradient(d_projection_out, kept.ot, c_buf, halves(width))
            yield from window_backward(kept)
        else:
            waiting = [(d_up_weight, kept.a2t, kept.g, [part]) for part in halves(hidden)]
            waiting += [(d_projection_out, kept.ot, c_buf, [part]) for part in halves(width)]

            def beside():
                if waiting:
                    weight_gradient(*waiting.pop(0))

            frame_backward(kept, beside)
        total[...] = mm_bt(dqkv_buf[...], projection_in[...])
        yield
        for n, (at, f, within) in enumerate(blocks):
            if n % 2 == 0:
                weight_gradient(d_projection_in, kept.a1t, dqkv_buf, halves(COLS_AT_ONCE, n // 2 * COLS_AT_ONCE))
            d_normed = total[at, :]
            unit, rstd = standardize(kept.x[f, within].astype(F32))
            sum_ag[...] += fold8(d_normed * unit)
            sum_ab[...] += fold8(d_normed)
            dx = wide[at, :] + norm_backward(d_normed, unit, rstd, attention_gain[...])
            do_buf[at, :] = dx.astype(BF16)
        yield
        dxbuf[dx_slot] = do_buf[...].reshape(frames, window, width)
        dx_store(chunk).start()
        if not spatial:
            dx_remote(chunk).start()

    def emit(pieces):
        for _ in pieces:
            pass

    def step(t, carry):
        chunk = t - lead
        ahead = (t, kept_a, lax.rem(t, SLOTS), lax.rem(t, 2))
        behind = (chunk, lax.rem(chunk + SLOTS, SLOTS), lax.rem(chunk + 2, 2))

        @pl.when(t < count)
        def _():
            @pl.when(leading)
            def _():
                x_load(t).wait()

                @pl.when(t + 1 < count)
                def _():
                    x_load(t + 1).start()

            @pl.when(trailing)
            def _():
                y_remote(t).wait_recv()

                @pl.when(t + 1 < count)
                def _():
                    dy_load(t + 1).start()

            @pl.when(t >= 2)
            def _():
                y_store(t - 2).wait()

                @pl.when(leading)
                def _():
                    y_remote(t - 2).wait_send()

        @pl.when(leading & (t > 0) & (t <= count))
        def _():
            wait_all(park(t - 1))

        @pl.when(leading & (t == 1))
        def _():
            start_all(fetch(0))

        @pl.when(leading & (t < count))
        def _():
            emit(forward(True, *ahead))
            start_all(park(t))

        @pl.when(leading & (chunk >= 0))
        def _():
            wait_all(fetch(chunk))
            emit(backward(True, chunk, kept_b, *behind[1:]))

            @pl.when(chunk + 1 < count)
            def _():
                start_all(fetch(chunk + 1))

        @pl.when(trailing & (t < count))
        def _():
            emit(forward(False, *ahead))
            emit(backward(False, chunk, kept_a, *behind[1:]))

        return carry

    lax.fori_loop(0, count + LEAD, step, 0)

    vector[0] = jnp.zeros_like(vector[0])
    for row, partial_sum in enumerate((sum_ag, sum_ab, sum_ob, sum_fg, sum_fb, sum_db)):
        vector[0, row : row + 1, :] = jnp.sum(partial_sum[...], axis=0, keepdims=True)
    for n in range(hidden // width):
        up_sum = jnp.sum(sum_ub[:, n * width : (n + 1) * width], axis=0, keepdims=True)
        vector[0, 6 + n : 7 + n, :] = up_sum

    def block_piece(number):
        block, r = divmod(number, width // PIECE)
        at = slice(r * PIECE, (r + 1) * PIECE)
        if block < 3:
            return d_projection_in[at, block * width : (block + 1) * width].astype(BF16)
        if block < 4:
            return d_projection_out[at, :].astype(BF16)
        if block < 8:
            return d_up_weight[at, (block - 4) * width : (block - 3) * width].astype(BF16)
        start = (block - 8) * width + r * PIECE
        return d_down_weight[:, start : start + PIECE].astype(BF16).T

    def pack(half):
        count_half = GROUP * UNIT // PIECE // 2
        for number in range(half * count_half, (half + 1) * count_half):
            u, r = divmod(number, UNIT // PIECE)
            at = slice(r * PIECE, (r + 1) * PIECE)
            packed[u // LINE, at, u % LINE * width : (u % LINE + 1) * width] = block_piece(number)

    def finish():
        for last in (count - 2, count - 1):
            y_store(last).wait()
            dx_store(last).wait()

            @pl.when(leading)
            def _():
                y_remote(last).wait_send()

            @pl.when(trailing)
            def _():
                dx_remote(last).wait_send()

    if not grouped:
        pack(0)
        pack(1)
        finish()
        for u in range(GROUP):
            cols = slice(u % LINE * width, (u % LINE + 1) * width)
            pltpu.sync_copy(packed.at[u // LINE, :, cols], flat_ref.at[u * UNIT : (u + 1) * UNIT])
        pltpu.sync_copy(vector.at[0], vector_ref)
        return

    def landing(name, rel, place):
        col = slice(place * width, (place + 1) * width)
        if name == "core":
            return (kept_a.g if rel else kept_a.h).at[:, col]
        if name == "across":
            return kept_b.h.at[ACROSS_FIRST, col]
        if name == "across 2":
            return e_buf.at[:PIECE]
        kind, up = name
        if kind == 1:
            return (kept_b.g if up else kept_a.qkv).at[ACROSS_FIRST, col]
        if up:
            return (kept_b.g if rel else kept_b.h).at[LINE_FIRST, col]
        if rel:
            return dqkv_buf.at[:PIECE, col]
        return kept_a.qkv.at[LINE_FIRST, col]

    sum_over_group(
        pack, packed, result, landing, vector, flat_ref, vector_ref, group_send, group_recv, group_out, ready
    )
    finish()


def output_kernel(
    flat,
    vector,
    act,
    grad,
    d_in,
    d_out,
    d_up,
    d_down,
    ag,
    ab,
    ob,
    fg,
    fb,
    d_up_bias,
    db,
    act_out,
    grad_out,
    low,
    wide,
    carried,
    low_sem,
    wide_sem,
    in_sem,
    out_sem,
):
    blocks, width, _ = low.shape

    def load(n):
        return pltpu.make_async_copy(flat.at[n * width : (n + 1) * width], low.at[n], low_sem.at[n])

    def target(n):
        if n < 3:
            return d_in.at[:, n * width : (n + 1) * width]
        if n == 3:
            return d_out
        if n < 8:
            return d_up.at[:, (n - 4) * width : (n - 3) * width]
        return d_down.at[(n - 8) * width : (n - 7) * width]

    def store(n):
        return pltpu.make_async_copy(wide.at[n], target(n), wide_sem.at[n])

    arrays = [
        (ref.at[n, f], out.at[n, f])
        for ref, out in ((act, act_out), (grad, grad_out))
        for n in range(act.shape[0])
        for f in range(act.shape[1])
    ]

    def bring(n):
        return pltpu.make_async_copy(arrays[n][0], carried.at[n], in_sem.at[n])

    def take(n):
        return pltpu.make_async_copy(carried.at[n], arrays[n][1], out_sem.at[n])

    for n in range(blocks):
        load(n).start()
    for n in range(len(arrays)):
        bring(n).start()
    for row, out in enumerate((ag, ab, ob, fg, fb, db)):
        out[...] = vector[row : row + 1, :]
    for n in range(d_up_bias.shape[1] // width):
        d_up_bias[:, n * width : (n + 1) * width] = vector[6 + n : 7 + n, :]
    for n in range(blocks):
        load(n).wait()
        wide[n] = low[n].astype(F32)
        store(n).start()
    for n in range(len(arrays)):
        bring(n).wait()
        take(n).start()
    for n in range(blocks):
        store(n).wait()
    for n in range(len(arrays)):
        take(n).wait()


def per_device(
    clip_tokens,
    window_cols,
    time_groups,
    cotangent,
    attention_gain,
    attention_bias,
    projection_in,
    projection_out,
    output_bias,
    feedforward_gain,
    feedforward_bias,
    up_weight,
    up_bias,
    down_weight,
    down_bias,
):
    micro, _, frames, band, width = clip_tokens.shape
    hidden = up_weight.shape[2]
    window = band // WCAP
    rows = frames * window
    weights = (
        attention_gain,
        attention_bias,
        projection_in[0],
        projection_out[0],
        output_bias,
        feedforward_gain,
        feedforward_bias,
        up_weight[0],
        up_bias,
        down_weight[0],
        down_bias,
    )
    smem = pl.BlockSpec(memory_space=pltpu.SMEM)
    vmem = pl.BlockSpec(memory_space=pltpu.VMEM)
    hbm = pl.BlockSpec(memory_space=pl.ANY)
    tokens = jax.ShapeDtypeStruct((micro, frames, band, width), BF16)
    chunk = (frames, window, width)
    group_size = lax.axis_size("dp")
    grouped = group_size % GROUP == 0
    flat_shape = (GROUP * UNIT, width)
    kept_shapes = Kept(
        x=(chunk, BF16),
        a1t=((width, rows), BF16),
        qkv=((rows, 3 * width), BF16),
        p=((rows, width), BF16),
        ot=((width, rows), BF16),
        xh2=((rows, width), BF16),
        a2t=((width, rows), BF16),
        rs2=((rows, 128), F32),
        h=((rows, hidden), BF16),
        g=((rows, hidden), BF16),
    )
    results = pl.pallas_call(
        partial(relay_kernel, (micro, frames, window, width, hidden, grouped)),
        out_shape=(
            tokens,
            tokens,
            jax.ShapeDtypeStruct(flat_shape, BF16),
            jax.ShapeDtypeStruct((VECTOR_ROWS, width), F32),
        )
        + tuple(jax.ShapeDtypeStruct((SLOTS,) + shape, kind) for shape, kind in kept_shapes[1:]),
        in_specs=[smem, smem, hbm, hbm] + [vmem if value.shape[0] == 1 else hbm for value in weights],
        out_specs=[hbm] * (3 + len(kept_shapes)),
        scratch_shapes=[pltpu.VMEM(*kept) for kept in kept_shapes * 2]
        + [
            pltpu.VMEM((width, 3 * width), F32),
            pltpu.VMEM((width, width), F32),
            pltpu.VMEM((width, hidden), F32),
            pltpu.VMEM((width, hidden), F32),
            pltpu.VMEM((SLOTS,) + chunk, BF16),
            pltpu.VMEM((SLOTS,) + chunk, BF16),
            pltpu.VMEM((2,) + chunk, BF16),
            pltpu.VMEM((2,) + chunk, BF16),
            pltpu.VMEM((rows, width), BF16),
            pltpu.VMEM((frames * frames // 2, HEADS, 128), F32),
            pltpu.VMEM((frames * frames // 2, HEADS, 128), F32),
            pltpu.VMEM((rows, width), BF16),
            pltpu.VMEM((rows, width), BF16),
            pltpu.VMEM((rows, width), F32),
            pltpu.VMEM((rows, width), F32),
            pltpu.VMEM((2, rows, FF_BLOCK), F32),
            pltpu.VMEM((rows, width), BF16),
            pltpu.VMEM((width, rows), BF16),
            pltpu.VMEM((rows, width), BF16),
            pltpu.VMEM((rows, width), BF16),
            pltpu.VMEM((rows, 3 * width), BF16),
            pltpu.VMEM((3 * width, rows), F32),
            pltpu.VMEM((width, rows), F32),
            pltpu.VMEM((3 * width, rows), BF16),
            pltpu.VMEM((8, width), F32),
            pltpu.VMEM((8, width), F32),
            pltpu.VMEM((8, width), F32),
            pltpu.VMEM((8, width), F32),
            pltpu.VMEM((8, width), F32),
            pltpu.VMEM((8, hidden), F32),
            pltpu.VMEM((8, width), F32),
            pltpu.SemaphoreType.DMA((SLOTS,)),
            pltpu.SemaphoreType.DMA((SLOTS,)),
            pltpu.SemaphoreType.DMA((2,)),
            pltpu.SemaphoreType.DMA((2,)),
            pltpu.SemaphoreType.DMA((2,)),
            pltpu.SemaphoreType.DMA((2,)),
            pltpu.VMEM((LINE, UNIT, hidden), BF16),
            pltpu.VMEM((LINE, UNIT, hidden), BF16),
            pltpu.VMEM((width, 3 * width), BF16),
            pltpu.VMEM((width, width), BF16),
            pltpu.VMEM((width, hidden), BF16),
            pltpu.VMEM((hidden, width), BF16),
            pltpu.SemaphoreType.DMA((4,)),
            pltpu.SemaphoreType.DMA((len(kept_shapes),)),
            pltpu.SemaphoreType.DMA((len(kept_shapes),)),
            pltpu.VMEM((4 + LINE, VECTOR_ROWS, width), F32),
            pltpu.SemaphoreType.DMA((FAMILIES * LINE,)),
            pltpu.SemaphoreType.DMA((FAMILIES * LINE,)),
            pltpu.SemaphoreType.DMA((2 * GROUP + 1,)),
            pltpu.SemaphoreType.REGULAR((4,)),
        ],
        compiler_params=pltpu.CompilerParams(
            collective_id=0, has_side_effects=True, vmem_limit_bytes=63 * 1024 * 1024
        ),
        name="relay",
    )(
        window_cols.T,
        time_groups,
        clip_tokens.reshape(micro, frames, band, width),
        cotangent.reshape(micro, frames, band, width),
        *weights,
    )
    activations, input_grads, flat, vector = results[:4]
    if group_size != GROUP:
        groups = None
        if grouped:
            groups = [[first + n for first in range(0, group_size, GROUP)] for n in range(GROUP)]
        flat, vector = lax.psum((flat, vector), "dp", axis_index_groups=groups)
    square = (width, width)
    row = jax.ShapeDtypeStruct((1, width), F32)
    blocks = GROUP * UNIT // width
    d_in, d_out, d_up, d_down, ag, ab, ob, fg, fb, d_up_bias, db, activations, input_grads = pl.pallas_call(
        output_kernel,
        in_specs=[hbm, vmem, hbm, hbm],
        out_specs=[hbm] * 4 + [vmem] * 7 + [hbm] * 2,
        out_shape=[
            jax.ShapeDtypeStruct((width, 3 * width), F32),
            jax.ShapeDtypeStruct(square, F32),
            jax.ShapeDtypeStruct((width, hidden), F32),
            jax.ShapeDtypeStruct((hidden, width), F32),
        ]
        + [row] * 5
        + [jax.ShapeDtypeStruct((1, hidden), F32), row, tokens, tokens],
        scratch_shapes=[
            pltpu.VMEM((blocks,) + square, BF16),
            pltpu.VMEM((blocks,) + square, F32),
            pltpu.VMEM((2 * micro * frames, band, width), BF16),
            pltpu.SemaphoreType.DMA((blocks,)),
            pltpu.SemaphoreType.DMA((blocks,)),
            pltpu.SemaphoreType.DMA((2 * micro * frames,)),
            pltpu.SemaphoreType.DMA((2 * micro * frames,)),
        ],
        compiler_params=pltpu.CompilerParams(vmem_limit_bytes=62 * 1024 * 1024),
        name="outputs",
    )(flat, vector, activations, input_grads)
    shape_out = (1, micro, 1, frames, band, width)
    return (
        activations.reshape(shape_out),
        input_grads.reshape(shape_out),
        ag,
        ab,
        d_in[None],
        d_out[None],
        ob,
        fg,
        fb,
        d_up[None],
        d_up_bias,
        d_down[None],
        db,
    )


def solution(mesh):
    wide, deep = P("section", None), P("section", None, None)
    tokens = P(None, "dp", None, None, None)
    weights = (wide, wide, deep, deep, wide, wide, wide, deep, wide, deep, wide)
    outputs = P("section", None, "dp", None, None, None)
    return jax.shard_map(
        per_device,
        mesh=mesh,
        in_specs=(tokens, P(None, "dp"), P(None, "dp", None), tokens) + weights,
        out_specs=(outputs, outputs) + weights,
        check_vma=False,
    )
```

```python
from collections import namedtuple
from functools import partial

import jax
import jax.numpy as jnp
from jax import lax
from jax.experimental import pallas as pl
from jax.experimental.pallas import tpu as pltpu
from jax.sharding import PartitionSpec as P

HEADS = 8
WCAP = 5
EPSILON = 1e-05
MASKED = -1e30
MESH = pl.DeviceIdType.MESH

F32 = jnp.float32
BF16 = jnp.bfloat16

LEAD = 4
SLOTS = LEAD + 1
Kept = namedtuple("Kept", ("x", "a1t", "qkv", "p", "ot", "xh2", "a2t", "rs2", "h", "g"))
FF_BLOCK = 512
ROWS_AT_ONCE = 32
COLS_AT_ONCE = 256

INV_SQRT2 = 0.7071067811865476
PDF = 0.3989422804014327
LOG2E = 1.4426950408889634


def mm(a, b):
    return lax.dot_general(a, b, (((1,), (0,)), ((), ())), preferred_element_type=F32)


def mm_bt(a, b):
    return lax.dot_general(a, b, (((1,), (1,)), ((), ())), preferred_element_type=F32)


def mm_at(a, b):
    return lax.dot_general(a, b, (((0,), (0,)), ((), ())), preferred_element_type=F32)


def gelu_and_slope(u):
    cdf = 0.5 + 0.5 * lax.erf(INV_SQRT2 * u)
    bell = jnp.exp2((-0.5 * LOG2E) * (u * u))
    return u * cdf, cdf + (PDF * u) * bell


def fold8(values):
    rows, cols = values.shape
    return jnp.sum(values.reshape(rows // 8, 8, cols), axis=0)


GROUP = 16
LINE = 4
LINE_ORDER = (3, 0, 2, 1)
UNIT = 384
PIECE = 128
WHOLE = slice(0, UNIT)
ACROSS_FIRST = slice(0, 256)
LINE_FIRST = slice(256, UNIT)
PART = {1: ACROSS_FIRST, 2: LINE_FIRST}
SIDES = {1: (0,), 2: (0, 1)}
FAMILIES = 32
VECTOR_ROWS = 16


def group_place():
    me = lax.axis_index("dp")
    core, across, line = lax.rem(me, 2), lax.rem(lax.div(me, 2), 2), lax.rem(lax.div(me, 4), LINE)
    sibling, beside = {"dp": me + 1 - 2 * core}, {"dp": me + 2 - 4 * across}
    return core, across, line, sibling, beside, {"dp": me + 4}, {"dp": me - 4}


def sum_over_group(packed, result, landing, vector, flat_ref, vector_ref, send_sem, recv_sem, out_sem, ready):
    core, across, line, sibling, beside, above, below = group_place()
    sides = (across, 1 - across)
    families = {}
    pending = []

    def when(condition, action):
        if condition is None:
            action()
        else:
            pl.when(condition)(action)

    def remote(family, place, source, target, device):
        number = families.setdefault(family, len(families)) * LINE + place
        return pltpu.make_async_remote_copy(
            src_ref=source,
            dst_ref=target,
            send_sem=send_sem.at[number],
            recv_sem=recv_sem.at[number],
            device_id=device,
            device_id_type=MESH,
        )

    def start(family, place, source, target, device):
        remote(family, place, source, target, device).start()

    def sent(family, place, source, device, condition=None):
        pending.append((condition, lambda: remote(family, place, source, source, device).wait_send()))

    def received(family, place, target, device):
        remote(family, place, target, target, device).wait_recv()

    def unit(ref, half, side, place, part):
        column = place * 512 if isinstance(place, int) else pl.multiple_of(place * 512, 512)
        return ref.at[half * 2 + side, part, pl.ds(column, 512)]

    def add(target, arrived):
        for r in range(0, target.shape[0], 64):
            at = slice(r, r + 64)
            target[at] = (target[at].astype(F32) + arrived[at].astype(F32)).astype(BF16)

    def store(far, rel, place, kind):
        half, side, part = (1 - core if far else core), sides[rel], PART[kind]
        row = pl.multiple_of(((half * 2 + side) * LINE + place) * UNIT + part.start, PIECE)
        return pltpu.make_async_copy(
            unit(result, half, side, place, part),
            flat_ref.at[pl.ds(row, part.stop - part.start)],
            out_sem.at[((far * 2 + rel) * 2 + kind - 1) * LINE + place],
        )

    for number, (device, condition) in enumerate(
        ((sibling, None), (beside, None), (below, line > 0), (above, line < LINE - 1))
    ):
        there = number if number < 2 else 5 - number
        when(
            condition,
            partial(pl.semaphore_signal, ready.at[there], inc=1, device_id=device, device_id_type=MESH),
        )
    pl.semaphore_wait(ready.at[0], 1)

    start("vector core", 0, vector.at[0], vector.at[1], sibling)
    sent("vector core", 0, vector.at[0], sibling)
    for place in LINE_ORDER:
        for side in range(2):
            source = unit(packed, 1 - core, side, place, WHOLE)
            start(("core", side), place, source, landing("core", side, place), sibling)
            sent(("core", side), place, source, sibling)
    pl.semaphore_wait(ready.at[1], 1)
    pl.when(line > 0)(lambda: pl.semaphore_wait(ready.at[2], 1))
    pl.when(line < LINE - 1)(lambda: pl.semaphore_wait(ready.at[3], 1))

    def line_send(kind, place, up, condition):
        device = above if up else below

        def go():
            for rel in SIDES[kind]:
                source = unit(packed, core, sides[rel], place, PART[kind])
                start((kind, up, rel), place, source, landing((kind, up), rel, place), device)

        pl.when(condition)(go)
        for rel in SIDES[kind]:
            sent((kind, up, rel), place, unit(packed, core, sides[rel], place, PART[kind]), device, condition)

    def line_take(kind, place, up, condition):
        def go():
            for rel in SIDES[kind]:
                spot = landing((kind, up), rel, place)
                received((kind, up, rel), place, spot, below if up else above)
                add(unit(packed, core, sides[rel], place, PART[kind]), spot)

        pl.when(condition)(go)

    def from_ends(kind, place):
        if place > 0:
            line_send(kind, place, True, line == 0)
        if place < LINE - 1:
            line_send(kind, place, False, line == LINE - 1)

    def inner_step(kind, k):
        place = LINE - 1 - k
        line_take(kind, place, True, (line > 0) & (line <= place))
        if place > 1:
            line_send(kind, place, True, (line > 0) & (line < place))
        place = k
        line_take(kind, place, False, (line < LINE - 1) & (line >= place))
        if place < LINE - 2:
            line_send(kind, place, False, (line < LINE - 1) & (line > place))

    def take_across(place):
        spot = landing("across", 0, place)
        received("across", place, spot, beside)
        add(unit(packed, core, sides[0], place, ACROSS_FIRST), spot)
        from_ends(1, place)

    for place in LINE_ORDER:
        for side in range(2):
            spot = landing("core", side, place)
            received(("core", side), place, spot, sibling)
            add(unit(packed, core, side, place, WHOLE), spot)
        source = unit(packed, core, sides[1], place, ACROSS_FIRST)
        start("across", place, source, landing("across", 0, place), beside)
        sent("across", place, source, beside)
        from_ends(2, place)
    received("vector core", 0, vector.at[1], sibling)
    vector[2] = vector[0] + vector[1]
    start("vector across", 0, vector.at[2], vector.at[3], beside)
    sent("vector across", 0, vector.at[2], beside)
    for k in range(LINE - 1):
        take_across(LINE_ORDER[k])
        inner_step(2, k)
    take_across(LINE_ORDER[LINE - 1])
    source = unit(packed, core, sides[1], line, LINE_FIRST)
    start("across 2", 0, source, landing("across 2", 0, 0), beside)
    sent("across 2", 0, source, beside)
    received("vector across", 0, vector.at[3], beside)
    vector[4 + line] = vector[2] + vector[3]
    inner_step(1, 0)
    inner_step(1, 1)
    spot = landing("across 2", 0, 0)
    received("across 2", 0, spot, beside)
    own = unit(packed, core, sides[0], line, LINE_FIRST)
    add(own, spot)
    own_two = unit(result, core, sides[0], line, LINE_FIRST)
    own_two[...] = own[...]
    start("gather across 2", 0, own_two, own_two, beside)
    sent("gather across 2", 0, own_two, beside)
    inner_step(1, 2)
    own_one = unit(result, core, sides[0], line, ACROSS_FIRST)
    own_one[...] = unit(packed, core, sides[0], line, ACROSS_FIRST)[...]

    def spread(family, place, spot, up, down):
        if up is not None:
            pl.when(up)(lambda: start((family, True), place, spot, spot, above))
        if down is not None:
            pl.when(down)(lambda: start((family, False), place, spot, spot, below))

    def hand_over(kind, rel, place):
        spot = unit(result, core, sides[rel], place, PART[kind])
        start(("gather core", kind, rel), place, spot, spot, sibling)
        store(0, rel, place, kind).start()

    def have(kind, rel, place, up, down):
        spot = unit(result, core, sides[rel], place, PART[kind])
        spread(("spread", kind, rel), place, spot, up, down)
        if kind == 1:
            start("gather across", place, spot, spot, beside)
        hand_over(kind, rel, place)

    def come(distance, action):
        pl.when(line >= distance)(lambda: action(line - distance, True))
        pl.when(line + distance < LINE)(lambda: action(line + distance, False))

    def arrive(kind, rel, distance):
        def action(place, up):
            spot = unit(result, core, sides[rel], place, PART[kind])
            received((("spread", kind, rel), up), place, spot, below if up else above)
            have(kind, rel, place, line < LINE - 1 if up else None, None if up else line > 0)

        come(distance, action)

    def arrive_vector(distance):
        def action(place, up):
            spot = vector.at[4 + place]
            received(("vector", up), place, spot, below if up else above)
            spread("vector", place, spot, line < LINE - 1 if up else None, None if up else line > 0)

        come(distance, action)

    def arrive_across(distance):
        def action(place, up):
            received("gather across", place, unit(result, core, sides[1], place, ACROSS_FIRST), beside)
            hand_over(1, 1, place)

        if distance == 0:
            action(line, True)
        else:
            come(distance, action)

    have(1, 0, line, line < LINE - 1, line > 0)
    have(2, 0, line, line < LINE - 1, line > 0)
    spread("vector", line, vector.at[4 + line], line < LINE - 1, line > 0)
    received("gather across 2", 0, unit(result, core, sides[1], line, LINE_FIRST), beside)
    have(2, 1, line, line < LINE - 1, line > 0)
    for distance in range(1, LINE):
        arrive(1, 0, distance)
        arrive(2, 0, distance)
        arrive(2, 1, distance)
        arrive_vector(distance)
        arrive_across(distance - 1)
    arrive_across(LINE - 1)
    vector[1] = (vector[4] + vector[5]) + (vector[6] + vector[7])
    vector_out = pltpu.make_async_copy(vector.at[1], vector_ref, out_sem.at[2 * GROUP])
    vector_out.start()
    for place in range(LINE):
        for kind in (1, 2):
            for rel in range(2):
                spot = unit(result, 1 - core, sides[rel], place, PART[kind])
                received(("gather core", kind, rel), place, spot, sibling)
                store(1, rel, place, kind).start()
    vector_out.wait()

    for place in range(LINE):
        for kind in (1, 2):
            for rel in range(2):
                spot = unit(result, core, sides[rel], place, PART[kind])
                sent(("gather core", kind, rel), place, spot, sibling)
                store(0, rel, place, kind).wait()
                store(1, rel, place, kind).wait()
            for rel in SIDES[kind]:
                spot = unit(result, core, sides[rel], place, PART[kind])
                sent((("spread", kind, rel), True), place, spot, above, (line >= place) & (line < LINE - 1))
                sent((("spread", kind, rel), False), place, spot, below, (line <= place) & (line > 0))
        sent("gather across", place, unit(result, core, sides[0], place, ACROSS_FIRST), beside)
        sent(("vector", True), place, vector.at[4 + place], above, (line >= place) & (line < LINE - 1))
        sent(("vector", False), place, vector.at[4 + place], below, (line <= place) & (line > 0))
    for condition, wait in pending:
        when(condition, wait)


def relay_kernel(
    dims,
    cols_ref,
    groups_ref,
    clip_ref,
    cot_ref,
    attention_gain,
    attention_bias,
    projection_in,
    projection_out,
    output_bias,
    feedforward_gain,
    feedforward_bias,
    up_weight,
    up_bias,
    down_weight,
    down_bias,
    act_ref,
    grad_ref,
    flat_ref,
    vector_ref,
    *scratch,
):
    micro, frames, window, width, hidden, grouped = dims
    parked, scratch = scratch[: len(Kept._fields) - 1], scratch[len(Kept._fields) - 1 :]
    kept_a, scratch = Kept(*scratch[: len(Kept._fields)]), scratch[len(Kept._fields) :]
    kept_b, scratch = Kept(*scratch[: len(Kept._fields)]), scratch[len(Kept._fields) :]
    (
    d_projection_in,
    d_projection_out,
    d_up_weight,
    d_down_weight,
    xbuf,
    dybuf,
    ybuf,
    dxbuf,
    a1_buf,
    pf_buf,
    ds_buf,
    o_buf,
    a2_buf,
    wide,
    total,
    u_buf,
    e_buf,
    et_buf,
    c_buf,
    do_buf,
    dqkv_buf,
    qkvt_buf,
    dot_buf,
    dqkvt_buf,
    sum_ag,
    sum_ab,
    sum_ob,
    sum_fg,
    sum_fb,
    sum_ub,
    sum_db,
    x_sem,
    dy_sem,
    y_sem,
    y_send,
    dx_sem,
    dx_send,
    packed,
    result,
    park_sem,
    fetch_sem,
    vector,
    group_send,
    group_recv,
    group_out,
    ready,
    ) = scratch
    rows = frames * window
    count = micro * WCAP
    head = width // HEADS
    pair = 2 * head
    scale = head ** (-0.5)
    section = lax.axis_index("section")
    leading = section == 0
    trailing = section != 0
    lead = LEAD * (1 - section)
    partner = {"section": 1 - section}

    def hbm_chunk(ref, chunk):
        start = pl.multiple_of(lax.rem(chunk, WCAP) * window, window)
        return ref.at[lax.div(chunk, WCAP), :, pl.ds(start, window), :]

    def x_load(chunk):
        slot = lax.rem(chunk, SLOTS)
        return pltpu.make_async_copy(hbm_chunk(clip_ref, chunk), xbuf.at[slot], x_sem.at[slot])

    def dy_load(chunk):
        slot = lax.rem(chunk, SLOTS)
        return pltpu.make_async_copy(hbm_chunk(cot_ref, chunk), dybuf.at[slot], dy_sem.at[slot])

    def y_store(chunk):
        slot = lax.rem(chunk, 2)
        return pltpu.make_async_copy(ybuf.at[slot], hbm_chunk(act_ref, chunk), y_sem.at[slot])

    def dx_store(chunk):
        slot = lax.rem(chunk, 2)
        return pltpu.make_async_copy(dxbuf.at[slot], hbm_chunk(grad_ref, chunk), dx_sem.at[slot])

    def park(chunk):
        slot = lax.rem(chunk, SLOTS)
        return [
            pltpu.make_async_copy(here, there.at[slot], park_sem.at[n])
            for n, (here, there) in enumerate(zip(kept_a[1:], parked))
        ]

    def fetch(chunk):
        slot = lax.rem(chunk, SLOTS)
        return [pltpu.make_async_copy(hbm_chunk(clip_ref, chunk), kept_b.x, fetch_sem.at[0])] + [
            pltpu.make_async_copy(there.at[slot], here, fetch_sem.at[n + 1])
            for n, (here, there) in enumerate(zip(kept_b[1:], parked))
        ]

    def start_all(copies):
        for copy in copies:
            copy.start()

    def wait_all(copies):
        for copy in copies:
            copy.wait()

    def y_remote(chunk):
        slot, there = lax.rem(chunk, 2), lax.rem(chunk, SLOTS)
        return pltpu.make_async_remote_copy(
            src_ref=ybuf.at[slot],
            dst_ref=xbuf.at[there],
            send_sem=y_send.at[slot],
            recv_sem=x_sem.at[there],
            device_id=partner,
            device_id_type=MESH,
        )

    def dx_remote(chunk):
        slot, there = lax.rem(chunk, 2), lax.rem(chunk, SLOTS)
        return pltpu.make_async_remote_copy(
            src_ref=dxbuf.at[slot],
            dst_ref=dybuf.at[there],
            send_sem=dx_send.at[slot],
            recv_sem=dy_sem.at[there],
            device_id=partner,
            device_id_type=MESH,
        )

    barrier = pltpu.get_barrier_semaphore()
    greeted = 1
    pl.semaphore_signal(barrier, inc=1, device_id=partner, device_id_type=MESH)
    if grouped:
        _, _, line, sibling, beside, above, below = group_place()
        has_below, has_above = line > 0, line < LINE - 1
        for device, condition in ((sibling, None), (beside, None), (below, has_below), (above, has_above)):
            greet = partial(pl.semaphore_signal, barrier, inc=1, device_id=device, device_id_type=MESH)
            if condition is None:
                greet()
            else:
                pl.when(condition)(greet)
        greeted = 3 + has_below.astype(jnp.int32) + has_above.astype(jnp.int32)

    @pl.when(leading)
    def _():
        x_load(0).start()

    @pl.when(trailing)
    def _():
        dy_load(0).start()

    for total_ref in (d_projection_in, d_projection_out, d_up_weight, d_down_weight):
        total_ref[...] = jnp.zeros_like(total_ref)
    for total_ref in (sum_ag, sum_ab, sum_ob, sum_fg, sum_fb, sum_ub, sum_db):
        total_ref[...] = jnp.zeros_like(total_ref)

    pl.semaphore_wait(barrier, greeted)

    def frame_rows(i):
        return slice(i * window, (i + 1) * window)

    half = lax.broadcasted_iota(jnp.int32, (window, pair), 1) < head
    low_half = jnp.where(half, 1.0, 0.0).astype(BF16)
    high_half = jnp.where(half, 0.0, 1.0).astype(BF16)

    def by_head(values):
        return jnp.concatenate([values * low_half, values * high_half], axis=0)

    def join_heads(values):
        return jnp.where(half, values[:window], values[window:])

    heads_of = [
        (frame_rows(f), slice(n * pair, (n + 1) * pair), n) for f in range(frames) for n in range(width // pair)
    ]

    def of_pair(ref, at, which, n):
        return ref[at, which * width + n * pair : which * width + (n + 1) * pair]

    def window_forward(kept):
        for at, lanes, n in heads_of:
            keys = of_pair(kept.qkv, at, 1, n)
            total[at, lanes] = mm_bt(keys, by_head(of_pair(kept.qkv, at, 0, n)))
        yield
        for at, lanes, n in heads_of:
            scores = total[at, lanes] * scale
            scores = jnp.exp(scores - jnp.max(scores, axis=0, keepdims=True))
            probs = scores * (1.0 / jnp.sum(scores, axis=0, keepdims=True))
            kept.p[at, lanes] = probs.astype(BF16)
        yield
        for at, lanes, n in heads_of:
            values = of_pair(kept.qkv, at, 2, n)
            o_buf[at, lanes] = join_heads(mm_at(kept.p[at, lanes], values)).astype(BF16)

    def window_backward(kept):
        for at, lanes, n in heads_of:
            up = by_head(do_buf[at, lanes])
            total[at, lanes] = mm_bt(of_pair(kept.qkv, at, 2, n), up)
            dv = mm(kept.p[at, lanes], up)
            dqkv_buf[at, 2 * width + n * pair : 2 * width + (n + 1) * pair] = dv.astype(BF16)
        yield
        for at, lanes, n in heads_of:
            probs = kept.p[at, lanes].astype(F32)
            dp = total[at, lanes]
            ds = probs * (dp - jnp.sum(probs * dp, axis=0, keepdims=True))
            e_buf[at, lanes] = ds.astype(BF16)
        yield
        for at, lanes, n in heads_of:
            ds = e_buf[at, lanes]
            dk = mm(ds, by_head(of_pair(kept.qkv, at, 0, n))) * scale
            dqkv_buf[at, width + n * pair : width + (n + 1) * pair] = dk.astype(BF16)
            dq = join_heads(mm_at(ds, of_pair(kept.qkv, at, 1, n))) * scale
            dqkv_buf[at, lanes] = dq.astype(BF16)

    low_frame = lax.broadcasted_iota(jnp.int32, (1, 128), 1) < window

    def lane_tiles(i):
        return min(i + 1, frames - 1) // 2 + 1

    def tile(t):
        return slice(t * 128, (t + 1) * 128)

    def head_rows(which, h):
        return slice(which * width + h * head, which * width + (h + 1) * head)

    def other_half(values):
        return pltpu.roll(values, window, axis=1)

    def both_frames(ref, at, t):
        values = ref[at, tile(t)]
        turned = other_half(values)
        return jnp.where(low_frame, values, turned), jnp.where(low_frame, turned, values)

    def frame_forward(chunk, kept):
        tile_count = frames // 2
        for n in range(3):
            flat = kept.qkv[:, n * width : (n + 1) * width].T
            qkvt_buf[n * width : (n + 1) * width, :] = flat.astype(F32)
        for h in range(HEADS):
            keys = [qkvt_buf[head_rows(1, h), tile(t)] for t in range(tile_count)]
            for pair_index in range(tile_count):
                queries = both_frames(qkvt_buf, head_rows(0, h), pair_index)
                for i in (2 * pair_index, 2 * pair_index + 1):
                    for t in range(lane_tiles(i)):
                        score = jnp.sum(queries[i % 2] * keys[t], axis=0, keepdims=True)
                        ds_buf[i * tile_count + t, h : h + 1, :] = score
        yield
        item = lax.div(chunk, WCAP)
        labels = [
            jnp.where(low_frame, groups_ref[item, 0, 2 * t], groups_ref[item, 0, 2 * t + 1])
            for t in range(tile_count)
        ]
        for i in range(frames):
            mine = groups_ref[item, 0, i]
            parts = [
                jnp.where(labels[t] <= mine, ds_buf[i * tile_count + t] * scale, MASKED)
                for t in range(lane_tiles(i))
            ]
            largest = parts[0]
            for part in parts[1:]:
                largest = jnp.maximum(largest, part)
            largest = jnp.maximum(largest, other_half(largest))
            parts = [jnp.exp(part - largest) for part in parts]
            whole = parts[0]
            for part in parts[1:]:
                whole = whole + part
            whole = 1.0 / (whole + other_half(whole))
            for t, part in enumerate(parts):
                pf_buf[i * tile_count + t] = part * whole
        yield
        for h in range(HEADS):
            values = [qkvt_buf[head_rows(2, h), tile(t)] for t in range(tile_count)]
            for pair_index in range(tile_count):
                mixed = []
                for i in (2 * pair_index, 2 * pair_index + 1):
                    part = 0.0
                    for t in range(lane_tiles(i)):
                        part = part + pf_buf[i * tile_count + t, h : h + 1, :] * values[t]
                    mixed.append(part + other_half(part))
                both = jnp.where(low_frame, mixed[0], mixed[1])
                kept.ot[head_rows(0, h), tile(pair_index)] = both.astype(BF16)

    def frame_backward(kept, beside):
        tile_count = frames // 2
        for h in range(HEADS):
            beside()
            values = [qkvt_buf[head_rows(2, h), tile(t)] for t in range(tile_count)]
            dv = [0.0] * tile_count
            for pair_index in range(tile_count):
                ups = both_frames(dot_buf, head_rows(0, h), pair_index)
                for i in (2 * pair_index, 2 * pair_index + 1):
                    for t in range(lane_tiles(i)):
                        ds_buf[i * tile_count + t, h : h + 1, :] = jnp.sum(
                            ups[i % 2] * values[t], axis=0, keepdims=True
                        )
                        dv[t] = dv[t] + pf_buf[i * tile_count + t, h : h + 1, :] * ups[i % 2]
            for t in range(tile_count):
                dqkvt_buf[head_rows(2, h), tile(t)] = dv[t].astype(BF16)
        for i in range(frames):
            spots = [i * tile_count + t for t in range(lane_tiles(i))]
            along = pf_buf[spots[0]] * ds_buf[spots[0]]
            for spot in spots[1:]:
                along = along + pf_buf[spot] * ds_buf[spot]
            along = along + other_half(along)
            for spot in spots:
                ds_buf[spot] = pf_buf[spot] * (ds_buf[spot] - along) * scale
        for h in range(HEADS):
            beside()
            keys = [qkvt_buf[head_rows(1, h), tile(t)] for t in range(tile_count)]
            dk = [0.0] * tile_count
            for pair_index in range(tile_count):
                queries = both_frames(qkvt_buf, head_rows(0, h), pair_index)
                dq = []
                for i in (2 * pair_index, 2 * pair_index + 1):
                    part = 0.0
                    for t in range(lane_tiles(i)):
                        ds = ds_buf[i * tile_count + t, h : h + 1, :]
                        part = part + ds * keys[t]
                        dk[t] = dk[t] + ds * queries[i % 2]
                    dq.append(part + other_half(part))
                both = jnp.where(low_frame, dq[0], dq[1])
                dqkvt_buf[head_rows(0, h), tile(pair_index)] = both.astype(BF16)
            for t in range(tile_count):
                dqkvt_buf[head_rows(1, h), tile(t)] = dk[t].astype(BF16)
        for n in range(3):
            dqkv_buf[:, n * width : (n + 1) * width] = dqkvt_buf[n * width : (n + 1) * width, :].T

    def live_of(chunk):
        cols = cols_ref[0, lax.div(chunk, WCAP)]
        return jnp.where(lax.rem(chunk, WCAP) < cols, 1.0, 0.0).astype(F32)

    def standardize(values):
        centered = values - jnp.mean(values, axis=-1, keepdims=True)
        rstd = lax.rsqrt(jnp.mean(centered * centered, axis=-1, keepdims=True) + EPSILON)
        return centered * rstd, rstd

    blocks = [
        (slice(r, r + ROWS_AT_ONCE), r // window, slice(r % window, r % window + ROWS_AT_ONCE))
        for r in range(0, rows, ROWS_AT_ONCE)
    ]
    ff_parts = [slice(c, c + FF_BLOCK) for c in range(0, hidden, FF_BLOCK)]

    def halves(cols, start=0, step=COLS_AT_ONCE):
        return [slice(c, c + step) for c in range(start, start + cols, step)]

    def forward(spatial, chunk, kept, slot, y_slot):
        kept.x[...] = xbuf[slot]
        for at, f, within in blocks:
            unit, _ = standardize(kept.x[f, within].astype(F32))
            a1_buf[at, :] = (unit * attention_gain[...] + attention_bias[...]).astype(BF16)
        yield
        kept.a1t[...] = a1_buf[...].T
        for part in halves(3 * width, step=width):
            kept.qkv[:, part] = mm(a1_buf[...], projection_in[:, part]).astype(BF16)
        yield
        if spatial:
            yield from window_forward(kept)
            yield
            kept.ot[...] = o_buf[...].T
        else:
            yield from frame_forward(chunk, kept)
            yield
            o_buf[...] = kept.ot[...].T
        wide[...] = mm(o_buf[...], projection_out[...])
        yield
        for at, f, within in blocks:
            middle = kept.x[f, within].astype(F32) + (wide[at, :] + output_bias[...])
            wide[at, :] = middle + down_bias[...]
            unit, rstd = standardize(middle)
            kept.xh2[at, :] = unit.astype(BF16)
            kept.rs2[at, :] = jnp.broadcast_to(rstd, (ROWS_AT_ONCE, 128))
            a2_buf[at, :] = (unit * feedforward_gain[...] + feedforward_bias[...]).astype(BF16)
        yield
        kept.a2t[...] = a2_buf[...].T
        u_buf[0] = mm(a2_buf[...], up_weight[:, ff_parts[0]])
        yield
        for n, part in enumerate(ff_parts):
            if n + 1 < len(ff_parts):
                u_buf[(n + 1) % 2] = mm(a2_buf[...], up_weight[:, ff_parts[n + 1]])
            for at, _, _ in blocks:
                for inner, outer in zip(halves(FF_BLOCK), halves(FF_BLOCK, part.start)):
                    h, slope = gelu_and_slope(u_buf[n % 2, at, inner] + up_bias[:, outer])
                    kept.h[at, outer] = h.astype(BF16)
                    kept.g[at, outer] = slope.astype(BF16)
            yield
        total[...] = mm(kept.h[...], down_weight[...])
        yield
        live = live_of(chunk)
        for at, f, within in blocks:
            ybuf[y_slot, f, within] = ((wide[at, :] + total[at, :]) * live).astype(BF16)
        y_store(chunk).start()
        if spatial:
            y_remote(chunk).start()

    def norm_backward(d_normed, unit, rstd, gain):
        d_unit = d_normed * gain
        along = jnp.mean(d_unit * unit, axis=-1, keepdims=True)
        return rstd * (d_unit - jnp.mean(d_unit, axis=-1, keepdims=True) - unit * along)

    def weight_gradient(total_ref, left, right, cols):
        for part in cols:
            total_ref[:, part] += mm(left[...], right[:, part])

    def backward(spatial, chunk, kept, slot, dx_slot):
        if spatial:
            dx_remote(chunk).wait_recv()
        else:
            dy_load(chunk).wait()

        @pl.when(chunk >= 2)
        def _():
            dx_store(chunk - 2).wait()
            if not spatial:
                dx_remote(chunk - 2).wait_send()

        live = live_of(chunk)
        e_buf[...] = (dybuf[slot].reshape(rows, width).astype(F32) * live).astype(BF16)
        for at, f, within in blocks:
            sum_db[...] += fold8(e_buf[at, :].astype(F32))
        yield
        et_buf[...] = e_buf[...].T
        u_buf[0] = mm_bt(e_buf[...], down_weight[ff_parts[0], :])
        yield
        for n, part in enumerate(ff_parts):
            if n + 1 < len(ff_parts):
                u_buf[(n + 1) % 2] = mm_bt(e_buf[...], down_weight[ff_parts[n + 1], :])
            if spatial:
                weight_gradient(d_down_weight, et_buf, kept.h, halves(FF_BLOCK, part.start))
            for at, _, _ in blocks:
                for inner, outer in zip(halves(FF_BLOCK), halves(FF_BLOCK, part.start)):
                    du = u_buf[n % 2, at, inner] * kept.g[at, outer].astype(F32)
                    sum_ub[:, outer] += fold8(du)
                    kept.g[at, outer] = du.astype(BF16)
            yield
        total[...] = mm_bt(kept.g[...], up_weight[...])
        yield
        for n, (at, _, _) in enumerate(blocks):
            if n % 3 == 0:
                grown = (d_up_weight, kept.a2t, kept.g) if spatial else (d_down_weight, et_buf, kept.h)
                weight_gradient(*grown, halves(FF_BLOCK, n // 3 * FF_BLOCK))
            d_normed = total[at, :]
            unit = kept.xh2[at, :].astype(F32)
            sum_fg[...] += fold8(d_normed * unit)
            sum_fb[...] += fold8(d_normed)
            rstd = kept.rs2[at, 0:1]
            d_middle = e_buf[at, :].astype(F32) + norm_backward(d_normed, unit, rstd, feedforward_gain[...])
            wide[at, :] = d_middle
            sum_ob[...] += fold8(d_middle)
            c_buf[at, :] = d_middle.astype(BF16)
        yield
        if spatial:
            do_buf[...] = mm_bt(c_buf[...], projection_out[...]).astype(BF16)
        else:
            dot_buf[...] = mm_bt(projection_out[...], c_buf[...])
        if spatial:
            weight_gradient(d_projection_out, kept.ot, c_buf, halves(width))
            yield from window_backward(kept)
        else:
            waiting = [(d_up_weight, kept.a2t, kept.g, [part]) for part in halves(hidden)]
            waiting += [(d_projection_out, kept.ot, c_buf, [part]) for part in halves(width)]

            def beside():
                if waiting:
                    weight_gradient(*waiting.pop(0))

            frame_backward(kept, beside)
        total[...] = mm_bt(dqkv_buf[...], projection_in[...])
        yield
        for n, (at, f, within) in enumerate(blocks):
            if n % 2 == 0:
                weight_gradient(d_projection_in, kept.a1t, dqkv_buf, halves(COLS_AT_ONCE, n // 2 * COLS_AT_ONCE))
            d_normed = total[at, :]
            unit, rstd = standardize(kept.x[f, within].astype(F32))
            sum_ag[...] += fold8(d_normed * unit)
            sum_ab[...] += fold8(d_normed)
            dx = wide[at, :] + norm_backward(d_normed, unit, rstd, attention_gain[...])
            do_buf[at, :] = dx.astype(BF16)
        yield
        dxbuf[dx_slot] = do_buf[...].reshape(frames, window, width)
        dx_store(chunk).start()
        if not spatial:
            dx_remote(chunk).start()

    def emit(pieces):
        for _ in pieces:
            pass

    def step(t, carry):
        chunk = t - lead
        ahead = (t, kept_a, lax.rem(t, SLOTS), lax.rem(t, 2))
        behind = (chunk, lax.rem(chunk + SLOTS, SLOTS), lax.rem(chunk + 2, 2))

        @pl.when(t < count)
        def _():
            @pl.when(leading)
            def _():
                x_load(t).wait()

                @pl.when(t + 1 < count)
                def _():
                    x_load(t + 1).start()

            @pl.when(trailing)
            def _():
                y_remote(t).wait_recv()

                @pl.when(t + 1 < count)
                def _():
                    dy_load(t + 1).start()

            @pl.when(t >= 2)
            def _():
                y_store(t - 2).wait()

                @pl.when(leading)
                def _():
                    y_remote(t - 2).wait_send()

        @pl.when(leading & (t > 0) & (t <= count))
        def _():
            wait_all(park(t - 1))

        @pl.when(leading & (t == 1))
        def _():
            start_all(fetch(0))

        @pl.when(leading & (t < count))
        def _():
            emit(forward(True, *ahead))
            start_all(park(t))

        @pl.when(leading & (chunk >= 0))
        def _():
            wait_all(fetch(chunk))
            emit(backward(True, chunk, kept_b, *behind[1:]))

            @pl.when(chunk + 1 < count)
            def _():
                start_all(fetch(chunk + 1))

        @pl.when(trailing & (t < count))
        def _():
            emit(forward(False, *ahead))
            emit(backward(False, chunk, kept_a, *behind[1:]))

        return carry

    lax.fori_loop(0, count + LEAD, step, 0)

    vector[0] = jnp.zeros_like(vector[0])
    for row, partial_sum in enumerate((sum_ag, sum_ab, sum_ob, sum_fg, sum_fb, sum_db)):
        vector[0, row : row + 1, :] = jnp.sum(partial_sum[...], axis=0, keepdims=True)
    for n in range(hidden // width):
        up_sum = jnp.sum(sum_ub[:, n * width : (n + 1) * width], axis=0, keepdims=True)
        vector[0, 6 + n : 7 + n, :] = up_sum

    def block_piece(number):
        block, r = divmod(number, width // PIECE)
        at = slice(r * PIECE, (r + 1) * PIECE)
        if block < 3:
            return d_projection_in[at, block * width : (block + 1) * width].astype(BF16)
        if block < 4:
            return d_projection_out[at, :].astype(BF16)
        if block < 8:
            return d_up_weight[at, (block - 4) * width : (block - 3) * width].astype(BF16)
        start = (block - 8) * width + r * PIECE
        return d_down_weight[:, start : start + PIECE].astype(BF16).T

    for number in range(GROUP * UNIT // PIECE):
        u, r = divmod(number, UNIT // PIECE)
        at = slice(r * PIECE, (r + 1) * PIECE)
        packed[u // LINE, at, u % LINE * width : (u % LINE + 1) * width] = block_piece(number)

    def finish():
        for last in (count - 2, count - 1):
            y_store(last).wait()
            dx_store(last).wait()

            @pl.when(leading)
            def _():
                y_remote(last).wait_send()

            @pl.when(trailing)
            def _():
                dx_remote(last).wait_send()

    if not grouped:
        finish()
        for u in range(GROUP):
            cols = slice(u % LINE * width, (u % LINE + 1) * width)
            pltpu.sync_copy(packed.at[u // LINE, :, cols], flat_ref.at[u * UNIT : (u + 1) * UNIT])
        pltpu.sync_copy(vector.at[0], vector_ref)
        return

    def landing(name, rel, place):
        col = slice(place * width, (place + 1) * width)
        if name == "core":
            return (kept_a.g if rel else kept_a.h).at[:, col]
        if name == "across":
            return kept_b.h.at[ACROSS_FIRST, col]
        if name == "across 2":
            return e_buf.at[:PIECE]
        kind, up = name
        if kind == 1:
            return (kept_b.g if up else kept_a.qkv).at[ACROSS_FIRST, col]
        if up:
            return (kept_b.g if rel else kept_b.h).at[LINE_FIRST, col]
        if rel:
            return dqkv_buf.at[:PIECE, col]
        return kept_a.qkv.at[LINE_FIRST, col]

    sum_over_group(
        packed, result, landing, vector, flat_ref, vector_ref, group_send, group_recv, group_out, ready
    )
    finish()


def output_kernel(
    flat,
    vector,
    act,
    grad,
    d_in,
    d_out,
    d_up,
    d_down,
    ag,
    ab,
    ob,
    fg,
    fb,
    d_up_bias,
    db,
    act_out,
    grad_out,
    low,
    wide,
    carried,
    low_sem,
    wide_sem,
    in_sem,
    out_sem,
):
    blocks, width, _ = low.shape

    def load(n):
        return pltpu.make_async_copy(flat.at[n * width : (n + 1) * width], low.at[n], low_sem.at[n])

    def target(n):
        if n < 3:
            return d_in.at[:, n * width : (n + 1) * width]
        if n == 3:
            return d_out
        if n < 8:
            return d_up.at[:, (n - 4) * width : (n - 3) * width]
        return d_down.at[(n - 8) * width : (n - 7) * width]

    def store(n):
        return pltpu.make_async_copy(wide.at[n], target(n), wide_sem.at[n])

    arrays = [(ref.at[n], out.at[n]) for ref, out in ((act, act_out), (grad, grad_out)) for n in range(act.shape[0])]

    def bring(n):
        return pltpu.make_async_copy(arrays[n][0], carried.at[n], in_sem.at[n])

    def take(n):
        return pltpu.make_async_copy(carried.at[n], arrays[n][1], out_sem.at[n])

    for n in range(blocks):
        load(n).start()
    for n in range(len(arrays)):
        bring(n).start()
    for row, out in enumerate((ag, ab, ob, fg, fb, db)):
        out[...] = vector[row : row + 1, :]
    for n in range(d_up_bias.shape[1] // width):
        d_up_bias[:, n * width : (n + 1) * width] = vector[6 + n : 7 + n, :]
    for n in range(blocks):
        load(n).wait()
        wide[n] = low[n].astype(F32)
        store(n).start()
    for n in range(len(arrays)):
        bring(n).wait()
        take(n).start()
    for n in range(blocks):
        store(n).wait()
    for n in range(len(arrays)):
        take(n).wait()


def per_device(
    clip_tokens,
    window_cols,
    time_groups,
    cotangent,
    attention_gain,
    attention_bias,
    projection_in,
    projection_out,
    output_bias,
    feedforward_gain,
    feedforward_bias,
    up_weight,
    up_bias,
    down_weight,
    down_bias,
):
    micro, _, frames, band, width = clip_tokens.shape
    hidden = up_weight.shape[2]
    window = band // WCAP
    rows = frames * window
    weights = (
        attention_gain,
        attention_bias,
        projection_in[0],
        projection_out[0],
        output_bias,
        feedforward_gain,
        feedforward_bias,
        up_weight[0],
        up_bias,
        down_weight[0],
        down_bias,
    )
    smem = pl.BlockSpec(memory_space=pltpu.SMEM)
    vmem = pl.BlockSpec(memory_space=pltpu.VMEM)
    hbm = pl.BlockSpec(memory_space=pl.ANY)
    tokens = jax.ShapeDtypeStruct((micro, frames, band, width), BF16)
    chunk = (frames, window, width)
    group_size = lax.axis_size("dp")
    grouped = group_size % GROUP == 0
    flat_shape = (GROUP * UNIT, width)
    kept_shapes = Kept(
        x=(chunk, BF16),
        a1t=((width, rows), BF16),
        qkv=((rows, 3 * width), BF16),
        p=((rows, width), BF16),
        ot=((width, rows), BF16),
        xh2=((rows, width), BF16),
        a2t=((width, rows), BF16),
        rs2=((rows, 128), F32),
        h=((rows, hidden), BF16),
        g=((rows, hidden), BF16),
    )
    results = pl.pallas_call(
        partial(relay_kernel, (micro, frames, window, width, hidden, grouped)),
        out_shape=(
            tokens,
            tokens,
            jax.ShapeDtypeStruct(flat_shape, BF16),
            jax.ShapeDtypeStruct((VECTOR_ROWS, width), F32),
        )
        + tuple(jax.ShapeDtypeStruct((SLOTS,) + shape, kind) for shape, kind in kept_shapes[1:]),
        in_specs=[smem, smem, hbm, hbm] + [vmem] * len(weights),
        out_specs=[hbm] * (3 + len(kept_shapes)),
        scratch_shapes=[pltpu.VMEM(*kept) for kept in kept_shapes * 2]
        + [
            pltpu.VMEM((width, 3 * width), F32),
            pltpu.VMEM((width, width), F32),
            pltpu.VMEM((width, hidden), F32),
            pltpu.VMEM((width, hidden), F32),
            pltpu.VMEM((SLOTS,) + chunk, BF16),
            pltpu.VMEM((SLOTS,) + chunk, BF16),
            pltpu.VMEM((2,) + chunk, BF16),
            pltpu.VMEM((2,) + chunk, BF16),
            pltpu.VMEM((rows, width), BF16),
            pltpu.VMEM((frames * frames // 2, HEADS, 128), F32),
            pltpu.VMEM((frames * frames // 2, HEADS, 128), F32),
            pltpu.VMEM((rows, width), BF16),
            pltpu.VMEM((rows, width), BF16),
            pltpu.VMEM((rows, width), F32),
            pltpu.VMEM((rows, width), F32),
            pltpu.VMEM((2, rows, FF_BLOCK), F32),
            pltpu.VMEM((rows, width), BF16),
            pltpu.VMEM((width, rows), BF16),
            pltpu.VMEM((rows, width), BF16),
            pltpu.VMEM((rows, width), BF16),
            pltpu.VMEM((rows, 3 * width), BF16),
            pltpu.VMEM((3 * width, rows), F32),
            pltpu.VMEM((width, rows), F32),
            pltpu.VMEM((3 * width, rows), BF16),
            pltpu.VMEM((8, width), F32),
            pltpu.VMEM((8, width), F32),
            pltpu.VMEM((8, width), F32),
            pltpu.VMEM((8, width), F32),
            pltpu.VMEM((8, width), F32),
            pltpu.VMEM((8, hidden), F32),
            pltpu.VMEM((8, width), F32),
            pltpu.SemaphoreType.DMA((SLOTS,)),
            pltpu.SemaphoreType.DMA((SLOTS,)),
            pltpu.SemaphoreType.DMA((2,)),
            pltpu.SemaphoreType.DMA((2,)),
            pltpu.SemaphoreType.DMA((2,)),
            pltpu.SemaphoreType.DMA((2,)),
            pltpu.VMEM((LINE, UNIT, hidden), BF16),
            pltpu.VMEM((LINE, UNIT, hidden), BF16),
            pltpu.SemaphoreType.DMA((len(kept_shapes),)),
            pltpu.SemaphoreType.DMA((len(kept_shapes),)),
            pltpu.VMEM((4 + LINE, VECTOR_ROWS, width), F32),
            pltpu.SemaphoreType.DMA((FAMILIES * LINE,)),
            pltpu.SemaphoreType.DMA((FAMILIES * LINE,)),
            pltpu.SemaphoreType.DMA((2 * GROUP + 1,)),
            pltpu.SemaphoreType.REGULAR((4,)),
        ],
        compiler_params=pltpu.CompilerParams(
            collective_id=0, has_side_effects=True, vmem_limit_bytes=63 * 1024 * 1024
        ),
        name="relay",
    )(
        window_cols.T,
        time_groups,
        clip_tokens.reshape(micro, frames, band, width),
        cotangent.reshape(micro, frames, band, width),
        *weights,
    )
    activations, input_grads, flat, vector = results[:4]
    if group_size != GROUP:
        groups = None
        if grouped:
            groups = [[first + n for first in range(0, group_size, GROUP)] for n in range(GROUP)]
        flat, vector = lax.psum((flat, vector), "dp", axis_index_groups=groups)
    square = (width, width)
    row = jax.ShapeDtypeStruct((1, width), F32)
    blocks = GROUP * UNIT // width
    d_in, d_out, d_up, d_down, ag, ab, ob, fg, fb, d_up_bias, db, activations, input_grads = pl.pallas_call(
        output_kernel,
        in_specs=[hbm, vmem, hbm, hbm],
        out_specs=[hbm] * 4 + [vmem] * 7 + [hbm] * 2,
        out_shape=[
            jax.ShapeDtypeStruct((width, 3 * width), F32),
            jax.ShapeDtypeStruct(square, F32),
            jax.ShapeDtypeStruct((width, hidden), F32),
            jax.ShapeDtypeStruct((hidden, width), F32),
        ]
        + [row] * 5
        + [jax.ShapeDtypeStruct((1, hidden), F32), row, tokens, tokens],
        scratch_shapes=[
            pltpu.VMEM((blocks,) + square, BF16),
            pltpu.VMEM((blocks,) + square, F32),
            pltpu.VMEM((2 * micro, frames, band, width), BF16),
            pltpu.SemaphoreType.DMA((blocks,)),
            pltpu.SemaphoreType.DMA((blocks,)),
            pltpu.SemaphoreType.DMA((2 * micro,)),
            pltpu.SemaphoreType.DMA((2 * micro,)),
        ],
        compiler_params=pltpu.CompilerParams(vmem_limit_bytes=62 * 1024 * 1024),
        name="outputs",
    )(flat, vector, activations, input_grads)
    shape_out = (1, micro, 1, frames, band, width)
    return (
        activations.reshape(shape_out),
        input_grads.reshape(shape_out),
        ag,
        ab,
        d_in[None],
        d_out[None],
        ob,
        fg,
        fb,
        d_up[None],
        d_up_bias,
        d_down[None],
        db,
    )


def solution(mesh):
    wide, deep = P("section", None), P("section", None, None)
    tokens = P(None, "dp", None, None, None)
    weights = (wide, wide, deep, deep, wide, wide, wide, deep, wide, deep, wide)
    outputs = P("section", None, "dp", None, None, None)
    return jax.shard_map(
        per_device,
        mesh=mesh,
        in_specs=(tokens, P(None, "dp"), P(None, "dp", None), tokens) + weights,
        out_specs=(outputs, outputs) + weights,
        check_vma=False,
    )
```
